32 devices in a mesh: row: 8 (over y, x, core), col: 4 (over z).
Axes of the slice: x: 2, y: 2, z: 4, core: 2. Of those that a mesh axis runs over, the one named last changes fastest.
Arguments:
- diag: float32 [4, 1024, 1024], P(None, 'row'), as said below
- panel_rows: float32 [16, 8, 64, 1024], P('row', None, None, 'col')
- panel_cols: float32 [4, 8, 64, 1024], P('col', None, 'row')
- trailing: float32 [16, 4, 8, 64, 1024], P('row', 'col')
- sketch: float32 [64, 1024], replicated, may hold values from -6 to 6
- panel_rank: int32 [16], P('row'), may hold values from 16 to 64
- col_rank: int32 [4], P('col'), may hold values from 16 to 64
- tile_rank: int32 [16, 4], P('row', 'col'), may hold values from 32 to 64
- keep_rank: int32 [16, 4], P('row', 'col'), may hold values from 8 to 32
Outputs:
- new_tiles: float32 [16, 4, 8, 64, 1024], P('row', 'col')
The draws below stay inside these ranges and needn't reach their ends.
Inputs may be any that keep to these rules, and one draw needn't show every extreme that they name: `keep_rank`: recompression ranks, never above the tile's rank. diag[0] is symmetric positive definite with smallest eigenvalue 0.5 or more; the tangents are symmetric.
All inputs are finite; a program needn't handle non-finite values.
Results may differ from the reference program's by a relative error of at most 0.0003.
Values sent between devices are 32-bit elements; how exact they have to be, the bound alone decides.
No kernel may reach another device: no remote copies, remote signals or barrier semaphores. Data moves between devices by JAX's collectives and lax.ppermute only.
A program may use at most 192 MiB of HBM per device.

```python
import math
import jax
import jax.numpy as jnp
from jax import lax

NB = 1024
RMAX = 64
TROWS = 16
TCOLS = 4


def factor_draw(key, shape, v_scale):
    values = jax.random.normal(key, shape, jnp.float32)
    scales = jnp.where(jnp.arange(8) < 4, 1.0, v_scale).astype(jnp.float32)
    return values * scales[:, None, None]


def draw_panel_rows(key, part):
    return factor_draw(key, (TROWS, 8, RMAX, NB), 1.0 / 32.0)


def draw_panel_cols(key, part):
    return factor_draw(key, (TCOLS, 8, RMAX, NB), 1.0 / 32.0)


def draw_trailing(key, part):
    return factor_draw(key, (TROWS, TCOLS, 8, RMAX, NB), 1.0 / 8.0)


def draw_diag(key, part):
    point_key = jax.random.fold_in(key, 11)
    noise_key = jax.random.fold_in(key, 23)
    points = jax.random.uniform(point_key, (NB, 2), jnp.float32)
    variance = 16.0
    length_scale = 0.06
    noise = 0.05 * jax.random.normal(noise_key, (3, NB, NB), jnp.float32)
    noise = (noise + jnp.swapaxes(noise, 1, 2)) / math.sqrt(2.0)
    offsets = points[:, None, :] - points[None, :, :]
    distance = jnp.sqrt(jnp.sum(offsets * offsets, axis=-1))
    scaled = math.sqrt(3.0) * distance / length_scale
    kernel = (1.0 + scaled) * jnp.exp(-scaled)
    identity = jnp.eye(NB, dtype=jnp.float32)
    primal = variance * kernel + 0.5 * identity
    tangents = jnp.stack([variance * kernel, variance * scaled * scaled * jnp.exp(-scaled), identity]) + noise
    return jnp.concatenate([primal[None], tangents], axis=0)


def plant(entries, rng, least, top_value):
    index_at = [jax.random.randint(jax.random.fold_in(rng, axis), (), 0, length) for axis, length in enumerate(entries.shape)]
    longest = entries.shape.index(max(entries.shape))
    neighbour = index_at[:longest] + [(index_at[longest] + 1) % entries.shape[longest]] + index_at[longest + 1:]
    return entries.at[tuple(index_at)].set(least).at[tuple(neighbour)].set(top_value)


def bell_draw(own_key, extent, width, bound, kind=jnp.bfloat16):
    result = jax.random.normal(own_key, extent, jnp.float32) * width
    return jnp.minimum(jnp.maximum(result, -bound), bound).astype(kind)


def setup_inputs(seed: int = 0) -> dict:
    keys = jax.random.split(jax.random.key(seed), 10)
    diag = draw_diag(jax.random.fold_in(keys[9], 71), 0)
    panel_rows = draw_panel_rows(jax.random.fold_in(keys[9], 71), 0)
    panel_cols = draw_panel_cols(jax.random.fold_in(keys[9], 71), 0)
    trailing = draw_trailing(jax.random.fold_in(keys[9], 71), 0)
    sketch = bell_draw(keys[4], (RMAX, NB), 1.0, 6.0, jnp.float32)
    panel_rank = plant(jax.random.randint(keys[5], (TROWS,), RMAX // 4, RMAX + 1), jax.random.fold_in(keys[5], 1), RMAX // 4, RMAX).astype(jnp.int32)
    col_rank = plant(jax.random.randint(keys[6], (TCOLS,), RMAX // 4, RMAX + 1), jax.random.fold_in(keys[6], 1), RMAX // 4, RMAX).astype(jnp.int32)
    tile_rank = plant(jax.random.randint(keys[7], (TROWS, TCOLS), RMAX // 2, RMAX + 1), jax.random.fold_in(keys[7], 1), RMAX // 2, RMAX).astype(jnp.int32)
    keep_rank = plant(jax.random.randint(keys[8], (TROWS, TCOLS), RMAX // 8, RMAX // 2 + 1), jax.random.fold_in(keys[8], 1), RMAX // 8, (RMAX // 2 + 1) - 1).astype(jnp.int32)
    return {"diag": diag, "panel_rows": panel_rows, "panel_cols": panel_cols, "trailing": trailing, "sketch": sketch, "panel_rank": panel_rank, "col_rank": col_rank, "tile_rank": tile_rank, "keep_rank": keep_rank}


HIGHEST_PRECISION = lax.Precision.HIGHEST

def highest_accuracy(left, right):
    return jnp.dot(left.astype(jnp.float32), right.astype(jnp.float32), precision=HIGHEST_PRECISION, preferred_element_type=jnp.float32)

def rank_mask(rank_values, rank_count):
    return (jnp.arange(rank_count, dtype=jnp.int32) < rank_values[..., None]).astype(jnp.float32)

def inverse_apply(lower_factor, rank_rows):
    half_solved = jax.scipy.linalg.solve_triangular(lower_factor, rank_rows.T, lower=True)
    full_solved = jax.scipy.linalg.solve_triangular(lower_factor, half_solved, lower=True, trans=1)
    return full_solved.T

def sketch_apply(active_sketch, previous_left_factor, previous_right_factor, u_row, mix_in, u_col):
    return highest_accuracy(highest_accuracy(active_sketch, previous_right_factor.T), previous_left_factor) - highest_accuracy(highest_accuracy(highest_accuracy(active_sketch, u_col.T), mix_in.T), u_row)

def basis_apply(row_basis_matrix, previous_left_factor, previous_right_factor, u_row, mix_in, u_col):
    return highest_accuracy(highest_accuracy(row_basis_matrix, previous_left_factor.T), previous_right_factor) - highest_accuracy(highest_accuracy(highest_accuracy(row_basis_matrix, u_row.T), mix_in), u_col)

def compress_all(previous_left_factor, previous_right_factor, u_row, mix_in, u_col, du_old, dv_old, du_row, dmix_in, du_col, active_sketch, live_mask):
    sketched = sketch_apply(active_sketch, previous_left_factor, previous_right_factor, u_row, mix_in, u_col)
    gram_matrix = highest_accuracy(sketched, sketched.T) + jnp.diag(1.0 - live_mask)
    factor = jnp.linalg.cholesky(gram_matrix)
    row_basis_matrix = jax.scipy.linalg.solve_triangular(factor, sketched, lower=True)
    coefficients = basis_apply(row_basis_matrix, previous_left_factor, previous_right_factor, u_row, mix_in, u_col)
    up_scale = math.sqrt(previous_left_factor.shape[1])
    down_scale = math.sqrt(previous_left_factor.shape[0])

    def tangent_direction(previous_left_derivative, previous_right_derivative, row_left_derivative, mixing_derivative, column_left_derivative):
        sketch_derivative = highest_accuracy(highest_accuracy(active_sketch, previous_right_derivative.T), previous_left_factor) + highest_accuracy(highest_accuracy(active_sketch, previous_right_factor.T), previous_left_derivative)
        sketch_derivative = sketch_derivative - highest_accuracy(highest_accuracy(highest_accuracy(active_sketch, column_left_derivative.T), mix_in.T), u_row)
        sketch_derivative = sketch_derivative - highest_accuracy(highest_accuracy(highest_accuracy(active_sketch, u_col.T), mixing_derivative.T), u_row)
        sketch_derivative = sketch_derivative - highest_accuracy(highest_accuracy(highest_accuracy(active_sketch, u_col.T), mix_in.T), row_left_derivative)
        d_gram = highest_accuracy(sketch_derivative, sketched.T) + highest_accuracy(sketched, sketch_derivative.T)
        inner = jax.scipy.linalg.solve_triangular(factor, d_gram, lower=True)
        middle = jax.scipy.linalg.solve_triangular(factor, inner.T, lower=True)
        lower_part = jnp.tril(middle) - 0.5 * jnp.diag(jnp.diagonal(middle))
        d_factor = highest_accuracy(factor, lower_part)
        d_basis = jax.scipy.linalg.solve_triangular(factor, sketch_derivative - highest_accuracy(d_factor, row_basis_matrix), lower=True)
        coefficient_derivative = basis_apply(d_basis, previous_left_factor, previous_right_factor, u_row, mix_in, u_col)
        coefficient_derivative = coefficient_derivative + highest_accuracy(highest_accuracy(row_basis_matrix, previous_left_derivative.T), previous_right_factor) + highest_accuracy(highest_accuracy(row_basis_matrix, previous_left_factor.T), previous_right_derivative)
        coefficient_derivative = coefficient_derivative - highest_accuracy(highest_accuracy(highest_accuracy(row_basis_matrix, row_left_derivative.T), mix_in), u_col)
        coefficient_derivative = coefficient_derivative - highest_accuracy(highest_accuracy(highest_accuracy(row_basis_matrix, u_row.T), mixing_derivative), u_col)
        coefficient_derivative = coefficient_derivative - highest_accuracy(highest_accuracy(highest_accuracy(row_basis_matrix, u_row.T), mix_in), column_left_derivative)
        return (d_basis * up_scale, coefficient_derivative / down_scale)
    tangent_basis, tangent_coeff = jax.vmap(tangent_direction)(du_old, dv_old, du_row, dmix_in, du_col)
    return (row_basis_matrix * up_scale, coefficients / down_scale, tangent_basis, tangent_coeff)

def update_tile(row_tile, row_solved, col_tile, col_solved, col_products, old_tile, tile_mask, keep_mask, sketch):
    old_tile = old_tile * tile_mask[None, :, None]
    mixing = highest_accuracy(row_tile[4], col_solved.T)
    tangent_mix = jnp.stack([highest_accuracy(row_tile[5 + direction], col_solved.T) + highest_accuracy(row_solved, col_tile[5 + direction].T) - highest_accuracy(row_solved, col_products[direction].T) for direction in range(3)])
    active_sketch = sketch * keep_mask[:, None]
    basis_out, coeff_out, tangent_basis, tangent_coeff = compress_all(old_tile[0], old_tile[4], row_tile[0], mixing, col_tile[0], old_tile[1:4], old_tile[5:8], row_tile[1:4], tangent_mix, col_tile[1:4], active_sketch, keep_mask)
    return jnp.concatenate([basis_out[None], tangent_basis, coeff_out[None], tangent_coeff], axis=0)

def reference(diag, panel_rows, panel_cols, trailing, sketch, panel_rank, col_rank, tile_rank, keep_rank):
    lower_factor = jnp.linalg.cholesky(diag[0])
    rows_kept = panel_rows * rank_mask(panel_rank, RMAX)[:, None, :, None]
    cols_kept = panel_cols * rank_mask(col_rank, RMAX)[:, None, :, None]
    row_solved = inverse_apply(lower_factor, rows_kept[:, 4].reshape(-1, NB)).reshape(TROWS, RMAX, NB)
    col_solved = inverse_apply(lower_factor, cols_kept[:, 4].reshape(-1, NB)).reshape(TCOLS, RMAX, NB)
    col_products = jnp.einsum('caj,tij->ctai', col_solved, diag[1:], precision=HIGHEST_PRECISION)
    tile_live = rank_mask(tile_rank, RMAX)
    keep_live = rank_mask(keep_rank, RMAX)

    def one_row(row_items):
        row_tile, row_z, old_row, live_row, keep_row = row_items

        def one_tile(col_tile, col_z, col_prod, old_tile, tile_mask, keep_mask):
            return update_tile(row_tile, row_z, col_tile, col_z, col_prod, old_tile, tile_mask, keep_mask, sketch)
        return jax.vmap(one_tile)(cols_kept, col_solved, col_products, old_row, live_row, keep_row)
    return lax.map(one_row, (rows_kept, row_solved, trailing, tile_live, keep_live))
```

```python
import functools
import math

import jax
import jax.numpy as jnp
from jax import lax
from jax.experimental import pallas as pl
from jax.experimental.pallas import tpu as pltpu
from jax.sharding import PartitionSpec as P

HIGHEST = lax.Precision.HIGHEST
F32 = jnp.float32
BF16 = jnp.bfloat16
BLOCK = 128
SUB = 8
VMEM_LIMIT = 48 * 1024 * 1024

NN = (((1,), (0,)), ((), ()))
NT = (((1,), (1,)), ((), ()))


def mm(left, right, dims=NN):
    return lax.dot_general(left, right, dims, precision=HIGHEST, preferred_element_type=F32)


def split3(x):
    hi = x.astype(BF16)
    rest = x - hi.astype(F32)
    mid = rest.astype(BF16)
    lo = (rest - mid.astype(F32)).astype(BF16)
    return hi, mid, lo


def left_terms(x):
    hi, mid, lo = split3(x)
    return jnp.concatenate([hi, hi, mid, mid, hi, lo], axis=1)


def right_terms(x):
    hi, mid, lo = split3(x)
    return jnp.concatenate([hi, mid, hi, mid, lo, hi], axis=0)


def lane_rep(x, lane):
    return jnp.broadcast_to(x[:, lane : lane + 1], (SUB, BLOCK))


def sub_rep(x, row):
    return jnp.broadcast_to(x[row : row + 1, :], (SUB, BLOCK))


def tree_sum(terms):
    while len(terms) > 1:
        terms = [
            terms[i] + terms[i + 1] if i + 1 < len(terms) else terms[i]
            for i in range(0, len(terms), 2)
        ]
    return terms[0]


def sub_index():
    return lax.broadcasted_iota(jnp.int32, (SUB, BLOCK), 0)


def lane_index():
    return lax.broadcasted_iota(jnp.int32, (SUB, BLOCK), 1)


def micro_inverse(cols, want_factor):
    sub = sub_index()
    low = None
    pivots = jnp.zeros((SUB, BLOCK), F32)
    if want_factor:
        low = [jnp.where(sub == k, 1.0, 0.0) for k in range(SUB)]
    for j in range(SUB):
        here = sub == j
        piv = sub_rep(cols[j], j)
        inv_piv = 1.0 / piv
        factor = jnp.where(here, -1.0, cols[j])
        if want_factor:
            pivots = jnp.where(here, piv, pivots)
            below = jnp.where(sub > j, cols[j], 0.0)
            for k in range(j + 1):
                low[k] = low[k] - below * (sub_rep(low[k], j) * inv_piv)
        fresh = []
        for k in range(SUB):
            if k == j:
                fresh.append(-factor * inv_piv)
            else:
                row = sub_rep(cols[k], j) * inv_piv
                fresh.append(jnp.where(here, 0.0, cols[k]) - factor * row)
        cols = fresh
    if want_factor:
        scale = lax.rsqrt(pivots)
        return cols, [scale * c for c in low]
    return cols, None


def block_inverse(rows):
    rows = list(rows)
    count = len(rows)
    sub, lane = sub_index(), lane_index()
    for g in range(count):
        at = g * SUB
        inside = (lane >= at) & (lane < at + SUB)
        inv, _ = micro_inverse([lane_rep(rows[g], at + k) for k in range(SUB)], False)
        own = jnp.where(inside, jnp.where(lane - at == sub, 1.0, 0.0), rows[g])
        new = tree_sum([inv[k] * sub_rep(own, k) for k in range(SUB)])
        news = [sub_rep(new, k) for k in range(SUB)]
        order = [(g + 1 + i) % count for i in range(count - 1)]
        for i in order:
            kept = jnp.where(inside, 0.0, rows[i])
            rows[i] = kept - tree_sum([lane_rep(rows[i], at + k) * news[k] for k in range(SUB)])
        rows[g] = new
    return rows


def factor_inverse(rows, width):
    rows = list(rows)
    count = width // SUB
    for g in range(count):
        at = g * SUB
        inv, low = micro_inverse([lane_rep(rows[g], at + k) for k in range(SUB)], True)
        own = rows[g]
        own_rep = [sub_rep(own, k) for k in range(SUB)]
        new = tree_sum([inv[k] * own_rep[k] for k in range(SUB)])
        news = [sub_rep(new, k) for k in range(SUB)]
        for i in range(g + 1, count):
            rows[i] = rows[i] - tree_sum(
                [lane_rep(rows[i], at + k) * news[k] for k in range(SUB)]
            )
        rows[g] = tree_sum([low[k] * own_rep[k] for k in range(SUB)])
    return rows


def as_rows(x):
    return [x[i * SUB : (i + 1) * SUB, :] for i in range(x.shape[0] // SUB)]


def inverse_kernel(
    own_rows, gathered, col_rank, tangents, inverse, solved, products, pivot, left, right
):
    size = inverse.shape[0]
    steps = size // BLOCK
    shards = gathered.shape[0]

    def copy_in(r, _):
        inverse[pl.ds(pl.multiple_of(r * own_rows, own_rows), own_rows), :] = gathered[
            r, pl.ds(0, own_rows), :
        ]
        return _

    lax.fori_loop(0, shards, copy_in, 0)

    def invert_to_pivot(block):
        pivot[...] = jnp.concatenate(block_inverse(as_rows(block)), axis=0)

    def prepare(k):
        at = pl.ds(pl.multiple_of(k * BLOCK, BLOCK), BLOCK)
        inv = pivot[...]
        column = inverse[:, at]
        row = mm(inv, inverse[at, :])
        left[...] = left_terms(column)
        right[...] = right_terms(row)
        right[:, at] = right_terms(inv)
        inverse[:, at] = jnp.zeros((size, BLOCK), F32)
        return at, row, inv

    def update(at, row, inv):
        chunk = 256
        for c in range(size // chunk):
            part = slice(c * chunk, (c + 1) * chunk)
            inverse[part, :] = inverse[part, :] - lax.dot_general(
                left[part, :], right[...], NN, preferred_element_type=F32
            )
        inverse[at, :] = row
        inverse[at, at] = inv

    invert_to_pivot(inverse[:BLOCK, :BLOCK])

    def step(k, carry):
        nxt = pl.ds(pl.multiple_of((k + 1) * BLOCK, BLOCK), BLOCK)
        block = inverse[nxt, nxt]
        at, row, inv = prepare(k)
        block = block - lax.dot_general(
            left[nxt, :], right[:, nxt], NN, preferred_element_type=F32
        )
        update(at, row, inv)
        invert_to_pivot(block)
        return carry

    lax.fori_loop(0, steps - 1, step, 0)
    update(*prepare(steps - 1))

    rank_count = solved.shape[0]
    own_ranks = rank_count // shards
    values = jnp.concatenate(
        [gathered[r, own_rows : own_rows + own_ranks, :] for r in range(shards)], axis=0
    )
    live = lax.broadcasted_iota(jnp.int32, values.shape, 0) < col_rank[0]
    values = jnp.where(live, values, 0.0)
    z = mm(values, inverse[...])
    solved[...] = z
    for t in range(3):
        products[t] = mm(z, tangents[t], NT)


def run_inverse(gathered, tangents, col_rank, own_rows):
    shards, _, size = gathered.shape
    rank_count = (gathered.shape[1] - own_rows) * shards
    vmem = pl.BlockSpec(memory_space=pltpu.VMEM)
    return pl.pallas_call(
        functools.partial(inverse_kernel, own_rows),
        out_shape=(
            jax.ShapeDtypeStruct((size, size), F32),
            jax.ShapeDtypeStruct((rank_count, size), F32),
            jax.ShapeDtypeStruct((3, rank_count, own_rows), F32),
        ),
        in_specs=[vmem, pl.BlockSpec(memory_space=pltpu.SMEM), vmem],
        out_specs=(vmem, vmem, vmem),
        scratch_shapes=[
            pltpu.VMEM((BLOCK, BLOCK), F32),
            pltpu.VMEM((size, 6 * BLOCK), BF16),
            pltpu.VMEM((6 * BLOCK, size), BF16),
        ],
        compiler_params=pltpu.CompilerParams(vmem_limit_bytes=VMEM_LIMIT),
        cost_estimate=pl.CostEstimate(
            flops=40 * 10**9, bytes_accessed=10 * 2**20, transcendentals=0
        ),
        name="inverse",
    )(gathered, col_rank, tangents)


def row_mask(shape, rank):
    return lax.broadcasted_iota(jnp.int32, shape, 0) < rank


def load_rows(own_ref, shard_refs, position, p, comp, rank):
    count = 1 + len(shard_refs)
    own = own_ref[p, comp]
    parts = [own] + [ref[p, comp] for ref in shard_refs]
    pieces = []
    for j in range(count):
        piece = parts[0]
        for s in range(1, count):
            piece = jnp.where(lax.rem(position - s + count, count) == j, parts[s], piece)
        pieces.append(piece)
    whole = jnp.concatenate(pieces, axis=1)
    return jnp.where(row_mask(whole.shape, rank), whole, 0.0)


def load_cols(ref, comp, rank):
    groups = ref.shape[0]
    whole = jnp.concatenate([ref[g, comp] for g in range(groups)], axis=0)
    return jnp.where(row_mask(whole.shape, rank), whole, 0.0)


def primal_kernel(
    tiles,
    shards,
    place,
    panel_rank,
    col_rank,
    tile_rank,
    keep_rank,
    *refs,
):
    row_refs = refs[:shards]
    cols, trailing, sketch, solved = refs[shards : shards + 4]
    basis, coeffs, mixes, factors = refs[shards + 4 :]
    rank_count, size = sketch.shape
    position = place[0]
    z = solved[...]
    u_col = load_cols(cols, 0, col_rank[0])
    s = sketch[...]
    su_all = mm(s, u_col, NT)
    keep = []
    augmented = []
    for p in range(tiles):
        live = lax.broadcasted_iota(jnp.int32, (rank_count, 1), 0) < keep_rank[p, 0]
        u_row = load_rows(row_refs[0], row_refs[1:], position, p, 0, panel_rank[p])
        v_row = load_rows(row_refs[0], row_refs[1:], position, p, 1, panel_rank[p])
        old = row_mask((rank_count, size), tile_rank[p, 0])
        u_old = jnp.where(old, trailing[p, 0, 0], 0.0)
        v_old = jnp.where(old, trailing[p, 0, 4], 0.0)
        mix = mm(v_row, z, NT)
        su = jnp.where(live, su_all, 0.0)
        sv = jnp.where(live, mm(s, v_old, NT), 0.0)
        y = mm(sv, u_old) - mm(mm(su, mix, NT), u_row)
        gram = mm(y, y, NT)
        eye = lax.broadcasted_iota(jnp.int32, gram.shape, 0) == lax.broadcasted_iota(
            jnp.int32, gram.shape, 1
        )
        gram = gram + jnp.where(eye & jnp.logical_not(live), 1.0, 0.0)
        augmented.append(jnp.concatenate([gram, jnp.where(eye, 1.0, 0.0)], axis=1))
        keep.append((y, u_row, u_old, v_old, mix))
    inverses = [factor_inverse(as_rows(a), rank_count) for a in augmented]
    for p in range(tiles):
        y, u_row, u_old, v_old, mix = keep[p]
        rinv = jnp.concatenate(inverses[p], axis=0)[:, rank_count:]
        q = mm(rinv, y)
        b = mm(mm(q, u_old, NT), v_old) - mm(mm(mm(q, u_row, NT), mix), u_col)
        basis[p] = q
        coeffs[p] = b
        mixes[p] = mix
        factors[p] = rinv


def run_primal(place, ranks, row_shards, cols, trailing, sketch, solved):
    tiles = trailing.shape[0]
    rank_count, size = sketch.shape
    vmem = pl.BlockSpec(memory_space=pltpu.VMEM)
    smem = pl.BlockSpec(memory_space=pltpu.SMEM)
    big = jax.ShapeDtypeStruct((tiles, rank_count, size), F32)
    small = jax.ShapeDtypeStruct((tiles, rank_count, rank_count), F32)
    return pl.pallas_call(
        functools.partial(primal_kernel, tiles, len(row_shards)),
        out_shape=(big, big, small, small),
        in_specs=[smem] * 5 + [vmem] * (len(row_shards) + 4),
        out_specs=(vmem,) * 4,
        compiler_params=pltpu.CompilerParams(vmem_limit_bytes=VMEM_LIMIT),
        cost_estimate=pl.CostEstimate(
            flops=5 * 10**9, bytes_accessed=8 * 2**20, transcendentals=0
        ),
        name="primal",
    )(place, *ranks, *row_shards, cols, trailing, sketch, solved)


def tangent_kernel(
    tiles,
    shards,
    place,
    panel_rank,
    col_rank,
    tile_rank,
    keep_rank,
    *refs,
):
    row_refs = refs[:shards]
    tan_refs = refs[shards : 2 * shards]
    cols, trailing, sketch, solved, inverse, products, basis, coeffs, mixes, factors = refs[
        2 * shards : 2 * shards + 10
    ]
    (out,) = refs[2 * shards + 10 :]
    rank_count, size = sketch.shape
    up_scale = math.sqrt(size)
    down_scale = 1.0 / math.sqrt(rank_count)
    position = place[0]
    z = solved[...]
    u_col = [load_cols(cols, t, col_rank[0]) for t in range(4)]
    sides = []
    for t in range(3):
        whole = jnp.concatenate([products[r, t] for r in range(products.shape[0])], axis=1)
        sides.append(load_cols(cols, 5 + t, col_rank[0]) - whole)
    dz = mm(jnp.concatenate(sides, axis=0), inverse[...])
    s = sketch[...]
    su_all = mm(s, jnp.concatenate(u_col, axis=0), NT)
    for p in range(tiles):
        live = lax.broadcasted_iota(jnp.int32, (rank_count, 1), 0) < keep_rank[p, 0]
        load = functools.partial(load_rows, position=position, p=p, rank=panel_rank[p])
        u_row = [load(row_refs[0], row_refs[1:], comp=0)]
        v_row = load(row_refs[0], row_refs[1:], comp=1)
        u_row += [load(tan_refs[0], tan_refs[1:], comp=t) for t in range(3)]
        dv_row = jnp.concatenate(
            [load(tan_refs[0], tan_refs[1:], comp=3 + t) for t in range(3)], axis=0
        )
        old = row_mask((rank_count, size), tile_rank[p, 0])
        u_old = [jnp.where(old, trailing[p, 0, t], 0.0) for t in range(4)]
        v_old = [jnp.where(old, trailing[p, 0, 4 + t], 0.0) for t in range(4)]
        q, mix, rinv = basis[p], mixes[p], factors[p]
        dv_z = mm(dv_row, z, NT)
        v_dz = mm(v_row, dz, NT)
        su_p = jnp.where(live, su_all, 0.0)
        sv_p = jnp.where(live, mm(s, jnp.concatenate(v_old, axis=0), NT), 0.0)
        part = lambda x, t: x[:, t * rank_count : (t + 1) * rank_count]
        base_v = mm(rinv, part(sv_p, 0))
        base_u = mm(rinv, mm(part(su_p, 0), mix, NT))
        q_parts = mm(q, jnp.concatenate(u_old + u_row, axis=0), NT)
        q_mix = mm(part(q_parts, 4), mix)
        out[p, 0, 0] = q * up_scale
        out[p, 0, 4] = coeffs[p] * down_scale
        for t in range(3):
            dmix = dv_z[t * rank_count : (t + 1) * rank_count] + part(v_dz, t)
            u_side = mm(part(su_p, t + 1), mix, NT) + mm(part(su_p, 0), dmix, NT)
            left = jnp.concatenate(
                [mm(rinv, part(sv_p, t + 1)), base_v, -mm(rinv, u_side), -base_u], axis=1
            )
            right = jnp.concatenate([u_old[0], u_old[t + 1], u_row[0], u_row[t + 1]], axis=0)
            e = mm(left, right)
            cross = mm(e, q, NT)
            sym = cross + mm(q, e, NT)
            i0 = lax.broadcasted_iota(jnp.int32, sym.shape, 0)
            i1 = lax.broadcasted_iota(jnp.int32, sym.shape, 1)
            phi = jnp.where(i0 > i1, sym, jnp.where(i0 == i1, 0.5 * sym, 0.0))
            dq = e - mm(phi, q)
            dq_parts = mm(dq, jnp.concatenate([u_old[0], u_row[0]], axis=0), NT)
            on_v = part(dq_parts, 0) + part(q_parts, t + 1)
            on_u = mm(part(dq_parts, 1) + part(q_parts, 5 + t), mix) + mm(part(q_parts, 4), dmix)
            left = jnp.concatenate([on_v, part(q_parts, 0), -on_u, -q_mix], axis=1)
            right = jnp.concatenate([v_old[0], v_old[t + 1], u_col[0], u_col[t + 1]], axis=0)
            out[p, 0, 1 + t] = dq * up_scale
            out[p, 0, 5 + t] = mm(left, right) * down_scale


def run_tangent(
    place, ranks, row_shards, tan_shards, cols, trailing, sketch, solved, inverse, products, primal
):
    vmem = pl.BlockSpec(memory_space=pltpu.VMEM)
    smem = pl.BlockSpec(memory_space=pltpu.SMEM)
    return pl.pallas_call(
        functools.partial(tangent_kernel, trailing.shape[0], len(row_shards)),
        out_shape=jax.ShapeDtypeStruct(trailing.shape, F32),
        in_specs=[smem] * 5 + [vmem] * (2 * len(row_shards) + 6 + len(primal)),
        out_specs=vmem,
        compiler_params=pltpu.CompilerParams(vmem_limit_bytes=VMEM_LIMIT),
        cost_estimate=pl.CostEstimate(
            flops=10 * 10**9, bytes_accessed=20 * 2**20, transcendentals=0
        ),
        name="tangent",
    )(place, *ranks, *row_shards, *tan_shards, cols, trailing, sketch, solved, inverse, products, *primal)


def on_device(
    row_count,
    col_count,
    diag,
    panel_rows,
    panel_cols,
    trailing,
    sketch,
    panel_rank,
    col_rank,
    tile_rank,
    keep_rank,
):
    own_rows = diag.shape[1]
    own_ranks = panel_cols.shape[2]
    comps = panel_cols.shape[1]
    size = sketch.shape[1]
    gathered = lax.all_gather(
        jnp.concatenate([diag[0], panel_cols[0, 4]], axis=0), "row", axis=0
    )
    first = panel_rows[:, 0::4]
    second = jnp.concatenate([panel_rows[:, 1:4], panel_rows[:, 5:8]], axis=1)
    first_shards, second_shards = [first], [second]
    for source, shards in ((first, first_shards), (second, second_shards)):
        for s in range(1, col_count):
            shards.append(
                lax.ppermute(source, "col", [(i, (i + s) % col_count) for i in range(col_count)])
            )
    late_cols, gathered = lax.optimization_barrier((panel_cols[0], gathered))
    cols = lax.all_gather(late_cols, "row", axis=0)
    if own_ranks != SUB:
        cols = cols.reshape(-1, SUB // own_ranks, comps, own_ranks, size)
        cols = cols.transpose(0, 2, 1, 3, 4).reshape(-1, comps, SUB, size)
    inverse, solved, products = run_inverse(gathered, diag[1:], col_rank, own_rows)
    all_products = lax.all_gather(products, "row", axis=0)
    place = lax.axis_index("col").astype(jnp.int32).reshape(1)
    ranks = (panel_rank, col_rank, tile_rank, keep_rank)
    primal = run_primal(place, ranks, first_shards, cols, trailing, sketch, solved)
    return run_tangent(
        place,
        ranks,
        first_shards,
        second_shards,
        cols,
        trailing,
        sketch,
        solved,
        inverse,
        all_products,
        primal,
    )


def solution(mesh):
    in_specs = (
        P(None, "row", None),
        P("row", None, None, "col"),
        P("col", None, "row", None),
        P("row", "col", None, None, None),
        P(),
        P("row"),
        P("col"),
        P("row", "col"),
        P("row", "col"),
    )
    out_specs = P("row", "col", None, None, None)
    body = functools.partial(on_device, mesh.shape["row"], mesh.shape["col"])
    return jax.shard_map(body, mesh=mesh, in_specs=in_specs, out_specs=out_specs, check_vma=False)
```

```python
import functools
import math

import jax
import jax.numpy as jnp
from jax import lax
from jax.experimental import pallas as pl
from jax.experimental.pallas import tpu as pltpu
from jax.sharding import PartitionSpec as P

HIGHEST = lax.Precision.HIGHEST
F32 = jnp.float32
BF16 = jnp.bfloat16
BLOCK = 128
SUB = 8
VMEM_LIMIT = 48 * 1024 * 1024

NN = (((1,), (0,)), ((), ()))
NT = (((1,), (1,)), ((), ()))


def mm(left, right, dims=NN):
    return lax.dot_general(left, right, dims, precision=HIGHEST, preferred_element_type=F32)


def split3(x):
    hi = x.astype(BF16)
    rest = x - hi.astype(F32)
    mid = rest.astype(BF16)
    lo = (rest - mid.astype(F32)).astype(BF16)
    return hi, mid, lo


def left_terms(x):
    hi, mid, lo = split3(x)
    return jnp.concatenate([hi, hi, mid, mid, hi, lo], axis=1)


def right_terms(x):
    hi, mid, lo = split3(x)
    return jnp.concatenate([hi, mid, hi, mid, lo, hi], axis=0)


def lane_rep(x, lane):
    return jnp.broadcast_to(x[:, lane : lane + 1], (SUB, BLOCK))


def sub_rep(x, row):
    return jnp.broadcast_to(x[row : row + 1, :], (SUB, BLOCK))


def tree_sum(terms):
    while len(terms) > 1:
        terms = [
            terms[i] + terms[i + 1] if i + 1 < len(terms) else terms[i]
            for i in range(0, len(terms), 2)
        ]
    return terms[0]


def sub_index():
    return lax.broadcasted_iota(jnp.int32, (SUB, BLOCK), 0)


def lane_index():
    return lax.broadcasted_iota(jnp.int32, (SUB, BLOCK), 1)


def micro_inverse(cols):
    sub = sub_index()
    cols = list(cols)
    for j in range(0, SUB, 2):
        first, second = sub == j, sub == j + 1
        pair = first | second
        a, b, d = sub_rep(cols[j], j), sub_rep(cols[j], j + 1), sub_rep(cols[j + 1], j + 1)
        inv_det = 1.0 / (a * d - b * b)
        f0 = jnp.where(first, -1.0, jnp.where(second, 0.0, cols[j]))
        f1 = jnp.where(second, -1.0, jnp.where(first, 0.0, cols[j + 1]))
        fresh = []
        for k in range(SUB):
            if k == j:
                fresh.append((f1 * b - f0 * d) * inv_det)
            elif k == j + 1:
                fresh.append((f0 * b - f1 * a) * inv_det)
            else:
                x0, x1 = sub_rep(cols[k], j), sub_rep(cols[k], j + 1)
                change = f0 * (d * x0 - b * x1) + f1 * (a * x1 - b * x0)
                fresh.append(jnp.where(pair, 0.0, cols[k]) - change * inv_det)
        cols = fresh
    return cols


def micro_factor(cols):
    sub = sub_index()
    cols = list(cols)
    low = [jnp.where(sub == k, 1.0, 0.0) for k in range(SUB)]
    pivots = jnp.zeros((SUB, BLOCK), F32)
    for j in range(SUB):
        here = sub == j
        piv = sub_rep(cols[j], j)
        inv_piv = 1.0 / piv
        factor = jnp.where(here, -1.0, cols[j])
        pivots = jnp.where(here, piv, pivots)
        below = jnp.where(sub > j, cols[j], 0.0)
        for k in range(j + 1):
            low[k] = low[k] - below * sub_rep(low[k], j) * inv_piv
        cols = [
            -factor * inv_piv
            if k == j
            else jnp.where(here, 0.0, cols[k]) - factor * (sub_rep(cols[k], j) * inv_piv)
            for k in range(SUB)
        ]
    scale = lax.rsqrt(pivots)
    return cols, [scale * c for c in low]


def block_inverse(rows):
    rows = list(rows)
    count = len(rows)
    sub, lane = sub_index(), lane_index()
    for g in range(count):
        at = g * SUB
        inside = (lane >= at) & (lane < at + SUB)
        inv = micro_inverse([lane_rep(rows[g], at + k) for k in range(SUB)])
        own = jnp.where(inside, jnp.where(lane - at == sub, 1.0, 0.0), rows[g])
        new = tree_sum([inv[k] * sub_rep(own, k) for k in range(SUB)])
        news = [sub_rep(new, k) for k in range(SUB)]
        order = [(g + 1 + i) % count for i in range(count - 1)]
        for i in order:
            kept = jnp.where(inside, 0.0, rows[i])
            rows[i] = kept - tree_sum([lane_rep(rows[i], at + k) * news[k] for k in range(SUB)])
        rows[g] = new
    return rows


def factor_inverse(rows, width):
    rows = list(rows)
    count = width // SUB
    for g in range(count):
        at = g * SUB
        inv, low = micro_factor([lane_rep(rows[g], at + k) for k in range(SUB)])
        own = rows[g]
        own_rep = [sub_rep(own, k) for k in range(SUB)]
        new = tree_sum([inv[k] * own_rep[k] for k in range(SUB)])
        news = [sub_rep(new, k) for k in range(SUB)]
        for i in range(g + 1, count):
            rows[i] = rows[i] - tree_sum(
                [lane_rep(rows[i], at + k) * news[k] for k in range(SUB)]
            )
        rows[g] = tree_sum([low[k] * own_rep[k] for k in range(SUB)])
    return rows


def as_rows(x):
    return [x[i * SUB : (i + 1) * SUB, :] for i in range(x.shape[0] // SUB)]


def inverse_kernel(
    own_rows,
    gathered,
    col_rank,
    tangents,
    inverse,
    solved,
    products,
    pivot,
    left,
    right,
    scale_row,
    scale_col,
):
    size = inverse.shape[0]
    steps = size // BLOCK
    shards = gathered.shape[0]

    def copy_in(r, _):
        inverse[pl.ds(pl.multiple_of(r * own_rows, own_rows), own_rows), :] = gathered[
            r, pl.ds(0, own_rows), :
        ]
        return _

    lax.fori_loop(0, shards, copy_in, 0)

    eye = lax.broadcasted_iota(jnp.int32, (BLOCK, BLOCK), 0) == lax.broadcasted_iota(
        jnp.int32, (BLOCK, BLOCK), 1
    )
    for c in range(steps):
        part = slice(c * BLOCK, (c + 1) * BLOCK)
        own = jnp.where(eye, inverse[part, part], 0.0)
        scale_row[:, part] = lax.rsqrt(jnp.sum(own, axis=0, keepdims=True))
        scale_col[part, :] = jnp.broadcast_to(
            lax.rsqrt(jnp.sum(own, axis=1, keepdims=True)), (BLOCK, BLOCK)
        )

    def rescale():
        for c in range(steps):
            part = slice(c * BLOCK, (c + 1) * BLOCK)
            col = scale_col[part, :]
            for e in range(steps):
                other = slice(e * BLOCK, (e + 1) * BLOCK)
                inverse[part, other] = inverse[part, other] * col * scale_row[:, other]

    rescale()

    def invert_to_pivot(block):
        pivot[...] = jnp.concatenate(block_inverse(as_rows(block)), axis=0)

    def prepare(k):
        at = pl.ds(pl.multiple_of(k * BLOCK, BLOCK), BLOCK)
        inv = pivot[...]
        column = inverse[:, at]
        row = mm(inv, inverse[at, :])
        left[...] = left_terms(column)
        right[...] = right_terms(row)
        right[:, at] = right_terms(inv)
        inverse[:, at] = jnp.zeros((size, BLOCK), F32)
        return at, row, inv

    def update(at, row, inv):
        chunk = 256
        for c in range(size // chunk):
            part = slice(c * chunk, (c + 1) * chunk)
            inverse[part, :] = inverse[part, :] - lax.dot_general(
                left[part, :], right[...], NN, preferred_element_type=F32
            )
        inverse[at, :] = row
        inverse[at, at] = inv

    invert_to_pivot(inverse[:BLOCK, :BLOCK])

    def step(k, carry):
        nxt = pl.ds(pl.multiple_of((k + 1) * BLOCK, BLOCK), BLOCK)
        block = inverse[nxt, nxt]
        at, row, inv = prepare(k)
        block = block - lax.dot_general(
            left[nxt, :], right[:, nxt], NN, preferred_element_type=F32
        )
        update(at, row, inv)
        invert_to_pivot(block)
        return carry

    lax.fori_loop(0, steps - 1, step, 0)
    update(*prepare(steps - 1))
    rescale()

    rank_count = solved.shape[0]
    own_ranks = rank_count // shards
    values = jnp.concatenate(
        [gathered[r, own_rows : own_rows + own_ranks, :] for r in range(shards)], axis=0
    )
    live = lax.broadcasted_iota(jnp.int32, values.shape, 0) < col_rank[0]
    values = jnp.where(live, values, 0.0)
    z = mm(values, inverse[...])
    solved[...] = z
    for t in range(3):
        products[t] = mm(z, tangents[t], NT)


def run_inverse(gathered, tangents, col_rank, own_rows):
    shards, _, size = gathered.shape
    rank_count = (gathered.shape[1] - own_rows) * shards
    vmem = pl.BlockSpec(memory_space=pltpu.VMEM)
    return pl.pallas_call(
        functools.partial(inverse_kernel, own_rows),
        out_shape=(
            jax.ShapeDtypeStruct((size, size), F32),
            jax.ShapeDtypeStruct((rank_count, size), F32),
            jax.ShapeDtypeStruct((3, rank_count, own_rows), F32),
        ),
        in_specs=[vmem, pl.BlockSpec(memory_space=pltpu.SMEM), vmem],
        out_specs=(vmem, vmem, vmem),
        scratch_shapes=[
            pltpu.VMEM((BLOCK, BLOCK), F32),
            pltpu.VMEM((size, 6 * BLOCK), BF16),
            pltpu.VMEM((6 * BLOCK, size), BF16),
            pltpu.VMEM((1, size), F32),
            pltpu.VMEM((size, BLOCK), F32),
        ],
        compiler_params=pltpu.CompilerParams(vmem_limit_bytes=VMEM_LIMIT),
        cost_estimate=pl.CostEstimate(
            flops=40 * 10**9, bytes_accessed=10 * 2**20, transcendentals=0
        ),
        name="inverse",
    )(gathered, col_rank, tangents)


def split2(x):
    hi = x.astype(BF16)
    return hi, (x - hi.astype(F32)).astype(BF16)


def dot_split(left, right, dims=NN):
    left_hi, left_lo = left
    right_hi, right_lo = right
    rows = left_hi.shape[0]
    both = lax.dot_general(
        jnp.concatenate([left_hi, left_lo], axis=0), right_hi, dims, preferred_element_type=F32
    )
    cross = lax.dot_general(left_hi, right_lo, dims, preferred_element_type=F32)
    return both[:rows] + (both[rows:] + cross)


def keep_rows(x, rank):
    return jnp.where(lax.broadcasted_iota(jnp.int32, x.shape, 0) < rank, x, 0.0)


def put(refs, at, x):
    hi, lo = split2(x)
    refs[0][at] = hi
    refs[1][at] = lo


def put_shards(refs, slot, sources, position, p, comp, rank):
    count = len(sources)
    width = sources[0].shape[-1]
    rank_count = sources[0].shape[-2]
    for s, ref in enumerate(sources):
        owner = lax.rem(position - s + count, count)
        at = pl.ds(pl.multiple_of(owner * width, width), width)
        put(refs, (p, pl.ds(slot * rank_count, rank_count), at), keep_rows(ref[p, comp], rank))


def col_component(ref, comp, rank):
    whole = jnp.concatenate([ref[g, comp] for g in range(ref.shape[0])], axis=0)
    return keep_rows(whole, rank)


def recompress_kernel(
    tiles, shards, place, panel_rank, col_rank, tile_rank, keep_rank, *refs
):
    first = refs[:shards]
    second = refs[shards : 2 * shards]
    cols, trailing, sketch, solved, inverse, products, out = refs[2 * shards : 2 * shards + 7]
    left_hi, left_lo, right_hi, right_lo, panel_hi, panel_lo = refs[2 * shards + 7 :]
    lefts, rights, panels = (left_hi, left_lo), (right_hi, right_lo), (panel_hi, panel_lo)
    rank_count, size = sketch.shape
    up_scale = math.sqrt(size)
    down_scale = 1.0 / math.sqrt(rank_count)
    position = place[0]
    block = lambda x, i: x[:, i * rank_count : (i + 1) * rank_count]
    band = lambda x, i: x[i * rank_count : (i + 1) * rank_count]
    slot = lambda p, i, n=1: (p, slice(i * rank_count, (i + n) * rank_count), slice(None))
    take = lambda pair, at: (pair[0][at], pair[1][at])

    for t in range(4):
        u_col = col_component(cols, t, col_rank[0])
        for p in range(tiles):
            put(rights, slot(p, 1 if t == 0 else 4 + t), u_col)
    for p in range(tiles):
        for t in range(4):
            rank = tile_rank[p, 0]
            put(lefts, slot(p, 0 if t == 0 else 1 + t), keep_rows(trailing[p, 0, t], rank))
            put(rights, slot(p, 0 if t == 0 else 1 + t), keep_rows(trailing[p, 0, 4 + t], rank))
        put_shards(lefts, 1, first, position, p, 0, panel_rank[p])
        put_shards(panels, 0, first, position, p, 1, panel_rank[p])
        for t in range(3):
            put_shards(lefts, 5 + t, second, position, p, t, panel_rank[p])
            put_shards(panels, 1 + t, second, position, p, 3 + t, panel_rank[p])

    sides = []
    for t in range(3):
        whole = jnp.concatenate([products[r, t] for r in range(products.shape[0])], axis=1)
        sides.append(col_component(cols, 5 + t, col_rank[0]) - whole)
    dz = dot_split(split2(jnp.concatenate(sides, axis=0)), split2(inverse[...]))
    z_hi, z_lo = split2(solved[...])
    dz_hi, dz_lo = split2(dz)
    zz = (jnp.concatenate([z_hi, dz_hi], axis=0), jnp.concatenate([z_lo, dz_lo], axis=0))
    s = split2(sketch[...])

    state = []
    for p in range(tiles):
        live = lax.broadcasted_iota(jnp.int32, (rank_count, 1), 0) < keep_rank[p, 0]
        mixes = dot_split(take(panels, slot(p, 0, 4)), zz, NT)
        sketched = jnp.where(live, dot_split(s, take(rights, slot(p, 0, 8)), NT), 0.0)
        mix = mixes[:rank_count, :rank_count]
        base_u = -mm(block(sketched, 1), mix, NT)
        pair = jnp.concatenate([block(sketched, 0), base_u], axis=1)
        bases = take(lefts, slot(p, 0, 2))
        y = dot_split(split2(pair), bases)
        y_split = split2(y)
        gram = dot_split(y_split, y_split, NT)
        eye = lax.broadcasted_iota(jnp.int32, gram.shape, 0) == lax.broadcasted_iota(
            jnp.int32, gram.shape, 1
        )
        gram = gram + jnp.where(eye & jnp.logical_not(live), 1.0, 0.0)
        augmented = jnp.concatenate([gram, jnp.where(eye, 1.0, 0.0)], axis=1)
        cross = dot_split(bases, take(lefts, slot(p, 0, 8)), NT)
        state.append((mixes, sketched, pair, cross, augmented))

    factors = [factor_inverse(as_rows(entry[-1]), rank_count) for entry in state]

    for p in range(tiles):
        mixes, sketched, pair, cross, _ = state[p]
        rinv = jnp.concatenate(factors[p], axis=0)[:, rank_count:]
        mix = mixes[:rank_count, :rank_count]
        dmix = [band(block(mixes, 0), 1 + t) + band(block(mixes, 1 + t), 0) for t in range(3)]
        su = [block(sketched, 1)] + [block(sketched, 5 + t) for t in range(3)]
        u_mix = mm(jnp.concatenate(su[1:], axis=0), mix, NT)
        u_dmix = mm(su[0], jnp.concatenate(dmix, axis=0), NT)
        u_sides = [-(band(u_mix, t) + block(u_dmix, t)) for t in range(3)]
        sv = [block(sketched, 2 + t) for t in range(3)]
        coefs = mm(rinv, jnp.concatenate([pair] + sv + u_sides, axis=1))
        q_coef = coefs[:, : 2 * rank_count]
        q_parts = mm(q_coef, cross)
        phis = []
        for t in range(3):
            e_coef = jnp.concatenate(
                [block(coefs, 2 + t), block(coefs, 5 + t), q_coef], axis=1
            )
            q_side = jnp.concatenate(
                [block(q_parts, 0), block(q_parts, 1), block(q_parts, 2 + t), block(q_parts, 5 + t)],
                axis=1,
            )
            half = mm(e_coef, q_side, NT)
            sym = half + half.T
            i0 = lax.broadcasted_iota(jnp.int32, sym.shape, 0)
            i1 = lax.broadcasted_iota(jnp.int32, sym.shape, 1)
            phis.append(jnp.where(i0 > i1, sym, jnp.where(i0 == i1, 0.5 * sym, 0.0)))
        turned = mm(jnp.concatenate(phis, axis=0), q_coef)
        none = jnp.zeros((rank_count, rank_count), F32)
        rows = [jnp.concatenate([q_coef] + [none] * 6, axis=1)]
        for t in range(3):
            head = jnp.concatenate([block(coefs, 2 + t), block(coefs, 5 + t)], axis=1)
            tail = [none] * 6
            tail[t], tail[3 + t] = block(q_coef, 0), block(q_coef, 1)
            rows.append(jnp.concatenate([head - band(turned, t)] + tail, axis=1))
        basis_coef = jnp.concatenate(rows, axis=0)
        basis = dot_split(split2(basis_coef), take(lefts, slot(p, 0, 8))) * up_scale
        for t in range(4):
            out[p, 0, t] = band(basis, t)
        dq_parts = mm(basis_coef[rank_count:], cross, NT)
        on_u = mm(
            block(dq_parts, 1)
            + jnp.concatenate([block(q_parts, 5 + t) for t in range(3)], axis=0),
            mix,
        )
        on_dmix = mm(block(q_parts, 1), jnp.concatenate(dmix, axis=1))
        q_mix = mm(block(q_parts, 1), mix)
        rows = [jnp.concatenate([block(q_parts, 0), -q_mix] + [none] * 6, axis=1)]
        for t in range(3):
            on_v = band(block(dq_parts, 0), t) + block(q_parts, 2 + t)
            tail = [none] * 6
            tail[t], tail[3 + t] = block(q_parts, 0), -q_mix
            rows.append(
                jnp.concatenate([on_v, -(band(on_u, t) + block(on_dmix, t))] + tail, axis=1)
            )
        coeff = dot_split(
            split2(jnp.concatenate(rows, axis=0) * down_scale), take(rights, slot(p, 0, 8))
        )
        for t in range(4):
            out[p, 0, 4 + t] = band(coeff, t)


def run_recompress(
    place, ranks, first, second, cols, trailing, sketch, solved, inverse, products
):
    tiles = trailing.shape[0]
    rank_count, size = sketch.shape
    vmem = pl.BlockSpec(memory_space=pltpu.VMEM)
    smem = pl.BlockSpec(memory_space=pltpu.SMEM)
    return pl.pallas_call(
        functools.partial(recompress_kernel, tiles, len(first)),
        out_shape=jax.ShapeDtypeStruct(trailing.shape, F32),
        in_specs=[smem] * 5 + [vmem] * (2 * len(first) + 6),
        out_specs=vmem,
        scratch_shapes=[pltpu.VMEM((tiles, 8 * rank_count, size), BF16)] * 4
        + [pltpu.VMEM((tiles, 4 * rank_count, size), BF16)] * 2,
        compiler_params=pltpu.CompilerParams(vmem_limit_bytes=VMEM_LIMIT),
        cost_estimate=pl.CostEstimate(
            flops=10 * 10**9, bytes_accessed=20 * 2**20, transcendentals=0
        ),
        name="recompress",
    )(place, *ranks, *first, *second, cols, trailing, sketch, solved, inverse, products)


def on_device(
    row_count,
    col_count,
    diag,
    panel_rows,
    panel_cols,
    trailing,
    sketch,
    panel_rank,
    col_rank,
    tile_rank,
    keep_rank,
):
    own_rows = diag.shape[1]
    own_ranks = panel_cols.shape[2]
    comps = panel_cols.shape[1]
    size = sketch.shape[1]
    gathered = lax.all_gather(
        jnp.concatenate([diag[0], panel_cols[0, 4]], axis=0), "row", axis=0
    )
    first = panel_rows[:, 0::4]
    second = jnp.concatenate([panel_rows[:, 1:4], panel_rows[:, 5:8]], axis=1)
    first_shards, second_shards = [first], [second]
    for source, shards in ((first, first_shards), (second, second_shards)):
        for s in range(1, col_count):
            shards.append(
                lax.ppermute(source, "col", [(i, (i + s) % col_count) for i in range(col_count)])
            )
    late_cols, gathered = lax.optimization_barrier((panel_cols[0], gathered))
    cols = lax.all_gather(late_cols, "row", axis=0)
    if own_ranks != SUB:
        cols = cols.reshape(-1, SUB // own_ranks, comps, own_ranks, size)
        cols = cols.transpose(0, 2, 1, 3, 4).reshape(-1, comps, SUB, size)
    inverse, solved, products = run_inverse(gathered, diag[1:], col_rank, own_rows)
    all_products = lax.all_gather(products, "row", axis=0)
    place = lax.axis_index("col").astype(jnp.int32).reshape(1)
    ranks = (panel_rank, col_rank, tile_rank, keep_rank)
    return run_recompress(
        place,
        ranks,
        first_shards,
        second_shards,
        cols,
        trailing,
        sketch,
        solved,
        inverse,
        all_products,
    )


def solution(mesh):
    in_specs = (
        P(None, "row", None),
        P("row", None, None, "col"),
        P("col", None, "row", None),
        P("row", "col", None, None, None),
        P(),
        P("row"),
        P("col"),
        P("row", "col"),
        P("row", "col"),
    )
    out_specs = P("row", "col", None, None, None)
    body = functools.partial(on_device, mesh.shape["row"], mesh.shape["col"])
    return jax.shard_map(body, mesh=mesh, in_specs=in_specs, out_specs=out_specs, check_vma=False)
```

```python
import functools
import math

import jax
import jax.numpy as jnp
from jax import lax
from jax.experimental import pallas as pl
from jax.experimental.pallas import tpu as pltpu
from jax.sharding import PartitionSpec as P

HIGHEST = lax.Precision.HIGHEST
F32 = jnp.float32
BF16 = jnp.bfloat16
BLOCK = 128
SUB = 8
INVERSE_VMEM = 28 * 1024 * 1024
RECOMPRESS_VMEM = 40 * 1024 * 1024

NN = (((1,), (0,)), ((), ()))
NT = (((1,), (1,)), ((), ()))


def mm(left, right, dims=NN):
    return lax.dot_general(left, right, dims, precision=HIGHEST, preferred_element_type=F32)


def split3(x):
    hi = x.astype(BF16)
    rest = x - hi.astype(F32)
    mid = rest.astype(BF16)
    lo = (rest - mid.astype(F32)).astype(BF16)
    return hi, mid, lo


def left_terms(x):
    hi, mid, lo = split3(x)
    return jnp.concatenate([hi, hi, mid, mid, hi, lo], axis=1)


def right_terms(x):
    hi, mid, lo = split3(x)
    return jnp.concatenate([hi, mid, hi, mid, lo, hi], axis=0)


def lane_rep(x, lane):
    return jnp.broadcast_to(x[:, lane : lane + 1], (SUB, BLOCK))


def sub_rep(x, row):
    return jnp.broadcast_to(x[row : row + 1, :], (SUB, BLOCK))


def tree_sum(terms):
    while len(terms) > 1:
        terms = [
            terms[i] + terms[i + 1] if i + 1 < len(terms) else terms[i]
            for i in range(0, len(terms), 2)
        ]
    return terms[0]


def sub_index():
    return lax.broadcasted_iota(jnp.int32, (SUB, BLOCK), 0)


def lane_index():
    return lax.broadcasted_iota(jnp.int32, (SUB, BLOCK), 1)


def micro_inverse(cols):
    sub = sub_index()
    cols = list(cols)
    for j in range(0, SUB, 2):
        first, second = sub == j, sub == j + 1
        pair = first | second
        a, b, d = sub_rep(cols[j], j), sub_rep(cols[j], j + 1), sub_rep(cols[j + 1], j + 1)
        inv_det = 1.0 / (a * d - b * b)
        f0 = jnp.where(first, -1.0, jnp.where(second, 0.0, cols[j]))
        f1 = jnp.where(second, -1.0, jnp.where(first, 0.0, cols[j + 1]))
        fresh = []
        for k in range(SUB):
            if k == j:
                fresh.append((f1 * b - f0 * d) * inv_det)
            elif k == j + 1:
                fresh.append((f0 * b - f1 * a) * inv_det)
            else:
                x0, x1 = sub_rep(cols[k], j), sub_rep(cols[k], j + 1)
                change = f0 * (d * x0 - b * x1) + f1 * (a * x1 - b * x0)
                fresh.append(jnp.where(pair, 0.0, cols[k]) - change * inv_det)
        cols = fresh
    return cols


def micro_factor(cols):
    sub = sub_index()
    cols = list(cols)
    low = [jnp.where(sub == k, 1.0, 0.0) for k in range(SUB)]
    pivots = jnp.zeros((SUB, BLOCK), F32)
    for j in range(SUB):
        here = sub == j
        piv = sub_rep(cols[j], j)
        inv_piv = 1.0 / piv
        factor = jnp.where(here, -1.0, cols[j])
        pivots = jnp.where(here, piv, pivots)
        below = jnp.where(sub > j, cols[j], 0.0)
        for k in range(j + 1):
            low[k] = low[k] - below * sub_rep(low[k], j) * inv_piv
        cols = [
            -factor * inv_piv
            if k == j
            else jnp.where(here, 0.0, cols[k]) - factor * (sub_rep(cols[k], j) * inv_piv)
            for k in range(SUB)
        ]
    scale = lax.rsqrt(pivots)
    return cols, [scale * c for c in low]


def block_inverse(rows, work):
    rows = list(rows)
    count = len(rows)
    sub, lane = sub_index(), lane_index()
    for g in range(count):
        at = g * SUB
        inside = (lane >= at) & (lane < at + SUB)
        inv = micro_inverse([lane_rep(rows[g], at + k) for k in range(SUB)])
        own = jnp.where(inside, jnp.where(lane - at == sub, 1.0, 0.0), rows[g])
        new = tree_sum([inv[k] * sub_rep(own, k) for k in range(SUB)])
        news = [sub_rep(new, k) for k in range(SUB)]
        order = [(g + 1 + i) % count for i in range(count - 1)]
        for i in order:
            kept = jnp.where(inside, 0.0, rows[i])
            rows[i] = kept - tree_sum([lane_rep(rows[i], at + k) * news[k] for k in range(SUB)])
        rows[g] = new
        for piece in work[g * len(work) // count : (g + 1) * len(work) // count]:
            piece()
    return rows


def factor_inverse(rows, width):
    rows = list(rows)
    count = width // SUB
    for g in range(count):
        at = g * SUB
        inv, low = micro_factor([lane_rep(rows[g], at + k) for k in range(SUB)])
        own = rows[g]
        own_rep = [sub_rep(own, k) for k in range(SUB)]
        new = tree_sum([inv[k] * own_rep[k] for k in range(SUB)])
        news = [sub_rep(new, k) for k in range(SUB)]
        for i in range(g + 1, count):
            rows[i] = rows[i] - tree_sum(
                [lane_rep(rows[i], at + k) * news[k] for k in range(SUB)]
            )
        rows[g] = tree_sum([low[k] * own_rep[k] for k in range(SUB)])
    return rows


def as_rows(x):
    return [x[i * SUB : (i + 1) * SUB, :] for i in range(x.shape[0] // SUB)]


def inverse_kernel(
    own_rows,
    gathered,
    col_rank,
    tangents,
    inverse,
    solved,
    products,
    scale_row,
    pivot,
    left,
    right,
    scale_col,
):
    size = inverse.shape[0]
    steps = size // BLOCK
    shards, height, width = gathered.shape
    eye = lax.broadcasted_iota(jnp.int32, (BLOCK, BLOCK), 0) == lax.broadcasted_iota(
        jnp.int32, (BLOCK, BLOCK), 1
    )
    part = lambda c, n=BLOCK: slice(c * n, (c + 1) * n)

    def set_scale(c, block):
        own = jnp.where(eye, block, 0.0)
        scale_row[:, part(c)] = lax.rsqrt(jnp.sum(own, axis=0, keepdims=True))
        scale_col[part(c), :] = jnp.broadcast_to(
            lax.rsqrt(jnp.sum(own, axis=1, keepdims=True)), (BLOCK, BLOCK)
        )

    if width < size:
        for c in range(steps):
            set_scale(c, gathered[c, :BLOCK, :BLOCK])
        for r in range(steps):
            for o in range(width // BLOCK):
                c = (r + o) % steps
                block = gathered[r, :BLOCK, part(o)] * scale_col[part(r), :] * scale_row[:, part(c)]
                inverse[part(r), part(c)] = block
                if 0 < o and 2 * o < steps:
                    inverse[part(c), part(r)] = block.T
    else:
        for r in range(shards):
            inverse[part(r, own_rows), :] = gathered[r, :own_rows, :]
        for c in range(steps):
            set_scale(c, inverse[part(c), part(c)])
        for r in range(steps):
            for c in range(steps):
                inverse[part(r), part(c)] = (
                    inverse[part(r), part(c)] * scale_col[part(r), :] * scale_row[:, part(c)]
                )

    def eliminate(k, at, inv):
        chunk = 2 * BLOCK
        chunks = size // chunk
        twice = jnp.concatenate([inv, inv], axis=1)

        def fill_left(c):
            column = inverse[part(c, chunk), at]
            owner = 2 * c + lax.broadcasted_iota(jnp.int32, column.shape, 0) // BLOCK
            left[part(c, chunk), :] = left_terms(jnp.where(owner == k, 0.0, column))
            inverse[part(c, chunk), at] = jnp.zeros((chunk, BLOCK), F32)

        def fill_right(c):
            row = mm(inv, inverse[at, part(c, chunk)])
            owner = 2 * c + lax.broadcasted_iota(jnp.int32, row.shape, 1) // BLOCK
            row = jnp.where(owner == k, twice, row)
            right[:, part(c, chunk)] = right_terms(row)
            inverse[at, part(c, chunk)] = row

        def update(r, c):
            here = (part(r, chunk), part(c, chunk))
            inverse[here] = inverse[here] - lax.dot_general(
                left[here[0], :], right[:, here[1]], NN, preferred_element_type=F32
            )

        work = [functools.partial(fill_left, c) for c in range(chunks)]
        for c in range(chunks):
            work.append(functools.partial(fill_right, c))
            work += [functools.partial(update, r, c) for r in range(chunks)]
        return work

    def invert_to_pivot(block, work):
        pivot[...] = jnp.concatenate(block_inverse(as_rows(block), work), axis=0)

    invert_to_pivot(inverse[:BLOCK, :BLOCK], [])

    def step(k, carry):
        at = pl.ds(pl.multiple_of(k * BLOCK, BLOCK), BLOCK)
        nxt = pl.ds(pl.multiple_of((k + 1) * BLOCK, BLOCK), BLOCK)
        inv = pivot[...]
        block = inverse[nxt, nxt] - mm(inverse[nxt, at], mm(inv, inverse[at, nxt]))
        invert_to_pivot(block, eliminate(k, at, inv))
        return carry

    lax.fori_loop(0, steps - 1, step, 0)
    for piece in eliminate(steps - 1, slice(size - BLOCK, size), pivot[...]):
        piece()

    rank_count = solved.shape[0]
    own_ranks = rank_count // shards
    values = []
    for r in range(shards):
        pieces = []
        for at in range(own_rows, height, own_ranks):
            pieces.append(gathered[r, at : at + own_ranks, :])
        values.append(jnp.concatenate(pieces, axis=1)[:, :size])
    values = keep_rows(jnp.concatenate(values, axis=0), col_rank[0])
    z = mm(values * scale_row[...], inverse[...]) * scale_row[...]
    solved[...] = z
    for t in range(3):
        products[t] = mm(z, tangents[t], NT)


def run_inverse(gathered, tangents, col_rank, own_rows, own_ranks):
    shards = gathered.shape[0]
    size = tangents.shape[2]
    rank_count = own_ranks * shards
    vmem = pl.BlockSpec(memory_space=pltpu.VMEM)
    return pl.pallas_call(
        functools.partial(inverse_kernel, own_rows),
        out_shape=(
            jax.ShapeDtypeStruct((size, size), F32),
            jax.ShapeDtypeStruct((rank_count, size), F32),
            jax.ShapeDtypeStruct((3, rank_count, own_rows), F32),
            jax.ShapeDtypeStruct((1, size), F32),
        ),
        in_specs=[vmem, pl.BlockSpec(memory_space=pltpu.SMEM), vmem],
        out_specs=(vmem,) * 4,
        scratch_shapes=[
            pltpu.VMEM((BLOCK, BLOCK), F32),
            pltpu.VMEM((size, 6 * BLOCK), BF16),
            pltpu.VMEM((6 * BLOCK, size), BF16),
            pltpu.VMEM((size, BLOCK), F32),
        ],
        compiler_params=pltpu.CompilerParams(vmem_limit_bytes=INVERSE_VMEM),
        cost_estimate=pl.CostEstimate(
            flops=40 * 10**9, bytes_accessed=10 * 2**20, transcendentals=0
        ),
        name="inverse",
    )(gathered, col_rank, tangents)


def split2(x):
    hi = x.astype(BF16)
    return hi, (x - hi.astype(F32)).astype(BF16)


def dot_split(left, right, dims=NN):
    left_hi, left_lo = left
    right_hi, right_lo = right
    rows = left_hi.shape[0]
    both = lax.dot_general(
        jnp.concatenate([left_hi, left_lo], axis=0), right_hi, dims, preferred_element_type=F32
    )
    cross = lax.dot_general(left_hi, right_lo, dims, preferred_element_type=F32)
    return both[:rows] + (both[rows:] + cross)


def keep_rows(x, rank):
    return jnp.where(lax.broadcasted_iota(jnp.int32, x.shape, 0) < rank, x, 0.0)


def put(refs, at, x):
    hi, lo = split2(x)
    refs[0][at] = hi
    refs[1][at] = lo


def put_shards(refs, slot, sources, position, p, comp, rank):
    count = len(sources)
    width = sources[0].shape[-1]
    rank_count = sources[0].shape[-2]
    for s, ref in enumerate(sources):
        owner = lax.rem(position - s + count, count)
        at = pl.ds(pl.multiple_of(owner * width, width), width)
        put(refs, (p, pl.ds(slot * rank_count, rank_count), at), keep_rows(ref[p, comp], rank))


def col_component(ref, comp, rank):
    whole = jnp.concatenate([ref[g, comp] for g in range(ref.shape[0])], axis=0)
    return keep_rows(whole, rank)


def recompress_kernel(
    tiles, shards, place, panel_rank, col_rank, tile_rank, keep_rank, *refs
):
    first = refs[:shards]
    second = refs[shards : 2 * shards]
    cols, trailing, sketch, solved, inverse, scale, products, out = refs[
        2 * shards : 2 * shards + 8
    ]
    left_hi, left_lo, right_hi, right_lo, panel_hi, panel_lo = refs[2 * shards + 8 :]
    lefts, rights, panels = (left_hi, left_lo), (right_hi, right_lo), (panel_hi, panel_lo)
    rank_count, size = sketch.shape
    up_scale = math.sqrt(size)
    down_scale = 1.0 / math.sqrt(rank_count)
    position = place[0]
    block = lambda x, i: x[:, i * rank_count : (i + 1) * rank_count]
    band = lambda x, i: x[i * rank_count : (i + 1) * rank_count]
    slot = lambda p, i, n=1: (p, slice(i * rank_count, (i + n) * rank_count), slice(None))
    take = lambda pair, at: (pair[0][at], pair[1][at])

    for t in range(4):
        u_col = col_component(cols, t, col_rank[0])
        for p in range(tiles):
            put(rights, slot(p, 1 if t == 0 else 4 + t), u_col)
    for p in range(tiles):
        for t in range(4):
            rank = tile_rank[p, 0]
            put(lefts, slot(p, 0 if t == 0 else 1 + t), keep_rows(trailing[p, 0, t], rank))
            put(rights, slot(p, 0 if t == 0 else 1 + t), keep_rows(trailing[p, 0, 4 + t], rank))
        put_shards(lefts, 1, first, position, p, 0, panel_rank[p])
        put_shards(panels, 0, first, position, p, 1, panel_rank[p])
        for t in range(3):
            put_shards(lefts, 5 + t, second, position, p, t, panel_rank[p])
            put_shards(panels, 1 + t, second, position, p, 3 + t, panel_rank[p])

    sides = []
    for t in range(3):
        whole = jnp.concatenate([products[r, t] for r in range(products.shape[0])], axis=1)
        sides.append(col_component(cols, 5 + t, col_rank[0]) - whole)
    sides = jnp.concatenate(sides, axis=0) * scale[...]
    dz = dot_split(split2(sides), split2(inverse[...])) * scale[...]
    z_hi, z_lo = split2(solved[...])
    dz_hi, dz_lo = split2(dz)
    zz = (jnp.concatenate([z_hi, dz_hi], axis=0), jnp.concatenate([z_lo, dz_lo], axis=0))
    s = split2(sketch[...])

    state = []
    for p in range(tiles):
        live = lax.broadcasted_iota(jnp.int32, (rank_count, 1), 0) < keep_rank[p, 0]
        mixes = dot_split(take(panels, slot(p, 0, 4)), zz, NT)
        sketched = jnp.where(live, dot_split(s, take(rights, slot(p, 0, 8)), NT), 0.0)
        mix = mixes[:rank_count, :rank_count]
        base_u = -mm(block(sketched, 1), mix, NT)
        pair = jnp.concatenate([block(sketched, 0), base_u], axis=1)
        bases = take(lefts, slot(p, 0, 2))
        y = dot_split(split2(pair), bases)
        y_split = split2(y)
        gram = dot_split(y_split, y_split, NT)
        eye = lax.broadcasted_iota(jnp.int32, gram.shape, 0) == lax.broadcasted_iota(
            jnp.int32, gram.shape, 1
        )
        gram = gram + jnp.where(eye & jnp.logical_not(live), 1.0, 0.0)
        augmented = jnp.concatenate([gram, jnp.where(eye, 1.0, 0.0)], axis=1)
        cross = dot_split(bases, take(lefts, slot(p, 0, 8)), NT)
        state.append((mixes, sketched, pair, cross, augmented))

    factors = [factor_inverse(as_rows(entry[-1]), rank_count) for entry in state]

    for p in range(tiles):
        mixes, sketched, pair, cross, _ = state[p]
        rinv = jnp.concatenate(factors[p], axis=0)[:, rank_count:]
        mix = mixes[:rank_count, :rank_count]
        dmix = [band(block(mixes, 0), 1 + t) + band(block(mixes, 1 + t), 0) for t in range(3)]
        su = [block(sketched, 1)] + [block(sketched, 5 + t) for t in range(3)]
        u_mix = mm(jnp.concatenate(su[1:], axis=0), mix, NT)
        u_dmix = mm(su[0], jnp.concatenate(dmix, axis=0), NT)
        u_sides = [-(band(u_mix, t) + block(u_dmix, t)) for t in range(3)]
        sv = [block(sketched, 2 + t) for t in range(3)]
        coefs = mm(rinv, jnp.concatenate([pair] + sv + u_sides, axis=1))
        q_coef = coefs[:, : 2 * rank_count]
        q_parts = mm(q_coef, cross)
        phis = []
        for t in range(3):
            e_coef = jnp.concatenate(
                [block(coefs, 2 + t), block(coefs, 5 + t), q_coef], axis=1
            )
            q_side = jnp.concatenate(
                [block(q_parts, 0), block(q_parts, 1), block(q_parts, 2 + t), block(q_parts, 5 + t)],
                axis=1,
            )
            half = mm(e_coef, q_side, NT)
            sym = half + half.T
            i0 = lax.broadcasted_iota(jnp.int32, sym.shape, 0)
            i1 = lax.broadcasted_iota(jnp.int32, sym.shape, 1)
            phis.append(jnp.where(i0 > i1, sym, jnp.where(i0 == i1, 0.5 * sym, 0.0)))
        turned = mm(jnp.concatenate(phis, axis=0), q_coef)
        none = jnp.zeros((rank_count, rank_count), F32)
        rows = [jnp.concatenate([q_coef] + [none] * 6, axis=1)]
        for t in range(3):
            head = jnp.concatenate([block(coefs, 2 + t), block(coefs, 5 + t)], axis=1)
            tail = [none] * 6
            tail[t], tail[3 + t] = block(q_coef, 0), block(q_coef, 1)
            rows.append(jnp.concatenate([head - band(turned, t)] + tail, axis=1))
        basis_coef = jnp.concatenate(rows, axis=0)
        basis = dot_split(split2(basis_coef), take(lefts, slot(p, 0, 8))) * up_scale
        for t in range(4):
            out[p, 0, t] = band(basis, t)
        dq_parts = mm(basis_coef[rank_count:], cross, NT)
        on_u = mm(
            block(dq_parts, 1)
            + jnp.concatenate([block(q_parts, 5 + t) for t in range(3)], axis=0),
            mix,
        )
        on_dmix = mm(block(q_parts, 1), jnp.concatenate(dmix, axis=1))
        q_mix = mm(block(q_parts, 1), mix)
        rows = [jnp.concatenate([block(q_parts, 0), -q_mix] + [none] * 6, axis=1)]
        for t in range(3):
            on_v = band(block(dq_parts, 0), t) + block(q_parts, 2 + t)
            tail = [none] * 6
            tail[t], tail[3 + t] = block(q_parts, 0), -q_mix
            rows.append(
                jnp.concatenate([on_v, -(band(on_u, t) + block(on_dmix, t))] + tail, axis=1)
            )
        coeff = dot_split(
            split2(jnp.concatenate(rows, axis=0) * down_scale), take(rights, slot(p, 0, 8))
        )
        for t in range(4):
            out[p, 0, 4 + t] = band(coeff, t)


def run_recompress(
    place, ranks, first, second, cols, trailing, sketch, solved, inverse, scale, products
):
    tiles = trailing.shape[0]
    rank_count, size = sketch.shape
    vmem = pl.BlockSpec(memory_space=pltpu.VMEM)
    smem = pl.BlockSpec(memory_space=pltpu.SMEM)
    return pl.pallas_call(
        functools.partial(recompress_kernel, tiles, len(first)),
        out_shape=jax.ShapeDtypeStruct(trailing.shape, F32),
        in_specs=[smem] * 5 + [vmem] * (2 * len(first) + 7),
        out_specs=vmem,
        scratch_shapes=[pltpu.VMEM((tiles, 8 * rank_count, size), BF16)] * 4
        + [pltpu.VMEM((tiles, 4 * rank_count, size), BF16)] * 2,
        compiler_params=pltpu.CompilerParams(vmem_limit_bytes=RECOMPRESS_VMEM),
        cost_estimate=pl.CostEstimate(
            flops=10 * 10**9, bytes_accessed=20 * 2**20, transcendentals=0
        ),
        name="recompress",
    )(place, *ranks, *first, *second, cols, trailing, sketch, solved, inverse, scale, products)


def on_device(
    row_count,
    col_count,
    diag,
    panel_rows,
    panel_cols,
    trailing,
    sketch,
    panel_rank,
    col_rank,
    tile_rank,
    keep_rank,
):
    own_rows = diag.shape[1]
    own_ranks = panel_cols.shape[2]
    comps = panel_cols.shape[1]
    size = sketch.shape[1]
    values = panel_cols[0, 4]
    own = diag[0]
    if own_rows == BLOCK and row_count > 2:
        width = (row_count // 2 + 1) * BLOCK
        own = lax.dynamic_slice(
            jnp.concatenate([own, own[:, : width - BLOCK]], axis=1),
            (0, lax.axis_index("row") * BLOCK),
            (BLOCK, width),
        )
        values = jnp.pad(values, ((0, 0), (0, -size % width)))
        values = jnp.concatenate(
            [values[:, i : i + width] for i in range(0, values.shape[1], width)], axis=0
        )
    gathered = lax.all_gather(jnp.concatenate([own, values], axis=0), "row", axis=0)
    first = panel_rows[:, 0::4]
    second = jnp.concatenate([panel_rows[:, 1:4], panel_rows[:, 5:8]], axis=1)
    first_shards, second_shards = [first], [second]
    for source, shards in ((first, first_shards), (second, second_shards)):
        for s in range(1, col_count):
            shards.append(
                lax.ppermute(source, "col", [(i, (i + s) % col_count) for i in range(col_count)])
            )
    late_cols, gathered = lax.optimization_barrier((panel_cols[0], gathered))
    cols = lax.all_gather(late_cols, "row", axis=0)
    if own_ranks != SUB:
        cols = cols.reshape(-1, SUB // own_ranks, comps, own_ranks, size)
        cols = cols.transpose(0, 2, 1, 3, 4).reshape(-1, comps, SUB, size)
    inverse, solved, products, scale = run_inverse(
        gathered, diag[1:], col_rank, own_rows, own_ranks
    )
    all_products = lax.all_gather(products, "row", axis=0)
    place = lax.axis_index("col").astype(jnp.int32).reshape(1)
    ranks = (panel_rank, col_rank, tile_rank, keep_rank)
    return run_recompress(
        place,
        ranks,
        first_shards,
        second_shards,
        cols,
        trailing,
        sketch,
        solved,
        inverse,
        scale,
        all_products,
    )


def solution(mesh):
    in_specs = (
        P(None, "row", None),
        P("row", None, None, "col"),
        P("col", None, "row", None),
        P("row", "col", None, None, None),
        P(),
        P("row"),
        P("col"),
        P("row", "col"),
        P("row", "col"),
    )
    out_specs = P("row", "col", None, None, None)
    body = functools.partial(on_device, mesh.shape["row"], mesh.shape["col"])
    return jax.shard_map(body, mesh=mesh, in_specs=in_specs, out_specs=out_specs, check_vma=False)
```

```python
import functools
import math

import jax
import jax.numpy as jnp
from jax import lax
from jax.experimental import pallas as pl
from jax.experimental.pallas import tpu as pltpu
from jax.sharding import PartitionSpec as P

HIGHEST = lax.Precision.HIGHEST
F32 = jnp.float32
BF16 = jnp.bfloat16
BLOCK = 128
SUB = 8
BAND = 4
INVERSE_VMEM = 28 * 1024 * 1024
RECOMPRESS_VMEM = 46 * 1024 * 1024

NN = (((1,), (0,)), ((), ()))
NT = (((1,), (1,)), ((), ()))


def mm(left, right, dims=NN):
    return lax.dot_general(left, right, dims, precision=HIGHEST, preferred_element_type=F32)


def split3(x):
    hi = x.astype(BF16)
    rest = x - hi.astype(F32)
    mid = rest.astype(BF16)
    lo = (rest - mid.astype(F32)).astype(BF16)
    return hi, mid, lo


def left_terms(x):
    hi, mid, lo = split3(x)
    return jnp.concatenate([hi, hi, mid, mid, hi, lo], axis=1)


def right_terms(x):
    hi, mid, lo = split3(x)
    return jnp.concatenate([hi, mid, hi, mid, lo, hi], axis=0)


def lane_rep(x, lane):
    return jnp.broadcast_to(x[:, lane : lane + 1], (SUB, BLOCK))


def sub_rep(x, row):
    return jnp.broadcast_to(x[row : row + 1, :], (SUB, BLOCK))


def tree_sum(terms):
    while len(terms) > 1:
        terms = [
            terms[i] + terms[i + 1] if i + 1 < len(terms) else terms[i]
            for i in range(0, len(terms), 2)
        ]
    return terms[0]


def sub_index():
    return lax.broadcasted_iota(jnp.int32, (SUB, BLOCK), 0)


def lane_index():
    return lax.broadcasted_iota(jnp.int32, (SUB, BLOCK), 1)


def micro_inverse(cols):
    sub = sub_index()
    cols = list(cols)
    for j in range(0, SUB, 2):
        first, second = sub == j, sub == j + 1
        pair = first | second
        a, b, d = sub_rep(cols[j], j), sub_rep(cols[j], j + 1), sub_rep(cols[j + 1], j + 1)
        inv_det = 1.0 / (a * d - b * b)
        f0 = jnp.where(first, -1.0, jnp.where(second, 0.0, cols[j]))
        f1 = jnp.where(second, -1.0, jnp.where(first, 0.0, cols[j + 1]))
        fresh = []
        for k in range(SUB):
            if k == j:
                fresh.append((f1 * b - f0 * d) * inv_det)
            elif k == j + 1:
                fresh.append((f0 * b - f1 * a) * inv_det)
            else:
                x0, x1 = sub_rep(cols[k], j), sub_rep(cols[k], j + 1)
                change = f0 * (d * x0 - b * x1) + f1 * (a * x1 - b * x0)
                fresh.append(jnp.where(pair, 0.0, cols[k]) - change * inv_det)
        cols = fresh
    return cols


def micro_factor(cols):
    sub = sub_index()
    cols = list(cols)
    low = [jnp.where(sub == k, 1.0, 0.0) for k in range(SUB)]
    pivots = jnp.zeros((SUB, BLOCK), F32)
    for j in range(SUB):
        here = sub == j
        piv = sub_rep(cols[j], j)
        inv_piv = 1.0 / piv
        factor = jnp.where(here, -1.0, cols[j])
        pivots = jnp.where(here, piv, pivots)
        below = jnp.where(sub > j, cols[j], 0.0)
        for k in range(j + 1):
            low[k] = low[k] - below * sub_rep(low[k], j) * inv_piv
        cols = [
            -factor * inv_piv
            if k == j
            else jnp.where(here, 0.0, cols[k]) - factor * (sub_rep(cols[k], j) * inv_piv)
            for k in range(SUB)
        ]
    scale = lax.rsqrt(pivots)
    return cols, [scale * c for c in low]


def block_inverse(rows, work):
    rows = list(rows)
    count = len(rows)
    sub, lane = sub_index(), lane_index()
    for first in range(0, count, BAND):
        band = range(first, first + BAND)
        for g in band:
            at = g * SUB
            inside = (lane >= at) & (lane < at + SUB)
            inv = micro_inverse([lane_rep(rows[g], at + k) for k in range(SUB)])
            own = jnp.where(inside, jnp.where(lane - at == sub, 1.0, 0.0), rows[g])
            new = tree_sum([inv[k] * sub_rep(own, k) for k in range(SUB)])
            news = [sub_rep(new, k) for k in range(SUB)]
            for i in [first + (g - first + 1 + i) % BAND for i in range(BAND - 1)]:
                kept = jnp.where(inside, 0.0, rows[i])
                rows[i] = kept - tree_sum(
                    [lane_rep(rows[i], at + k) * news[k] for k in range(SUB)]
                )
            rows[g] = new
            for piece in work[g * len(work) // count : (g + 1) * len(work) // count]:
                piece()
        inside = (lane >= first * SUB) & (lane < (first + BAND) * SUB)
        others = [(first + BAND + i) % count for i in range(count - BAND)]
        none = jnp.zeros((SUB, BLOCK), F32)
        padded = jnp.concatenate([rows[i] if i in band else none for i in range(count)], axis=0)
        change = as_rows(mm(jnp.concatenate([rows[i] for i in others], axis=0), padded))
        for i, delta in zip(others, change):
            rows[i] = jnp.where(inside, 0.0, rows[i]) - delta
    return rows


def factor_inverse(rows, width):
    rows = list(rows)
    count = width // SUB
    for g in range(count):
        at = g * SUB
        inv, low = micro_factor([lane_rep(rows[g], at + k) for k in range(SUB)])
        own = rows[g]
        own_rep = [sub_rep(own, k) for k in range(SUB)]
        new = tree_sum([inv[k] * own_rep[k] for k in range(SUB)])
        news = [sub_rep(new, k) for k in range(SUB)]
        for i in range(g + 1, count):
            rows[i] = rows[i] - tree_sum(
                [lane_rep(rows[i], at + k) * news[k] for k in range(SUB)]
            )
        rows[g] = tree_sum([low[k] * own_rep[k] for k in range(SUB)])
    return rows


def as_rows(x):
    return [x[i * SUB : (i + 1) * SUB, :] for i in range(x.shape[0] // SUB)]


def inverse_kernel(
    own_rows,
    gathered,
    col_rank,
    diag,
    inverse_out,
    solved,
    products,
    scale_row,
    inverse,
    tangents,
    pivot,
    left,
    right,
    scale_col,
    sems,
):
    size = inverse.shape[0]
    steps = size // BLOCK
    shards, height, width = gathered.shape
    fetch = pltpu.make_async_copy(diag.at[pl.ds(1, 3)], tangents, sems.at[0])
    fetch.start()
    eye = lax.broadcasted_iota(jnp.int32, (BLOCK, BLOCK), 0) == lax.broadcasted_iota(
        jnp.int32, (BLOCK, BLOCK), 1
    )
    part = lambda c, n=BLOCK: slice(c * n, (c + 1) * n)

    def set_scale(c, block):
        own = jnp.where(eye, block, 0.0)
        scale_row[:, part(c)] = lax.rsqrt(jnp.sum(own, axis=0, keepdims=True))
        scale_col[part(c), :] = jnp.broadcast_to(
            lax.rsqrt(jnp.sum(own, axis=1, keepdims=True)), (BLOCK, BLOCK)
        )

    if width < size:
        for c in range(steps):
            set_scale(c, gathered[c, :BLOCK, :BLOCK])
        for r in range(steps):
            for o in range(width // BLOCK):
                c = (r + o) % steps
                block = gathered[r, :BLOCK, part(o)] * scale_col[part(r), :] * scale_row[:, part(c)]
                inverse[part(r), part(c)] = block
                if 0 < o and 2 * o < steps:
                    inverse[part(c), part(r)] = block.T
    else:
        for r in range(shards):
            inverse[part(r, own_rows), :] = gathered[r, :own_rows, :]
        for c in range(steps):
            set_scale(c, inverse[part(c), part(c)])
        for r in range(steps):
            for c in range(steps):
                inverse[part(r), part(c)] = (
                    inverse[part(r), part(c)] * scale_col[part(r), :] * scale_row[:, part(c)]
                )

    def eliminate(k, at, inv):
        chunk = 2 * BLOCK
        chunks = size // chunk
        twice = jnp.concatenate([inv, inv], axis=1)

        def fill_left(c):
            column = inverse[part(c, chunk), at]
            owner = 2 * c + lax.broadcasted_iota(jnp.int32, column.shape, 0) // BLOCK
            left[part(c, chunk), :] = left_terms(jnp.where(owner == k, 0.0, column))
            inverse[part(c, chunk), at] = jnp.zeros((chunk, BLOCK), F32)

        def fill_right(c):
            row = mm(inv, inverse[at, part(c, chunk)])
            owner = 2 * c + lax.broadcasted_iota(jnp.int32, row.shape, 1) // BLOCK
            row = jnp.where(owner == k, twice, row)
            right[:, part(c, chunk)] = right_terms(row)
            inverse[at, part(c, chunk)] = row

        def update(r, c):
            here = (part(r, chunk), part(c, chunk))
            inverse[here] = inverse[here] - lax.dot_general(
                left[here[0], :], right[:, here[1]], NN, preferred_element_type=F32
            )

        work = [functools.partial(fill_left, c) for c in range(chunks)]
        for c in range(chunks):
            work.append(functools.partial(fill_right, c))
            work += [functools.partial(update, r, c) for r in range(chunks)]
        return work

    def invert_to_pivot(block, work):
        pivot[...] = jnp.concatenate(block_inverse(as_rows(block), work), axis=0)

    invert_to_pivot(inverse[:BLOCK, :BLOCK], [])

    def step(k, carry):
        at = pl.ds(pl.multiple_of(k * BLOCK, BLOCK), BLOCK)
        nxt = pl.ds(pl.multiple_of((k + 1) * BLOCK, BLOCK), BLOCK)
        inv = pivot[...]
        block = inverse[nxt, nxt] - mm(inverse[nxt, at], mm(inv, inverse[at, nxt]))
        invert_to_pivot(block, eliminate(k, at, inv))
        return carry

    lax.fori_loop(0, steps - 1, step, 0)
    for piece in eliminate(steps - 1, slice(size - BLOCK, size), pivot[...]):
        piece()
    store = pltpu.make_async_copy(inverse, inverse_out, sems.at[1])
    store.start()

    rank_count = solved.shape[0]
    own_ranks = rank_count // shards
    values = []
    for r in range(shards):
        pieces = []
        for at in range(own_rows, height, own_ranks):
            pieces.append(gathered[r, at : at + own_ranks, :])
        values.append(jnp.concatenate(pieces, axis=1)[:, :size])
    values = keep_rows(jnp.concatenate(values, axis=0), col_rank[0])
    z = mm(values * scale_row[...], inverse[...]) * scale_row[...]
    solved[...] = z
    fetch.wait()
    for t in range(3):
        products[t] = mm(z, tangents[t], NT)
    store.wait()


def run_inverse(gathered, diag, col_rank, own_ranks):
    shards = gathered.shape[0]
    _, own_rows, size = diag.shape
    rank_count = own_ranks * shards
    vmem = pl.BlockSpec(memory_space=pltpu.VMEM)
    return pl.pallas_call(
        functools.partial(inverse_kernel, own_rows),
        out_shape=(
            jax.ShapeDtypeStruct((size, size), F32),
            jax.ShapeDtypeStruct((rank_count, size), F32),
            jax.ShapeDtypeStruct((3, rank_count, own_rows), F32),
            jax.ShapeDtypeStruct((1, size), F32),
        ),
        in_specs=[
            vmem,
            pl.BlockSpec(memory_space=pltpu.SMEM),
            pl.BlockSpec(memory_space=pl.ANY),
        ],
        out_specs=(pl.BlockSpec(memory_space=pl.ANY), vmem, vmem, vmem),
        scratch_shapes=[
            pltpu.VMEM((size, size), F32),
            pltpu.VMEM((3, own_rows, size), F32),
            pltpu.VMEM((BLOCK, BLOCK), F32),
            pltpu.VMEM((size, 6 * BLOCK), BF16),
            pltpu.VMEM((6 * BLOCK, size), BF16),
            pltpu.VMEM((size, BLOCK), F32),
            pltpu.SemaphoreType.DMA((2,)),
        ],
        compiler_params=pltpu.CompilerParams(vmem_limit_bytes=INVERSE_VMEM),
        cost_estimate=pl.CostEstimate(
            flops=40 * 10**9, bytes_accessed=10 * 2**20, transcendentals=0
        ),
        name="inverse",
    )(gathered, col_rank, diag)


def split2(x):
    hi = x.astype(BF16)
    return hi, (x - hi.astype(F32)).astype(BF16)


def dot_split(left, right, dims=NN):
    left_hi, left_lo = left
    right_hi, right_lo = right
    rows = left_hi.shape[0]
    both = lax.dot_general(
        jnp.concatenate([left_hi, left_lo], axis=0), right_hi, dims, preferred_element_type=F32
    )
    cross = lax.dot_general(left_hi, right_lo, dims, preferred_element_type=F32)
    return both[:rows] + (both[rows:] + cross)


def keep_rows(x, rank):
    return jnp.where(lax.broadcasted_iota(jnp.int32, x.shape, 0) < rank, x, 0.0)


def put(refs, at, x):
    hi, lo = split2(x)
    refs[0][at] = hi
    refs[1][at] = lo


def put_shards(refs, slot, sources, position, p, comp, rank):
    count = len(sources)
    width = sources[0].shape[-1]
    rank_count = sources[0].shape[-2]
    for s, ref in enumerate(sources):
        owner = lax.rem(position - s + count, count)
        at = pl.ds(pl.multiple_of(owner * width, width), width)
        put(refs, (p, pl.ds(slot * rank_count, rank_count), at), keep_rows(ref[p, comp], rank))


def col_component(ref, comp, rank):
    whole = jnp.concatenate([ref[g, comp] for g in range(ref.shape[0])], axis=0)
    return keep_rows(whole, rank)


def recompress_kernel(
    tiles, shards, place, panel_rank, col_rank, tile_rank, keep_rank, *refs
):
    first_any = refs[:shards]
    second_any = refs[shards : 2 * shards]
    (
        cols_any,
        trailing_any,
        sketch,
        solved,
        inverse_any,
        scale,
        products,
        out_any,
        left_hi,
        left_lo,
        right_hi,
        right_lo,
        panel_hi,
        panel_lo,
        cols,
        trailing,
        first_all,
        second_all,
        inverse,
        out,
        sems,
    ) = refs[2 * shards :]
    first = [first_all.at[i] for i in range(shards)]
    second = [second_all.at[i] for i in range(shards)]
    pairs = [(cols_any, cols)]
    pairs += [(trailing_any.at[p], trailing.at[p]) for p in range(tiles)]
    pairs += list(zip(first_any, first)) + list(zip(second_any, second))
    pairs.append((inverse_any, inverse))
    copies = [
        pltpu.make_async_copy(source, target, sems.at[i])
        for i, (source, target) in enumerate(pairs)
    ]
    for copy in copies:
        copy.start()
    stores = []

    def store(p, begin):
        part = pl.ds(begin, 4)
        copy = pltpu.make_async_copy(
            out.at[p, 0, part], out_any.at[p, 0, part], sems.at[len(pairs) + len(stores)]
        )
        copy.start()
        stores.append(copy)

    lefts, rights, panels = (left_hi, left_lo), (right_hi, right_lo), (panel_hi, panel_lo)
    rank_count, size = sketch.shape
    up_scale = math.sqrt(size)
    down_scale = 1.0 / math.sqrt(rank_count)
    position = place[0]
    block = lambda x, i: x[:, i * rank_count : (i + 1) * rank_count]
    band = lambda x, i: x[i * rank_count : (i + 1) * rank_count]
    slot = lambda p, i, n=1: (p, slice(i * rank_count, (i + n) * rank_count), slice(None))
    take = lambda pair, at: (pair[0][at], pair[1][at])

    copies[0].wait()
    for t in range(4):
        u_col = col_component(cols, t, col_rank[0])
        for p in range(tiles):
            put(rights, slot(p, 1 if t == 0 else 4 + t), u_col)
    for p in range(tiles):
        copies[1 + p].wait()
        for t in range(4):
            rank = tile_rank[p, 0]
            put(lefts, slot(p, 0 if t == 0 else 1 + t), keep_rows(trailing[p, 0, t], rank))
            put(rights, slot(p, 0 if t == 0 else 1 + t), keep_rows(trailing[p, 0, 4 + t], rank))
    for copy in copies[1 + tiles : -1]:
        copy.wait()
    for p in range(tiles):
        put_shards(lefts, 1, first, position, p, 0, panel_rank[p])
        put_shards(panels, 0, first, position, p, 1, panel_rank[p])
        for t in range(3):
            put_shards(lefts, 5 + t, second, position, p, t, panel_rank[p])
            put_shards(panels, 1 + t, second, position, p, 3 + t, panel_rank[p])

    sides = []
    for t in range(3):
        whole = jnp.concatenate([products[r, t] for r in range(products.shape[0])], axis=1)
        sides.append(col_component(cols, 5 + t, col_rank[0]) - whole)
    sides = jnp.concatenate(sides, axis=0) * scale[...]
    copies[-1].wait()
    dz = dot_split(split2(sides), split2(inverse[...])) * scale[...]
    z_hi, z_lo = split2(solved[...])
    dz_hi, dz_lo = split2(dz)
    zz = (jnp.concatenate([z_hi, dz_hi], axis=0), jnp.concatenate([z_lo, dz_lo], axis=0))
    s = split2(sketch[...])

    state = []
    for p in range(tiles):
        live = lax.broadcasted_iota(jnp.int32, (rank_count, 1), 0) < keep_rank[p, 0]
        mixes = dot_split(take(panels, slot(p, 0, 4)), zz, NT)
        sketched = jnp.where(live, dot_split(s, take(rights, slot(p, 0, 8)), NT), 0.0)
        mix = mixes[:rank_count, :rank_count]
        base_u = -mm(block(sketched, 1), mix, NT)
        pair = jnp.concatenate([block(sketched, 0), base_u], axis=1)
        bases = take(lefts, slot(p, 0, 2))
        y = dot_split(split2(pair), bases)
        y_split = split2(y)
        gram = dot_split(y_split, y_split, NT)
        eye = lax.broadcasted_iota(jnp.int32, gram.shape, 0) == lax.broadcasted_iota(
            jnp.int32, gram.shape, 1
        )
        gram = gram + jnp.where(eye & jnp.logical_not(live), 1.0, 0.0)
        augmented = jnp.concatenate([gram, jnp.where(eye, 1.0, 0.0)], axis=1)
        cross = dot_split(bases, take(lefts, slot(p, 0, 8)), NT)
        state.append((mixes, sketched, pair, cross, augmented))

    factors = [factor_inverse(as_rows(entry[-1]), rank_count) for entry in state]

    for p in range(tiles):
        mixes, sketched, pair, cross, _ = state[p]
        rinv = jnp.concatenate(factors[p], axis=0)[:, rank_count:]
        mix = mixes[:rank_count, :rank_count]
        dmix = [band(block(mixes, 0), 1 + t) + band(block(mixes, 1 + t), 0) for t in range(3)]
        su = [block(sketched, 1)] + [block(sketched, 5 + t) for t in range(3)]
        u_mix = mm(jnp.concatenate(su[1:], axis=0), mix, NT)
        u_dmix = mm(su[0], jnp.concatenate(dmix, axis=0), NT)
        u_sides = [-(band(u_mix, t) + block(u_dmix, t)) for t in range(3)]
        sv = [block(sketched, 2 + t) for t in range(3)]
        coefs = mm(rinv, jnp.concatenate([pair] + sv + u_sides, axis=1))
        q_coef = coefs[:, : 2 * rank_count]
        q_parts = mm(q_coef, cross)
        phis = []
        for t in range(3):
            e_coef = jnp.concatenate(
                [block(coefs, 2 + t), block(coefs, 5 + t), q_coef], axis=1
            )
            q_side = jnp.concatenate(
                [block(q_parts, 0), block(q_parts, 1), block(q_parts, 2 + t), block(q_parts, 5 + t)],
                axis=1,
            )
            half = mm(e_coef, q_side, NT)
            sym = half + half.T
            i0 = lax.broadcasted_iota(jnp.int32, sym.shape, 0)
            i1 = lax.broadcasted_iota(jnp.int32, sym.shape, 1)
            phis.append(jnp.where(i0 > i1, sym, jnp.where(i0 == i1, 0.5 * sym, 0.0)))
        turned = mm(jnp.concatenate(phis, axis=0), q_coef)
        none = jnp.zeros((rank_count, rank_count), F32)
        rows = [jnp.concatenate([q_coef] + [none] * 6, axis=1)]
        for t in range(3):
            head = jnp.concatenate([block(coefs, 2 + t), block(coefs, 5 + t)], axis=1)
            tail = [none] * 6
            tail[t], tail[3 + t] = block(q_coef, 0), block(q_coef, 1)
            rows.append(jnp.concatenate([head - band(turned, t)] + tail, axis=1))
        basis_coef = jnp.concatenate(rows, axis=0)
        basis = dot_split(split2(basis_coef), take(lefts, slot(p, 0, 8))) * up_scale
        for t in range(4):
            out[p, 0, t] = band(basis, t)
        store(p, 0)
        dq_parts = mm(basis_coef[rank_count:], cross, NT)
        on_u = mm(
            block(dq_parts, 1)
            + jnp.concatenate([block(q_parts, 5 + t) for t in range(3)], axis=0),
            mix,
        )
        on_dmix = mm(block(q_parts, 1), jnp.concatenate(dmix, axis=1))
        q_mix = mm(block(q_parts, 1), mix)
        rows = [jnp.concatenate([block(q_parts, 0), -q_mix] + [none] * 6, axis=1)]
        for t in range(3):
            on_v = band(block(dq_parts, 0), t) + block(q_parts, 2 + t)
            tail = [none] * 6
            tail[t], tail[3 + t] = block(q_parts, 0), -q_mix
            rows.append(
                jnp.concatenate([on_v, -(band(on_u, t) + block(on_dmix, t))] + tail, axis=1)
            )
        coeff = dot_split(
            split2(jnp.concatenate(rows, axis=0) * down_scale), take(rights, slot(p, 0, 8))
        )
        for t in range(4):
            out[p, 0, 4 + t] = band(coeff, t)
        store(p, 4)
    for copy in stores:
        copy.wait()


def run_recompress(
    place, ranks, first, second, cols, trailing, sketch, solved, inverse, scale, products
):
    tiles = trailing.shape[0]
    rank_count, size = sketch.shape
    vmem = pl.BlockSpec(memory_space=pltpu.VMEM)
    smem = pl.BlockSpec(memory_space=pltpu.SMEM)
    hbm = pl.BlockSpec(memory_space=pl.ANY)
    return pl.pallas_call(
        functools.partial(recompress_kernel, tiles, len(first)),
        out_shape=jax.ShapeDtypeStruct(trailing.shape, F32),
        in_specs=[smem] * 5
        + [hbm] * (2 * len(first) + 2)
        + [vmem] * 2
        + [hbm]
        + [vmem] * 2,
        out_specs=hbm,
        scratch_shapes=[pltpu.VMEM((tiles, 8 * rank_count, size), BF16)] * 4
        + [pltpu.VMEM((tiles, 4 * rank_count, size), BF16)] * 2
        + [
            pltpu.VMEM(cols.shape, F32),
            pltpu.VMEM(trailing.shape, F32),
            pltpu.VMEM((len(first),) + first[0].shape, F32),
            pltpu.VMEM((len(second),) + second[0].shape, F32),
            pltpu.VMEM(inverse.shape, F32),
            pltpu.VMEM(trailing.shape, F32),
            pltpu.SemaphoreType.DMA((2 + tiles + 2 * len(first) + 2 * tiles,)),
        ],
        compiler_params=pltpu.CompilerParams(vmem_limit_bytes=RECOMPRESS_VMEM),
        cost_estimate=pl.CostEstimate(
            flops=10 * 10**9, bytes_accessed=20 * 2**20, transcendentals=0
        ),
        name="recompress",
    )(place, *ranks, *first, *second, cols, trailing, sketch, solved, inverse, scale, products)


def on_device(
    row_count,
    col_count,
    diag,
    panel_rows,
    panel_cols,
    trailing,
    sketch,
    panel_rank,
    col_rank,
    tile_rank,
    keep_rank,
):
    own_rows = diag.shape[1]
    own_ranks = panel_cols.shape[2]
    comps = panel_cols.shape[1]
    size = sketch.shape[1]
    values = panel_cols[0, 4]
    own = diag[0]
    if own_rows == BLOCK and row_count > 2:
        width = (row_count // 2 + 1) * BLOCK
        own = lax.dynamic_slice(
            jnp.concatenate([own, own[:, : width - BLOCK]], axis=1),
            (0, lax.axis_index("row") * BLOCK),
            (BLOCK, width),
        )
        values = jnp.pad(values, ((0, 0), (0, -size % width)))
        values = jnp.concatenate(
            [values[:, i : i + width] for i in range(0, values.shape[1], width)], axis=0
        )
    gathered = lax.all_gather(jnp.concatenate([own, values], axis=0), "row", axis=0)
    first = panel_rows[:, 0::4]
    second = jnp.concatenate([panel_rows[:, 1:4], panel_rows[:, 5:8]], axis=1)
    first_shards, second_shards = [first], [second]
    for source, shards in ((first, first_shards), (second, second_shards)):
        for s in range(1, col_count):
            shards.append(
                lax.ppermute(source, "col", [(i, (i + s) % col_count) for i in range(col_count)])
            )
    late_cols, gathered = lax.optimization_barrier((panel_cols[0], gathered))
    cols = lax.all_gather(late_cols, "row", axis=0)
    if own_ranks != SUB:
        cols = cols.reshape(-1, SUB // own_ranks, comps, own_ranks, size)
        cols = cols.transpose(0, 2, 1, 3, 4).reshape(-1, comps, SUB, size)
    inverse, solved, products, scale = run_inverse(
        gathered, diag, col_rank, own_ranks
    )
    all_products = lax.all_gather(products, "row", axis=0)
    place = lax.axis_index("col").astype(jnp.int32).reshape(1)
    ranks = (panel_rank, col_rank, tile_rank, keep_rank)
    return run_recompress(
        place,
        ranks,
        first_shards,
        second_shards,
        cols,
        trailing,
        sketch,
        solved,
        inverse,
        scale,
        all_products,
    )


def solution(mesh):
    in_specs = (
        P(None, "row", None),
        P("row", None, None, "col"),
        P("col", None, "row", None),
        P("row", "col", None, None, None),
        P(),
        P("row"),
        P("col"),
        P("row", "col"),
        P("row", "col"),
    )
    out_specs = P("row", "col", None, None, None)
    body = functools.partial(on_device, mesh.shape["row"], mesh.shape["col"])
    return jax.shard_map(body, mesh=mesh, in_specs=in_specs, out_specs=out_specs, check_vma=False)
```

```python
import functools
import math

import jax
import jax.numpy as jnp
from jax import lax
from jax.experimental import pallas as pl
from jax.experimental.pallas import tpu as pltpu
from jax.sharding import PartitionSpec as P

HIGHEST = lax.Precision.HIGHEST
F32 = jnp.float32
BF16 = jnp.bfloat16
BLOCK = 128
SUB = 8
BAND = 4
INVERSE_VMEM = 28 * 1024 * 1024
RECOMPRESS_VMEM = 46 * 1024 * 1024

NN = (((1,), (0,)), ((), ()))
NT = (((1,), (1,)), ((), ()))


def mm(left, right, dims=NN):
    return lax.dot_general(left, right, dims, precision=HIGHEST, preferred_element_type=F32)


def split3(x):
    hi = x.astype(BF16)
    rest = x - hi.astype(F32)
    mid = rest.astype(BF16)
    lo = (rest - mid.astype(F32)).astype(BF16)
    return hi, mid, lo


def left_terms(x):
    hi, mid, lo = split3(x)
    return jnp.concatenate([hi, hi, mid, mid, hi, lo], axis=1)


def right_terms(x):
    hi, mid, lo = split3(x)
    return jnp.concatenate([hi, mid, hi, mid, lo, hi], axis=0)


def lane_rep(x, lane):
    return jnp.broadcast_to(x[:, lane : lane + 1], (SUB, BLOCK))


def sub_rep(x, row):
    return jnp.broadcast_to(x[row : row + 1, :], (SUB, BLOCK))


def tree_sum(terms):
    while len(terms) > 1:
        terms = [
            terms[i] + terms[i + 1] if i + 1 < len(terms) else terms[i]
            for i in range(0, len(terms), 2)
        ]
    return terms[0]


def sub_index():
    return lax.broadcasted_iota(jnp.int32, (SUB, BLOCK), 0)


def lane_index():
    return lax.broadcasted_iota(jnp.int32, (SUB, BLOCK), 1)


def micro_inverse(cols):
    sub = sub_index()
    cols = list(cols)
    for j in range(0, SUB, 2):
        first, second = sub == j, sub == j + 1
        pair = first | second
        a, b, d = sub_rep(cols[j], j), sub_rep(cols[j], j + 1), sub_rep(cols[j + 1], j + 1)
        inv_det = 1.0 / (a * d - b * b)
        f0 = jnp.where(first, -1.0, jnp.where(second, 0.0, cols[j]))
        f1 = jnp.where(second, -1.0, jnp.where(first, 0.0, cols[j + 1]))
        fresh = []
        for k in range(SUB):
            if k == j:
                fresh.append((f1 * b - f0 * d) * inv_det)
            elif k == j + 1:
                fresh.append((f0 * b - f1 * a) * inv_det)
            else:
                x0, x1 = sub_rep(cols[k], j), sub_rep(cols[k], j + 1)
                change = f0 * (d * x0 - b * x1) + f1 * (a * x1 - b * x0)
                fresh.append(jnp.where(pair, 0.0, cols[k]) - change * inv_det)
        cols = fresh
    return cols


def micro_factor(cols):
    sub = sub_index()
    cols = list(cols)
    low = [jnp.where(sub == k, 1.0, 0.0) for k in range(SUB)]
    pivots = jnp.zeros((SUB, BLOCK), F32)
    for j in range(SUB):
        here = sub == j
        piv = sub_rep(cols[j], j)
        inv_piv = 1.0 / piv
        factor = jnp.where(here, -1.0, cols[j])
        pivots = jnp.where(here, piv, pivots)
        below = jnp.where(sub > j, cols[j], 0.0)
        for k in range(j + 1):
            low[k] = low[k] - below * sub_rep(low[k], j) * inv_piv
        cols = [
            -factor * inv_piv
            if k == j
            else jnp.where(here, 0.0, cols[k]) - factor * (sub_rep(cols[k], j) * inv_piv)
            for k in range(SUB)
        ]
    scale = lax.rsqrt(pivots)
    return cols, [scale * c for c in low]


def band_left(x, band):
    lanes = BAND * SUB
    hi = x.astype(BF16).astype(F32)
    rest = x - hi
    mid = rest.astype(BF16).astype(F32)
    lo = rest - mid
    place = lax.rem(
        lax.broadcasted_iota(jnp.int32, x.shape, 1) // lanes - band + BLOCK // lanes, BLOCK // lanes
    )
    hi_next = pltpu.roll(hi, lanes, 1)
    mid_two = pltpu.roll(mid, 2 * lanes, 1)
    mid_three = pltpu.roll(mid, 3 * lanes, 1)
    one = jnp.where(
        place == 0, hi, jnp.where(place == 1, hi_next, jnp.where(place == 2, mid_two, mid_three))
    )
    two = jnp.where(place == 0, lo, jnp.where(place == 1, hi_next, 0.0))
    return jnp.concatenate([one, two], axis=1).astype(BF16)


def band_right(x, band):
    hi, mid, lo = split3(x)
    none = jnp.zeros(x.shape, BF16)
    turn = lambda parts: [parts[(i - band) % len(parts)] for i in range(len(parts))]
    return jnp.concatenate(turn([hi, mid, hi, mid]) + turn([hi, lo, none, none]), axis=0)


def block_inverse(rows, ahead, below, below_ahead, work):
    rows, ahead, below, below_ahead = list(rows), list(ahead), list(below), list(below_ahead)
    count = len(rows)
    sub, lane = sub_index(), lane_index()
    for first in range(0, count, BAND):
        band = range(first, first + BAND)
        others = [(first + BAND + i) % count for i in range(count - BAND)]
        left = band_left(
            jnp.concatenate([rows[i] for i in others] + below, axis=0), first // BAND
        )
        for g in band:
            at = g * SUB
            inside = (lane >= at) & (lane < at + SUB)
            inv = micro_inverse([lane_rep(rows[g], at + k) for k in range(SUB)])
            own = jnp.where(inside, jnp.where(lane - at == sub, 1.0, 0.0), rows[g])
            new = tree_sum([inv[k] * sub_rep(own, k) for k in range(SUB)])
            news = [sub_rep(new, k) for k in range(SUB)]
            new_ahead = tree_sum([inv[k] * sub_rep(ahead[g], k) for k in range(SUB)])
            news_ahead = [sub_rep(new_ahead, k) for k in range(SUB)]
            for i in [first + (g - first + 1 + i) % BAND for i in range(BAND - 1)]:
                factors = [lane_rep(rows[i], at + k) for k in range(SUB)]
                kept = jnp.where(inside, 0.0, rows[i])
                rows[i] = kept - tree_sum([factors[k] * news[k] for k in range(SUB)])
                ahead[i] = ahead[i] - tree_sum([factors[k] * news_ahead[k] for k in range(SUB)])
            rows[g], ahead[g] = new, new_ahead
            for piece in work[g * len(work) // count : (g + 1) * len(work) // count]:
                piece()
        inside = (lane >= first * SUB) & (lane < (first + BAND) * SUB)
        top = jnp.concatenate(
            [jnp.concatenate([x[i] for i in band], axis=0) for x in (rows, ahead)], axis=1
        )
        change = lax.dot_general(
            left, band_right(top, first // BAND), NN, preferred_element_type=F32
        )
        here, there = as_rows(change[:, :BLOCK]), as_rows(change[:, BLOCK:])
        for j, i in enumerate(others):
            rows[i] = jnp.where(inside, 0.0, rows[i]) - here[j]
            ahead[i] = ahead[i] - there[j]
        for j in range(count):
            below[j] = below[j] - here[len(others) + j]
            below_ahead[j] = below_ahead[j] - there[len(others) + j]
    return rows, below_ahead


def factor_inverse(rows, width):
    rows = list(rows)
    count = width // SUB
    for g in range(count):
        at = g * SUB
        inv, low = micro_factor([lane_rep(rows[g], at + k) for k in range(SUB)])
        own = rows[g]
        own_rep = [sub_rep(own, k) for k in range(SUB)]
        new = tree_sum([inv[k] * own_rep[k] for k in range(SUB)])
        news = [sub_rep(new, k) for k in range(SUB)]
        for i in range(g + 1, count):
            rows[i] = rows[i] - tree_sum(
                [lane_rep(rows[i], at + k) * news[k] for k in range(SUB)]
            )
        rows[g] = tree_sum([low[k] * own_rep[k] for k in range(SUB)])
    return rows


def as_rows(x):
    return [x[i * SUB : (i + 1) * SUB, :] for i in range(x.shape[0] // SUB)]


def inverse_kernel(
    own_rows,
    gathered_hbm,
    col_rank,
    diag,
    inverse_out,
    solved,
    products,
    scale_row,
    inverse,
    tangents,
    gathered,
    pivot,
    upcoming,
    left,
    right,
    scale_col,
    sems,
):
    size = inverse.shape[0]
    steps = size // BLOCK
    shards, height, width = gathered.shape
    fetch = pltpu.make_async_copy(diag.at[pl.ds(1, 3)], tangents, sems.at[0])
    receive = pltpu.make_async_copy(gathered_hbm, gathered, sems.at[2])
    receive.start()
    fetch.start()
    receive.wait()
    eye = lax.broadcasted_iota(jnp.int32, (BLOCK, BLOCK), 0) == lax.broadcasted_iota(
        jnp.int32, (BLOCK, BLOCK), 1
    )
    part = lambda c, n=BLOCK: slice(c * n, (c + 1) * n)

    def set_scale(c, block):
        own = jnp.where(eye, block, 0.0)
        scale_row[:, part(c)] = lax.rsqrt(jnp.sum(own, axis=0, keepdims=True))
        scale_col[part(c), :] = jnp.broadcast_to(
            lax.rsqrt(jnp.sum(own, axis=1, keepdims=True)), (BLOCK, BLOCK)
        )

    if width < size:
        for c in range(steps):
            set_scale(c, gathered[c, :BLOCK, :BLOCK])
        for r in range(steps):
            for o in range(width // BLOCK):
                c = (r + o) % steps
                block = gathered[r, :BLOCK, part(o)] * scale_col[part(r), :] * scale_row[:, part(c)]
                inverse[part(r), part(c)] = block
                if 0 < o and 2 * o < steps:
                    inverse[part(c), part(r)] = block.T
    else:
        for r in range(shards):
            inverse[part(r, own_rows), :] = gathered[r, :own_rows, :]
        for c in range(steps):
            set_scale(c, inverse[part(c), part(c)])
        for r in range(steps):
            for c in range(steps):
                inverse[part(r), part(c)] = (
                    inverse[part(r), part(c)] * scale_col[part(r), :] * scale_row[:, part(c)]
                )

    def eliminate(k, at, inv):
        chunk = 2 * BLOCK
        chunks = size // chunk
        twice = jnp.concatenate([inv, inv], axis=1)

        def fill_left(c):
            column = inverse[part(c, chunk), at]
            owner = 2 * c + lax.broadcasted_iota(jnp.int32, column.shape, 0) // BLOCK
            left[part(c, chunk), :] = left_terms(jnp.where(owner == k, 0.0, column))
            inverse[part(c, chunk), at] = jnp.zeros((chunk, BLOCK), F32)

        def fill_right(c):
            row = mm(inv, inverse[at, part(c, chunk)])
            owner = 2 * c + lax.broadcasted_iota(jnp.int32, row.shape, 1) // BLOCK
            row = jnp.where(owner == k, twice, row)
            right[:, part(c, chunk)] = right_terms(row)
            inverse[at, part(c, chunk)] = row

        def update(r, c):
            here = (part(r, chunk), part(c, chunk))
            inverse[here] = inverse[here] - lax.dot_general(
                left[here[0], :], right[:, here[1]], NN, preferred_element_type=F32
            )

        work = [functools.partial(fill_left, c) for c in range(chunks)]
        for c in range(chunks):
            work.append(functools.partial(fill_right, c))
            work += [functools.partial(update, r, c) for r in range(chunks)]
        return work

    def invert_to_pivot(blocks, work):
        inv, following = block_inverse(*[as_rows(block) for block in blocks], work)
        pivot[...] = jnp.concatenate(inv, axis=0)
        upcoming[...] = jnp.concatenate(following, axis=0)

    one, two = part(0), part(1)
    invert_to_pivot([inverse[one, one], inverse[one, two], inverse[two, one], inverse[two, two]], [])

    def step(k, carry):
        at = pl.ds(pl.multiple_of(k * BLOCK, BLOCK), BLOCK)
        one = pl.ds(pl.multiple_of((k + 1) * BLOCK, BLOCK), BLOCK)
        two = pl.ds(pl.multiple_of(lax.min(k + 2, steps - 1) * BLOCK, BLOCK), BLOCK)
        inv = pivot[...]
        block = upcoming[...]
        row = mm(inv, jnp.concatenate([inverse[at, one], inverse[at, two]], axis=1))
        ahead = inverse[one, two] - mm(inverse[one, at], row[:, BLOCK:])
        change = mm(inverse[two, at], row)
        below = inverse[two, one] - change[:, :BLOCK]
        below_ahead = inverse[two, two] - change[:, BLOCK:]
        invert_to_pivot([block, ahead, below, below_ahead], eliminate(k, at, inv))
        return carry

    lax.fori_loop(0, steps - 1, step, 0)
    for piece in eliminate(steps - 1, slice(size - BLOCK, size), pivot[...]):
        piece()
    store = pltpu.make_async_copy(inverse, inverse_out, sems.at[1])
    store.start()

    rank_count = solved.shape[0]
    own_ranks = rank_count // shards
    values = []
    for r in range(shards):
        pieces = []
        for at in range(own_rows, height, own_ranks):
            pieces.append(gathered[r, at : at + own_ranks, :])
        values.append(jnp.concatenate(pieces, axis=1)[:, :size])
    values = keep_rows(jnp.concatenate(values, axis=0), col_rank[0])
    z = mm(values * scale_row[...], inverse[...]) * scale_row[...]
    solved[...] = z
    fetch.wait()
    for t in range(3):
        products[t] = mm(z, tangents[t], NT)
    store.wait()


def run_inverse(gathered, diag, col_rank, own_ranks):
    shards = gathered.shape[0]
    _, own_rows, size = diag.shape
    rank_count = own_ranks * shards
    vmem = pl.BlockSpec(memory_space=pltpu.VMEM)
    hbm = pl.BlockSpec(memory_space=pltpu.HBM)
    return pl.pallas_call(
        functools.partial(inverse_kernel, own_rows),
        out_shape=(
            jax.ShapeDtypeStruct((size, size), F32),
            jax.ShapeDtypeStruct((rank_count, size), F32),
            jax.ShapeDtypeStruct((3, rank_count, own_rows), F32),
            jax.ShapeDtypeStruct((1, size), F32),
        ),
        in_specs=[hbm, pl.BlockSpec(memory_space=pltpu.SMEM), hbm],
        out_specs=(hbm, vmem, vmem, vmem),
        scratch_shapes=[
            pltpu.VMEM((size, size), F32),
            pltpu.VMEM((3, own_rows, size), F32),
            pltpu.VMEM(gathered.shape, F32),
            pltpu.VMEM((BLOCK, BLOCK), F32),
            pltpu.VMEM((BLOCK, BLOCK), F32),
            pltpu.VMEM((size, 6 * BLOCK), BF16),
            pltpu.VMEM((6 * BLOCK, size), BF16),
            pltpu.VMEM((size, BLOCK), F32),
            pltpu.SemaphoreType.DMA((3,)),
        ],
        compiler_params=pltpu.CompilerParams(vmem_limit_bytes=INVERSE_VMEM),
        cost_estimate=pl.CostEstimate(
            flops=40 * 10**9, bytes_accessed=10 * 2**20, transcendentals=0
        ),
        name="inverse",
    )(gathered, col_rank, diag)


def split2(x):
    hi = x.astype(BF16)
    return hi, (x - hi.astype(F32)).astype(BF16)


def dot_split(left, right, dims=NN):
    left_hi, left_lo = left
    right_hi, right_lo = right
    rows = left_hi.shape[0]
    both = lax.dot_general(
        jnp.concatenate([left_hi, left_lo], axis=0), right_hi, dims, preferred_element_type=F32
    )
    cross = lax.dot_general(left_hi, right_lo, dims, preferred_element_type=F32)
    return both[:rows] + (both[rows:] + cross)


def keep_rows(x, rank):
    return jnp.where(lax.broadcasted_iota(jnp.int32, x.shape, 0) < rank, x, 0.0)


def put(refs, at, x):
    hi, lo = split2(x)
    refs[0][at] = hi
    refs[1][at] = lo


def put_shards(refs, slot, sources, position, p, comp, rank):
    count = len(sources)
    width = sources[0].shape[-1]
    rank_count = sources[0].shape[-2]
    for s, ref in enumerate(sources):
        owner = lax.rem(position - s + count, count)
        at = pl.ds(pl.multiple_of(owner * width, width), width)
        put(refs, (p, pl.ds(slot * rank_count, rank_count), at), keep_rows(ref[p, comp], rank))


def col_component(ref, comp, rank):
    whole = jnp.concatenate([ref[g, comp] for g in range(ref.shape[0])], axis=0)
    return keep_rows(whole, rank)


def recompress_kernel(
    tiles, shards, place, panel_rank, col_rank, tile_rank, keep_rank, *refs
):
    first_any = refs[:shards]
    second_any = refs[shards : 2 * shards]
    (
        cols_any,
        trailing_any,
        sketch_any,
        solved_any,
        inverse_any,
        scale,
        products_any,
        out_any,
        left_hi,
        left_lo,
        right_hi,
        right_lo,
        panel_hi,
        panel_lo,
        cols,
        trailing,
        first_all,
        second_all,
        inverse,
        sketch,
        solved,
        products,
        out,
        sems,
    ) = refs[2 * shards :]
    first = [first_all.at[i] for i in range(shards)]
    second = [second_all.at[i] for i in range(shards)]
    pairs = [(cols_any, cols)]
    pairs += [(trailing_any.at[p], trailing.at[p]) for p in range(tiles)]
    pairs += list(zip(first_any, first)) + list(zip(second_any, second))
    pairs += [(sketch_any, sketch), (solved_any, solved), (products_any, products)]
    pairs.append((inverse_any, inverse))
    copies = [
        pltpu.make_async_copy(source, target, sems.at[i])
        for i, (source, target) in enumerate(pairs)
    ]
    for copy in copies:
        copy.start()
    stores = []

    def store(p, begin):
        part = pl.ds(begin, 4)
        copy = pltpu.make_async_copy(
            out.at[p, 0, part], out_any.at[p, 0, part], sems.at[len(pairs) + len(stores)]
        )
        copy.start()
        stores.append(copy)

    lefts, rights, panels = (left_hi, left_lo), (right_hi, right_lo), (panel_hi, panel_lo)
    rank_count, size = sketch.shape
    up_scale = math.sqrt(size)
    down_scale = 1.0 / math.sqrt(rank_count)
    position = place[0]
    block = lambda x, i: x[:, i * rank_count : (i + 1) * rank_count]
    band = lambda x, i: x[i * rank_count : (i + 1) * rank_count]
    slot = lambda p, i, n=1: (p, slice(i * rank_count, (i + n) * rank_count), slice(None))
    take = lambda pair, at: (pair[0][at], pair[1][at])

    copies[0].wait()
    for t in range(4):
        u_col = col_component(cols, t, col_rank[0])
        for p in range(tiles):
            put(rights, slot(p, 1 if t == 0 else 4 + t), u_col)
    for p in range(tiles):
        copies[1 + p].wait()
        for t in range(4):
            rank = tile_rank[p, 0]
            put(lefts, slot(p, 0 if t == 0 else 1 + t), keep_rows(trailing[p, 0, t], rank))
            put(rights, slot(p, 0 if t == 0 else 1 + t), keep_rows(trailing[p, 0, 4 + t], rank))
    for copy in copies[1 + tiles : -1]:
        copy.wait()
    for p in range(tiles):
        put_shards(lefts, 1, first, position, p, 0, panel_rank[p])
        put_shards(panels, 0, first, position, p, 1, panel_rank[p])
        for t in range(3):
            put_shards(lefts, 5 + t, second, position, p, t, panel_rank[p])
            put_shards(panels, 1 + t, second, position, p, 3 + t, panel_rank[p])

    sides = []
    for t in range(3):
        whole = jnp.concatenate([products[r, t] for r in range(products.shape[0])], axis=1)
        sides.append(col_component(cols, 5 + t, col_rank[0]) - whole)
    sides = jnp.concatenate(sides, axis=0) * scale[...]
    copies[-1].wait()
    dz = dot_split(split2(sides), split2(inverse[...])) * scale[...]
    z_hi, z_lo = split2(solved[...])
    dz_hi, dz_lo = split2(dz)
    zz = (jnp.concatenate([z_hi, dz_hi], axis=0), jnp.concatenate([z_lo, dz_lo], axis=0))
    s = split2(sketch[...])

    state = []
    for p in range(tiles):
        live = lax.broadcasted_iota(jnp.int32, (rank_count, 1), 0) < keep_rank[p, 0]
        mixes = dot_split(take(panels, slot(p, 0, 4)), zz, NT)
        sketched = jnp.where(live, dot_split(s, take(rights, slot(p, 0, 8)), NT), 0.0)
        mix = mixes[:rank_count, :rank_count]
        base_u = -mm(block(sketched, 1), mix, NT)
        pair = jnp.concatenate([block(sketched, 0), base_u], axis=1)
        bases = take(lefts, slot(p, 0, 2))
        y = dot_split(split2(pair), bases)
        y_split = split2(y)
        gram = dot_split(y_split, y_split, NT)
        eye = lax.broadcasted_iota(jnp.int32, gram.shape, 0) == lax.broadcasted_iota(
            jnp.int32, gram.shape, 1
        )
        gram = gram + jnp.where(eye & jnp.logical_not(live), 1.0, 0.0)
        augmented = jnp.concatenate([gram, jnp.where(eye, 1.0, 0.0)], axis=1)
        cross = dot_split(bases, take(lefts, slot(p, 0, 8)), NT)
        state.append((mixes, sketched, pair, cross, augmented))

    factors = [factor_inverse(as_rows(entry[-1]), rank_count) for entry in state]

    for p in range(tiles):
        mixes, sketched, pair, cross, _ = state[p]
        rinv = jnp.concatenate(factors[p], axis=0)[:, rank_count:]
        mix = mixes[:rank_count, :rank_count]
        dmix = [band(block(mixes, 0), 1 + t) + band(block(mixes, 1 + t), 0) for t in range(3)]
        su = [block(sketched, 1)] + [block(sketched, 5 + t) for t in range(3)]
        u_mix = mm(jnp.concatenate(su[1:], axis=0), mix, NT)
        u_dmix = mm(su[0], jnp.concatenate(dmix, axis=0), NT)
        u_sides = [-(band(u_mix, t) + block(u_dmix, t)) for t in range(3)]
        sv = [block(sketched, 2 + t) for t in range(3)]
        coefs = mm(rinv, jnp.concatenate([pair] + sv + u_sides, axis=1))
        q_coef = coefs[:, : 2 * rank_count]
        q_parts = mm(q_coef, cross)
        phis = []
        for t in range(3):
            e_coef = jnp.concatenate(
                [block(coefs, 2 + t), block(coefs, 5 + t), q_coef], axis=1
            )
            q_side = jnp.concatenate(
                [block(q_parts, 0), block(q_parts, 1), block(q_parts, 2 + t), block(q_parts, 5 + t)],
                axis=1,
            )
            half = mm(e_coef, q_side, NT)
            sym = half + half.T
            i0 = lax.broadcasted_iota(jnp.int32, sym.shape, 0)
            i1 = lax.broadcasted_iota(jnp.int32, sym.shape, 1)
            phis.append(jnp.where(i0 > i1, sym, jnp.where(i0 == i1, 0.5 * sym, 0.0)))
        turned = mm(jnp.concatenate(phis, axis=0), q_coef)
        none = jnp.zeros((rank_count, rank_count), F32)
        rows = [jnp.concatenate([q_coef] + [none] * 6, axis=1)]
        for t in range(3):
            head = jnp.concatenate([block(coefs, 2 + t), block(coefs, 5 + t)], axis=1)
            tail = [none] * 6
            tail[t], tail[3 + t] = block(q_coef, 0), block(q_coef, 1)
            rows.append(jnp.concatenate([head - band(turned, t)] + tail, axis=1))
        basis_coef = jnp.concatenate(rows, axis=0)
        basis = dot_split(split2(basis_coef), take(lefts, slot(p, 0, 8))) * up_scale
        for t in range(4):
            out[p, 0, t] = band(basis, t)
        store(p, 0)
        dq_parts = mm(basis_coef[rank_count:], cross, NT)
        on_u = mm(
            block(dq_parts, 1)
            + jnp.concatenate([block(q_parts, 5 + t) for t in range(3)], axis=0),
            mix,
        )
        on_dmix = mm(block(q_parts, 1), jnp.concatenate(dmix, axis=1))
        q_mix = mm(block(q_parts, 1), mix)
        rows = [jnp.concatenate([block(q_parts, 0), -q_mix] + [none] * 6, axis=1)]
        for t in range(3):
            on_v = band(block(dq_parts, 0), t) + block(q_parts, 2 + t)
            tail = [none] * 6
            tail[t], tail[3 + t] = block(q_parts, 0), -q_mix
            rows.append(
                jnp.concatenate([on_v, -(band(on_u, t) + block(on_dmix, t))] + tail, axis=1)
            )
        coeff = dot_split(
            split2(jnp.concatenate(rows, axis=0) * down_scale), take(rights, slot(p, 0, 8))
        )
        for t in range(4):
            out[p, 0, 4 + t] = band(coeff, t)
        store(p, 4)
    for copy in stores:
        copy.wait()


def run_recompress(
    place, ranks, first, second, cols, trailing, sketch, solved, inverse, scale, products
):
    tiles = trailing.shape[0]
    rank_count, size = sketch.shape
    vmem = pl.BlockSpec(memory_space=pltpu.VMEM)
    smem = pl.BlockSpec(memory_space=pltpu.SMEM)
    hbm = pl.BlockSpec(memory_space=pltpu.HBM)
    return pl.pallas_call(
        functools.partial(recompress_kernel, tiles, len(first)),
        out_shape=jax.ShapeDtypeStruct(trailing.shape, F32),
        in_specs=[smem] * 5
        + [hbm] * (2 * len(first) + 5)
        + [vmem, hbm],
        out_specs=hbm,
        scratch_shapes=[pltpu.VMEM((tiles, 8 * rank_count, size), BF16)] * 4
        + [pltpu.VMEM((tiles, 4 * rank_count, size), BF16)] * 2
        + [
            pltpu.VMEM(cols.shape, F32),
            pltpu.VMEM(trailing.shape, F32),
            pltpu.VMEM((len(first),) + first[0].shape, F32),
            pltpu.VMEM((len(second),) + second[0].shape, F32),
            pltpu.VMEM(inverse.shape, F32),
            pltpu.VMEM(sketch.shape, F32),
            pltpu.VMEM(solved.shape, F32),
            pltpu.VMEM(products.shape, F32),
            pltpu.VMEM(trailing.shape, F32),
            pltpu.SemaphoreType.DMA((5 + tiles + 2 * len(first) + 2 * tiles,)),
        ],
        compiler_params=pltpu.CompilerParams(vmem_limit_bytes=RECOMPRESS_VMEM),
        cost_estimate=pl.CostEstimate(
            flops=10 * 10**9, bytes_accessed=20 * 2**20, transcendentals=0
        ),
        name="recompress",
    )(place, *ranks, *first, *second, cols, trailing, sketch, solved, inverse, scale, products)


def on_device(
    row_count,
    col_count,
    diag,
    panel_rows,
    panel_cols,
    trailing,
    sketch,
    panel_rank,
    col_rank,
    tile_rank,
    keep_rank,
):
    own_rows = diag.shape[1]
    own_ranks = panel_cols.shape[2]
    comps = panel_cols.shape[1]
    size = sketch.shape[1]
    values = panel_cols[0, 4]
    own = diag[0]
    if own_rows == BLOCK and row_count > 2:
        width = (row_count // 2 + 1) * BLOCK
        own = lax.dynamic_slice(
            jnp.concatenate([own, own[:, : width - BLOCK]], axis=1),
            (0, lax.axis_index("row") * BLOCK),
            (BLOCK, width),
        )
        values = jnp.pad(values, ((0, 0), (0, -size % width)))
        values = jnp.concatenate(
            [values[:, i : i + width] for i in range(0, values.shape[1], width)], axis=0
        )
    gathered = lax.all_gather(jnp.concatenate([own, values], axis=0), "row", axis=0)
    first = panel_rows[:, 0::4]
    second = jnp.concatenate([panel_rows[:, 1:4], panel_rows[:, 5:8]], axis=1)
    first_shards, second_shards = [first], [second]
    for source, shards in ((first, first_shards), (second, second_shards)):
        for s in range(1, col_count):
            shards.append(
                lax.ppermute(source, "col", [(i, (i + s) % col_count) for i in range(col_count)])
            )
    late_cols, gathered = lax.optimization_barrier((panel_cols[0], gathered))
    cols = lax.all_gather(late_cols, "row", axis=0)
    if own_ranks != SUB:
        cols = cols.reshape(-1, SUB // own_ranks, comps, own_ranks, size)
        cols = cols.transpose(0, 2, 1, 3, 4).reshape(-1, comps, SUB, size)
    inverse, solved, products, scale = run_inverse(
        gathered, diag, col_rank, own_ranks
    )
    all_products = lax.all_gather(products, "row", axis=0)
    place = lax.axis_index("col").astype(jnp.int32).reshape(1)
    ranks = (panel_rank, col_rank, tile_rank, keep_rank)
    return run_recompress(
        place,
        ranks,
        first_shards,
        second_shards,
        cols,
        trailing,
        sketch,
        solved,
        inverse,
        scale,
        all_products,
    )


def solution(mesh):
    in_specs = (
        P(None, "row", None),
        P("row", None, None, "col"),
        P("col", None, "row", None),
        P("row", "col", None, None, None),
        P(),
        P("row"),
        P("col"),
        P("row", "col"),
        P("row", "col"),
    )
    out_specs = P("row", "col", None, None, None)
    body = functools.partial(on_device, mesh.shape["row"], mesh.shape["col"])
    return jax.shard_map(body, mesh=mesh, in_specs=in_specs, out_specs=out_specs, check_vma=False)
```

```python
import functools
import math

import jax
import jax.numpy as jnp
from jax import lax
from jax.experimental import pallas as pl
from jax.experimental.pallas import tpu as pltpu
from jax.sharding import PartitionSpec as P

HIGHEST = lax.Precision.HIGHEST
F32 = jnp.float32
BF16 = jnp.bfloat16
BLOCK = 128
SUB = 8
BAND = 4
INVERSE_VMEM = 28 * 1024 * 1024
RECOMPRESS_VMEM = 46 * 1024 * 1024

NN = (((1,), (0,)), ((), ()))
NT = (((1,), (1,)), ((), ()))


def mm(left, right, dims=NN):
    return lax.dot_general(left, right, dims, precision=HIGHEST, preferred_element_type=F32)


def split3(x):
    hi = x.astype(BF16)
    rest = x - hi.astype(F32)
    mid = rest.astype(BF16)
    lo = (rest - mid.astype(F32)).astype(BF16)
    return hi, mid, lo


def split2(x):
    hi = x.astype(BF16)
    return hi, (x - hi.astype(F32)).astype(BF16)


def left_terms(x):
    hi, lo = split2(x)
    return jnp.concatenate([hi, hi, lo, lo], axis=1)


def right_terms(x):
    hi, lo = split2(x)
    return jnp.concatenate([hi, lo, hi, lo], axis=0)


def lane_rep(x, lane):
    return jnp.broadcast_to(x[:, lane : lane + 1], (SUB, BLOCK))


def sub_rep(x, row):
    return jnp.broadcast_to(x[row : row + 1, :], (SUB, BLOCK))


def tree_sum(terms):
    while len(terms) > 1:
        terms = [
            terms[i] + terms[i + 1] if i + 1 < len(terms) else terms[i]
            for i in range(0, len(terms), 2)
        ]
    return terms[0]


def sub_index():
    return lax.broadcasted_iota(jnp.int32, (SUB, BLOCK), 0)


def lane_index():
    return lax.broadcasted_iota(jnp.int32, (SUB, BLOCK), 1)


def micro_inverse(cols):
    sub = sub_index()
    cols = list(cols)
    for j in range(0, SUB, 2):
        first, second = sub == j, sub == j + 1
        pair = first | second
        a, b, d = sub_rep(cols[j], j), sub_rep(cols[j], j + 1), sub_rep(cols[j + 1], j + 1)
        inv_det = 1.0 / (a * d - b * b)
        f0 = jnp.where(first, -1.0, jnp.where(second, 0.0, cols[j]))
        f1 = jnp.where(second, -1.0, jnp.where(first, 0.0, cols[j + 1]))
        fresh = []
        for k in range(SUB):
            if k == j:
                fresh.append((f1 * b - f0 * d) * inv_det)
            elif k == j + 1:
                fresh.append((f0 * b - f1 * a) * inv_det)
            else:
                x0, x1 = sub_rep(cols[k], j), sub_rep(cols[k], j + 1)
                change = f0 * (d * x0 - b * x1) + f1 * (a * x1 - b * x0)
                fresh.append(jnp.where(pair, 0.0, cols[k]) - change * inv_det)
        cols = fresh
    return cols


def micro_factor(cols):
    sub = sub_index()
    cols = list(cols)
    low = [jnp.where(sub == k, 1.0, 0.0) for k in range(SUB)]
    pivots = jnp.zeros((SUB, BLOCK), F32)
    for j in range(SUB):
        here = sub == j
        piv = sub_rep(cols[j], j)
        inv_piv = 1.0 / piv
        factor = jnp.where(here, -1.0, cols[j])
        pivots = jnp.where(here, piv, pivots)
        below = jnp.where(sub > j, cols[j], 0.0)
        for k in range(j + 1):
            low[k] = low[k] - below * sub_rep(low[k], j) * inv_piv
        cols = [
            -factor * inv_piv
            if k == j
            else jnp.where(here, 0.0, cols[k]) - factor * (sub_rep(cols[k], j) * inv_piv)
            for k in range(SUB)
        ]
    scale = lax.rsqrt(pivots)
    return cols, [scale * c for c in low]


def band_left(x, band):
    lanes = BAND * SUB
    hi = x.astype(BF16).astype(F32)
    rest = x - hi
    mid = rest.astype(BF16).astype(F32)
    lo = rest - mid
    place = lax.rem(
        lax.broadcasted_iota(jnp.int32, x.shape, 1) // lanes - band + BLOCK // lanes, BLOCK // lanes
    )
    hi_next = pltpu.roll(hi, lanes, 1)
    mid_two = pltpu.roll(mid, 2 * lanes, 1)
    mid_three = pltpu.roll(mid, 3 * lanes, 1)
    one = jnp.where(
        place == 0, hi, jnp.where(place == 1, hi_next, jnp.where(place == 2, mid_two, mid_three))
    )
    two = jnp.where(place == 0, lo, jnp.where(place == 1, hi_next, 0.0))
    return jnp.concatenate([one, two], axis=1).astype(BF16)


def band_right(x, band):
    hi, mid, lo = split3(x)
    none = jnp.zeros(x.shape, BF16)
    turn = lambda parts: [parts[(i - band) % len(parts)] for i in range(len(parts))]
    return jnp.concatenate(turn([hi, mid, hi, mid]) + turn([hi, lo, none, none]), axis=0)


def block_inverse(rows, ahead, below, below_ahead, work):
    rows, ahead, below, below_ahead = list(rows), list(ahead), list(below), list(below_ahead)
    count = len(rows)
    sub, lane = sub_index(), lane_index()
    for first in range(0, count, BAND):
        band = range(first, first + BAND)
        others = [(first + BAND + i) % count for i in range(count - BAND)]
        left = band_left(
            jnp.concatenate([rows[i] for i in others] + below, axis=0), first // BAND
        )
        for g in band:
            at = g * SUB
            inside = (lane >= at) & (lane < at + SUB)
            inv = micro_inverse([lane_rep(rows[g], at + k) for k in range(SUB)])
            own = jnp.where(inside, jnp.where(lane - at == sub, 1.0, 0.0), rows[g])
            new = tree_sum([inv[k] * sub_rep(own, k) for k in range(SUB)])
            news = [sub_rep(new, k) for k in range(SUB)]
            new_ahead = tree_sum([inv[k] * sub_rep(ahead[g], k) for k in range(SUB)])
            news_ahead = [sub_rep(new_ahead, k) for k in range(SUB)]
            for i in [first + (g - first + 1 + i) % BAND for i in range(BAND - 1)]:
                factors = [lane_rep(rows[i], at + k) for k in range(SUB)]
                kept = jnp.where(inside, 0.0, rows[i])
                rows[i] = kept - tree_sum([factors[k] * news[k] for k in range(SUB)])
                ahead[i] = ahead[i] - tree_sum([factors[k] * news_ahead[k] for k in range(SUB)])
            rows[g], ahead[g] = new, new_ahead
            for piece in work[g * len(work) // count : (g + 1) * len(work) // count]:
                piece()
        inside = (lane >= first * SUB) & (lane < (first + BAND) * SUB)
        top = jnp.concatenate(
            [jnp.concatenate([x[i] for i in band], axis=0) for x in (rows, ahead)], axis=1
        )
        change = lax.dot_general(
            left, band_right(top, first // BAND), NN, preferred_element_type=F32
        )
        here, there = as_rows(change[:, :BLOCK]), as_rows(change[:, BLOCK:])
        for j, i in enumerate(others):
            rows[i] = jnp.where(inside, 0.0, rows[i]) - here[j]
            ahead[i] = ahead[i] - there[j]
        for j in range(count):
            below[j] = below[j] - here[len(others) + j]
            below_ahead[j] = below_ahead[j] - there[len(others) + j]
    return rows, below_ahead


def factor_inverse(rows, width):
    rows = list(rows)
    count = width // SUB
    for g in range(count):
        at = g * SUB
        inv, low = micro_factor([lane_rep(rows[g], at + k) for k in range(SUB)])
        own = rows[g]
        own_rep = [sub_rep(own, k) for k in range(SUB)]
        new = tree_sum([inv[k] * own_rep[k] for k in range(SUB)])
        news = [sub_rep(new, k) for k in range(SUB)]
        for i in range(g + 1, count):
            rows[i] = rows[i] - tree_sum(
                [lane_rep(rows[i], at + k) * news[k] for k in range(SUB)]
            )
        rows[g] = tree_sum([low[k] * own_rep[k] for k in range(SUB)])
    return rows


def as_rows(x):
    return [x[i * SUB : (i + 1) * SUB, :] for i in range(x.shape[0] // SUB)]


def inverse_kernel(
    own_rows,
    gathered_hbm,
    col_rank,
    diag,
    inverse_out,
    solved,
    products,
    scale_row,
    inverse,
    tangents,
    gathered,
    pivot,
    upcoming,
    left,
    right,
    scale_col,
    sems,
):
    size = inverse.shape[0]
    steps = size // BLOCK
    shards, height, width = gathered.shape
    fetch = pltpu.make_async_copy(diag.at[pl.ds(1, 3)], tangents, sems.at[0])
    receive = pltpu.make_async_copy(gathered_hbm, gathered, sems.at[2])
    receive.start()
    fetch.start()
    receive.wait()
    eye = lax.broadcasted_iota(jnp.int32, (BLOCK, BLOCK), 0) == lax.broadcasted_iota(
        jnp.int32, (BLOCK, BLOCK), 1
    )
    part = lambda c, n=BLOCK: slice(c * n, (c + 1) * n)

    def set_scale(c, block):
        own = jnp.where(eye, block, 0.0)
        scale_row[:, part(c)] = lax.rsqrt(jnp.sum(own, axis=0, keepdims=True))
        scale_col[part(c), :] = jnp.broadcast_to(
            lax.rsqrt(jnp.sum(own, axis=1, keepdims=True)), (BLOCK, BLOCK)
        )

    if width < size:
        for c in range(steps):
            set_scale(c, gathered[c, :BLOCK, :BLOCK])
        for r in range(steps):
            for o in range(width // BLOCK):
                c = (r + o) % steps
                block = gathered[r, :BLOCK, part(o)] * scale_col[part(r), :] * scale_row[:, part(c)]
                inverse[part(r), part(c)] = block
                if 0 < o and 2 * o < steps:
                    inverse[part(c), part(r)] = block.T
    else:
        for r in range(shards):
            inverse[part(r, own_rows), :] = gathered[r, :own_rows, :]
        for c in range(steps):
            set_scale(c, inverse[part(c), part(c)])
        for r in range(steps):
            for c in range(steps):
                inverse[part(r), part(c)] = (
                    inverse[part(r), part(c)] * scale_col[part(r), :] * scale_row[:, part(c)]
                )

    def eliminate(k, at, inv):
        chunk = 2 * BLOCK
        chunks = size // chunk
        twice = jnp.concatenate([inv, inv], axis=1)

        def fill_left(c):
            column = inverse[part(c, chunk), at]
            owner = 2 * c + lax.broadcasted_iota(jnp.int32, column.shape, 0) // BLOCK
            left[part(c, chunk), :] = left_terms(jnp.where(owner == k, 0.0, column))
            inverse[part(c, chunk), at] = jnp.zeros((chunk, BLOCK), F32)

        def fill_right(c):
            row = mm(inv, inverse[at, part(c, chunk)])
            owner = 2 * c + lax.broadcasted_iota(jnp.int32, row.shape, 1) // BLOCK
            row = jnp.where(owner == k, twice, row)
            right[:, part(c, chunk)] = right_terms(row)
            inverse[at, part(c, chunk)] = row

        def update(r, c):
            here = (part(r, 2 * chunk), part(c, chunk))
            inverse[here] = inverse[here] - lax.dot_general(
                left[here[0], :], right[:, here[1]], NN, preferred_element_type=F32
            )

        work = [functools.partial(fill_left, c) for c in range(chunks)]
        for c in range(chunks):
            work.append(functools.partial(fill_right, c))
            work += [functools.partial(update, r, c) for r in range(chunks // 2)]
        return work

    def invert_to_pivot(blocks, work):
        inv, following = block_inverse(*[as_rows(block) for block in blocks], work)
        pivot[...] = jnp.concatenate(inv, axis=0)
        upcoming[...] = jnp.concatenate(following, axis=0)

    one, two = part(0), part(1)
    invert_to_pivot([inverse[one, one], inverse[one, two], inverse[two, one], inverse[two, two]], [])

    def step(k, carry):
        at = pl.ds(pl.multiple_of(k * BLOCK, BLOCK), BLOCK)
        one = pl.ds(pl.multiple_of((k + 1) * BLOCK, BLOCK), BLOCK)
        two = pl.ds(pl.multiple_of(lax.min(k + 2, steps - 1) * BLOCK, BLOCK), BLOCK)
        inv = pivot[...]
        block = upcoming[...]
        row = mm(inv, jnp.concatenate([inverse[at, one], inverse[at, two]], axis=1))
        ahead = inverse[one, two] - mm(inverse[one, at], row[:, BLOCK:])
        change = mm(inverse[two, at], row)
        below = inverse[two, one] - change[:, :BLOCK]
        below_ahead = inverse[two, two] - change[:, BLOCK:]
        invert_to_pivot([block, ahead, below, below_ahead], eliminate(k, at, inv))
        return carry

    lax.fori_loop(0, steps - 1, step, 0)
    for piece in eliminate(steps - 1, slice(size - BLOCK, size), pivot[...]):
        piece()
    store = pltpu.make_async_copy(inverse, inverse_out, sems.at[1])
    store.start()

    rank_count = solved.shape[0]
    own_ranks = rank_count // shards
    values = []
    for r in range(shards):
        pieces = []
        for at in range(own_rows, height, own_ranks):
            pieces.append(gathered[r, at : at + own_ranks, :])
        values.append(jnp.concatenate(pieces, axis=1)[:, :size])
    values = keep_rows(jnp.concatenate(values, axis=0), col_rank[0])
    z = mm(values * scale_row[...], inverse[...]) * scale_row[...]
    solved[...] = z
    fetch.wait()
    for t in range(3):
        products[t] = mm(z, tangents[t], NT)
    store.wait()


def in_hbm(*arrays):
    return [pltpu.with_memory_space_constraint(x, pltpu.HBM) for x in arrays]


def run_inverse(gathered, diag, col_rank, own_ranks):
    shards = gathered.shape[0]
    _, own_rows, size = diag.shape
    rank_count = own_ranks * shards
    vmem = pl.BlockSpec(memory_space=pltpu.VMEM)
    hbm = pl.BlockSpec(memory_space=pltpu.HBM)
    gathered, diag = in_hbm(gathered, diag)
    return pl.pallas_call(
        functools.partial(inverse_kernel, own_rows),
        out_shape=(
            pltpu.HBM((size, size), F32),
            jax.ShapeDtypeStruct((rank_count, size), F32),
            jax.ShapeDtypeStruct((3, rank_count, own_rows), F32),
            jax.ShapeDtypeStruct((1, size), F32),
        ),
        in_specs=[hbm, pl.BlockSpec(memory_space=pltpu.SMEM), hbm],
        out_specs=(hbm, vmem, vmem, vmem),
        scratch_shapes=[
            pltpu.VMEM((size, size), F32),
            pltpu.VMEM((3, own_rows, size), F32),
            pltpu.VMEM(gathered.shape, F32),
            pltpu.VMEM((BLOCK, BLOCK), F32),
            pltpu.VMEM((BLOCK, BLOCK), F32),
            pltpu.VMEM((size, 4 * BLOCK), BF16),
            pltpu.VMEM((4 * BLOCK, size), BF16),
            pltpu.VMEM((size, BLOCK), F32),
            pltpu.SemaphoreType.DMA((3,)),
        ],
        compiler_params=pltpu.CompilerParams(vmem_limit_bytes=INVERSE_VMEM),
        cost_estimate=pl.CostEstimate(
            flops=40 * 10**9, bytes_accessed=10 * 2**20, transcendentals=0
        ),
        name="inverse",
    )(gathered, col_rank, diag)


def dot_split(left, right, dims=NN):
    left_hi, left_lo = left
    right_hi, right_lo = right
    rows = left_hi.shape[0]
    both = lax.dot_general(
        jnp.concatenate([left_hi, left_lo], axis=0), right_hi, dims, preferred_element_type=F32
    )
    cross = lax.dot_general(left_hi, right_lo, dims, preferred_element_type=F32)
    return both[:rows] + (both[rows:] + cross)


def keep_rows(x, rank):
    return jnp.where(lax.broadcasted_iota(jnp.int32, x.shape, 0) < rank, x, 0.0)


def put(refs, at, x):
    hi, lo = split2(x)
    refs[0][at] = hi
    refs[1][at] = lo


def put_shards(refs, slot, sources, position, p, comp, rank):
    count = len(sources)
    width = sources[0].shape[-1]
    rank_count = sources[0].shape[-2]
    for s, ref in enumerate(sources):
        owner = lax.rem(position - s + count, count)
        at = pl.ds(pl.multiple_of(owner * width, width), width)
        put(refs, (p, pl.ds(slot * rank_count, rank_count), at), keep_rows(ref[p, comp], rank))


def col_component(ref, comp, rank):
    whole = jnp.concatenate([ref[g, comp] for g in range(ref.shape[0])], axis=0)
    return keep_rows(whole, rank)


def recompress_kernel(
    tiles, shards, place, panel_rank, col_rank, tile_rank, keep_rank, *refs
):
    first_any = refs[:shards]
    second_any = refs[shards : 2 * shards]
    (
        cols_any,
        trailing_any,
        sketch_any,
        solved_any,
        inverse_any,
        scale,
        products_any,
        out_any,
        left_hi,
        left_lo,
        right_hi,
        right_lo,
        panel_hi,
        panel_lo,
        cols,
        trailing,
        first_all,
        second_all,
        inverse,
        sketch,
        solved,
        products,
        out,
        sems,
    ) = refs[2 * shards :]
    first = [first_all.at[i] for i in range(shards)]
    second = [second_all.at[i] for i in range(shards)]
    pairs = [(cols_any, cols)]
    pairs += [(trailing_any.at[p], trailing.at[p]) for p in range(tiles)]
    pairs += list(zip(first_any, first)) + list(zip(second_any, second))
    pairs += [(sketch_any, sketch), (solved_any, solved), (products_any, products)]
    pairs.append((inverse_any, inverse))
    copies = [
        pltpu.make_async_copy(source, target, sems.at[i])
        for i, (source, target) in enumerate(pairs)
    ]
    for copy in copies:
        copy.start()
    stores = []

    def store(p, begin):
        part = pl.ds(begin, 4)
        copy = pltpu.make_async_copy(
            out.at[p, 0, part], out_any.at[p, 0, part], sems.at[len(pairs) + len(stores)]
        )
        copy.start()
        stores.append(copy)

    lefts, rights, panels = (left_hi, left_lo), (right_hi, right_lo), (panel_hi, panel_lo)
    rank_count, size = sketch.shape
    up_scale = math.sqrt(size)
    down_scale = 1.0 / math.sqrt(rank_count)
    position = place[0]
    block = lambda x, i: x[:, i * rank_count : (i + 1) * rank_count]
    band = lambda x, i: x[i * rank_count : (i + 1) * rank_count]
    slot = lambda p, i, n=1: (p, slice(i * rank_count, (i + n) * rank_count), slice(None))
    take = lambda pair, at: (pair[0][at], pair[1][at])

    copies[0].wait()
    for t in range(4):
        u_col = col_component(cols, t, col_rank[0])
        for p in range(tiles):
            put(rights, slot(p, 1 if t == 0 else 4 + t), u_col)
    for p in range(tiles):
        copies[1 + p].wait()
        for t in range(4):
            rank = tile_rank[p, 0]
            put(lefts, slot(p, 0 if t == 0 else 1 + t), keep_rows(trailing[p, 0, t], rank))
            put(rights, slot(p, 0 if t == 0 else 1 + t), keep_rows(trailing[p, 0, 4 + t], rank))
    for copy in copies[1 + tiles : -1]:
        copy.wait()
    for p in range(tiles):
        put_shards(lefts, 1, first, position, p, 0, panel_rank[p])
        put_shards(panels, 0, first, position, p, 1, panel_rank[p])
        for t in range(3):
            put_shards(lefts, 5 + t, second, position, p, t, panel_rank[p])
            put_shards(panels, 1 + t, second, position, p, 3 + t, panel_rank[p])

    sides = []
    for t in range(3):
        whole = jnp.concatenate([products[r, t] for r in range(products.shape[0])], axis=1)
        sides.append(col_component(cols, 5 + t, col_rank[0]) - whole)
    sides = jnp.concatenate(sides, axis=0) * scale[...]
    copies[-1].wait()
    dz = dot_split(split2(sides), split2(inverse[...])) * scale[...]
    z_hi, z_lo = split2(solved[...])
    dz_hi, dz_lo = split2(dz)
    zz = (jnp.concatenate([z_hi, dz_hi], axis=0), jnp.concatenate([z_lo, dz_lo], axis=0))
    s = split2(sketch[...])

    state = []
    for p in range(tiles):
        live = lax.broadcasted_iota(jnp.int32, (rank_count, 1), 0) < keep_rank[p, 0]
        mixes = dot_split(take(panels, slot(p, 0, 4)), zz, NT)
        sketched = jnp.where(live, dot_split(s, take(rights, slot(p, 0, 8)), NT), 0.0)
        mix = mixes[:rank_count, :rank_count]
        base_u = -mm(block(sketched, 1), mix, NT)
        pair = jnp.concatenate([block(sketched, 0), base_u], axis=1)
        bases = take(lefts, slot(p, 0, 2))
        y = dot_split(split2(pair), bases)
        y_split = split2(y)
        gram = dot_split(y_split, y_split, NT)
        eye = lax.broadcasted_iota(jnp.int32, gram.shape, 0) == lax.broadcasted_iota(
            jnp.int32, gram.shape, 1
        )
        gram = gram + jnp.where(eye & jnp.logical_not(live), 1.0, 0.0)
        augmented = jnp.concatenate([gram, jnp.where(eye, 1.0, 0.0)], axis=1)
        cross = dot_split(bases, take(lefts, slot(p, 0, 8)), NT)
        state.append((mixes, sketched, pair, cross, augmented))

    factors = [factor_inverse(as_rows(entry[-1]), rank_count) for entry in state]

    for p in range(tiles):
        mixes, sketched, pair, cross, _ = state[p]
        rinv = jnp.concatenate(factors[p], axis=0)[:, rank_count:]
        mix = mixes[:rank_count, :rank_count]
        dmix = [band(block(mixes, 0), 1 + t) + band(block(mixes, 1 + t), 0) for t in range(3)]
        su = [block(sketched, 1)] + [block(sketched, 5 + t) for t in range(3)]
        u_mix = mm(jnp.concatenate(su[1:], axis=0), mix, NT)
        u_dmix = mm(su[0], jnp.concatenate(dmix, axis=0), NT)
        u_sides = [-(band(u_mix, t) + block(u_dmix, t)) for t in range(3)]
        sv = [block(sketched, 2 + t) for t in range(3)]
        coefs = mm(rinv, jnp.concatenate([pair] + sv + u_sides, axis=1))
        q_coef = coefs[:, : 2 * rank_count]
        q_parts = mm(q_coef, cross)
        phis = []
        for t in range(3):
            e_coef = jnp.concatenate(
                [block(coefs, 2 + t), block(coefs, 5 + t), q_coef], axis=1
            )
            q_side = jnp.concatenate(
                [block(q_parts, 0), block(q_parts, 1), block(q_parts, 2 + t), block(q_parts, 5 + t)],
                axis=1,
            )
            half = mm(e_coef, q_side, NT)
            sym = half + half.T
            i0 = lax.broadcasted_iota(jnp.int32, sym.shape, 0)
            i1 = lax.broadcasted_iota(jnp.int32, sym.shape, 1)
            phis.append(jnp.where(i0 > i1, sym, jnp.where(i0 == i1, 0.5 * sym, 0.0)))
        turned = mm(jnp.concatenate(phis, axis=0), q_coef)
        none = jnp.zeros((rank_count, rank_count), F32)
        rows = [jnp.concatenate([q_coef] + [none] * 6, axis=1)]
        for t in range(3):
            head = jnp.concatenate([block(coefs, 2 + t), block(coefs, 5 + t)], axis=1)
            tail = [none] * 6
            tail[t], tail[3 + t] = block(q_coef, 0), block(q_coef, 1)
            rows.append(jnp.concatenate([head - band(turned, t)] + tail, axis=1))
        basis_coef = jnp.concatenate(rows, axis=0)
        basis = dot_split(split2(basis_coef), take(lefts, slot(p, 0, 8))) * up_scale
        for t in range(4):
            out[p, 0, t] = band(basis, t)
        store(p, 0)
        dq_parts = mm(basis_coef[rank_count:], cross, NT)
        on_u = mm(
            block(dq_parts, 1)
            + jnp.concatenate([block(q_parts, 5 + t) for t in range(3)], axis=0),
            mix,
        )
        on_dmix = mm(block(q_parts, 1), jnp.concatenate(dmix, axis=1))
        q_mix = mm(block(q_parts, 1), mix)
        rows = [jnp.concatenate([block(q_parts, 0), -q_mix] + [none] * 6, axis=1)]
        for t in range(3):
            on_v = band(block(dq_parts, 0), t) + block(q_parts, 2 + t)
            tail = [none] * 6
            tail[t], tail[3 + t] = block(q_parts, 0), -q_mix
            rows.append(
                jnp.concatenate([on_v, -(band(on_u, t) + block(on_dmix, t))] + tail, axis=1)
            )
        coeff = dot_split(
            split2(jnp.concatenate(rows, axis=0) * down_scale), take(rights, slot(p, 0, 8))
        )
        for t in range(4):
            out[p, 0, 4 + t] = band(coeff, t)
        store(p, 4)
    for copy in stores:
        copy.wait()


def run_recompress(
    place, ranks, first, second, cols, trailing, sketch, solved, inverse, scale, products
):
    tiles = trailing.shape[0]
    rank_count, size = sketch.shape
    vmem = pl.BlockSpec(memory_space=pltpu.VMEM)
    smem = pl.BlockSpec(memory_space=pltpu.SMEM)
    hbm = pl.BlockSpec(memory_space=pltpu.HBM)
    cols, trailing, sketch, solved, inverse, products = in_hbm(
        cols, trailing, sketch, solved, inverse, products
    )
    return pl.pallas_call(
        functools.partial(recompress_kernel, tiles, len(first)),
        out_shape=jax.ShapeDtypeStruct(trailing.shape, F32),
        in_specs=[smem] * 5
        + [pl.BlockSpec(memory_space=pl.ANY)] * (2 * len(first))
        + [hbm] * 5
        + [vmem, hbm],
        out_specs=hbm,
        scratch_shapes=[pltpu.VMEM((tiles, 8 * rank_count, size), BF16)] * 4
        + [pltpu.VMEM((tiles, 4 * rank_count, size), BF16)] * 2
        + [
            pltpu.VMEM(cols.shape, F32),
            pltpu.VMEM(trailing.shape, F32),
            pltpu.VMEM((len(first),) + first[0].shape, F32),
            pltpu.VMEM((len(second),) + second[0].shape, F32),
            pltpu.VMEM(inverse.shape, F32),
            pltpu.VMEM(sketch.shape, F32),
            pltpu.VMEM(solved.shape, F32),
            pltpu.VMEM(products.shape, F32),
            pltpu.VMEM(trailing.shape, F32),
            pltpu.SemaphoreType.DMA((5 + tiles + 2 * len(first) + 2 * tiles,)),
        ],
        compiler_params=pltpu.CompilerParams(vmem_limit_bytes=RECOMPRESS_VMEM),
        cost_estimate=pl.CostEstimate(
            flops=10 * 10**9, bytes_accessed=20 * 2**20, transcendentals=0
        ),
        name="recompress",
    )(place, *ranks, *first, *second, cols, trailing, sketch, solved, inverse, scale, products)


def on_device(
    row_count,
    col_count,
    diag,
    panel_rows,
    panel_cols,
    trailing,
    sketch,
    panel_rank,
    col_rank,
    tile_rank,
    keep_rank,
):
    own_rows = diag.shape[1]
    own_ranks = panel_cols.shape[2]
    comps = panel_cols.shape[1]
    size = sketch.shape[1]
    values = panel_cols[0, 4]
    own = diag[0]
    if own_rows == BLOCK and row_count > 2:
        width = (row_count // 2 + 1) * BLOCK
        own = lax.dynamic_slice(
            jnp.concatenate([own, own[:, : width - BLOCK]], axis=1),
            (0, lax.axis_index("row") * BLOCK),
            (BLOCK, width),
        )
        values = jnp.pad(values, ((0, 0), (0, -size % width)))
        values = jnp.concatenate(
            [values[:, i : i + width] for i in range(0, values.shape[1], width)], axis=0
        )
    gathered = lax.all_gather(jnp.concatenate([own, values], axis=0), "row", axis=0)
    first = panel_rows[:, 0::4]
    second = jnp.concatenate([panel_rows[:, 1:4], panel_rows[:, 5:8]], axis=1)
    first_shards, second_shards = [first], [second]
    for source, shards in ((first, first_shards), (second, second_shards)):
        for s in range(1, col_count):
            shards.append(
                lax.ppermute(source, "col", [(i, (i + s) % col_count) for i in range(col_count)])
            )
    late_cols, gathered = lax.optimization_barrier((panel_cols[0], gathered))
    cols = lax.all_gather(late_cols, "row", axis=0)
    if own_ranks != SUB:
        cols = cols.reshape(-1, SUB // own_ranks, comps, own_ranks, size)
        cols = cols.transpose(0, 2, 1, 3, 4).reshape(-1, comps, SUB, size)
    inverse, solved, products, scale = run_inverse(
        gathered, diag, col_rank, own_ranks
    )
    all_products = lax.all_gather(products, "row", axis=0)
    place = lax.axis_index("col").astype(jnp.int32).reshape(1)
    ranks = (panel_rank, col_rank, tile_rank, keep_rank)
    return run_recompress(
        place,
        ranks,
        first_shards,
        second_shards,
        cols,
        trailing,
        sketch,
        solved,
        inverse,
        scale,
        all_products,
    )


def solution(mesh):
    in_specs = (
        P(None, "row", None),
        P("row", None, None, "col"),
        P("col", None, "row", None),
        P("row", "col", None, None, None),
        P(),
        P("row"),
        P("col"),
        P("row", "col"),
        P("row", "col"),
    )
    out_specs = P("row", "col", None, None, None)
    body = functools.partial(on_device, mesh.shape["row"], mesh.shape["col"])
    return jax.shard_map(body, mesh=mesh, in_specs=in_specs, out_specs=out_specs, check_vma=False)
```

```python
import functools
import math

import jax
import jax.numpy as jnp
from jax import lax
from jax.experimental import pallas as pl
from jax.experimental.pallas import tpu as pltpu
from jax.sharding import PartitionSpec as P

HIGHEST = lax.Precision.HIGHEST
F32 = jnp.float32
BF16 = jnp.bfloat16
BLOCK = 128
SUB = 8
BAND = 4
INVERSE_VMEM = 28 * 1024 * 1024
RECOMPRESS_VMEM = 46 * 1024 * 1024

NN = (((1,), (0,)), ((), ()))
NT = (((1,), (1,)), ((), ()))


def mm(left, right, dims=NN):
    return lax.dot_general(left, right, dims, precision=HIGHEST, preferred_element_type=F32)


def split3(x):
    hi = x.astype(BF16)
    rest = x - hi.astype(F32)
    mid = rest.astype(BF16)
    lo = (rest - mid.astype(F32)).astype(BF16)
    return hi, mid, lo


def split2(x):
    hi = x.astype(BF16)
    return hi, (x - hi.astype(F32)).astype(BF16)


def left_terms(x):
    hi, lo = split2(x)
    return jnp.concatenate([hi, hi, lo, lo], axis=1)


def right_terms(x):
    hi, lo = split2(x)
    return jnp.concatenate([hi, lo, hi, lo], axis=0)


def lane_rep(x, lane):
    return jnp.broadcast_to(x[:, lane : lane + 1], (SUB, BLOCK))


def sub_rep(x, row):
    return jnp.broadcast_to(x[row : row + 1, :], (SUB, BLOCK))


def tree_sum(terms):
    while len(terms) > 1:
        terms = [
            terms[i] + terms[i + 1] if i + 1 < len(terms) else terms[i]
            for i in range(0, len(terms), 2)
        ]
    return terms[0]


def sub_index():
    return lax.broadcasted_iota(jnp.int32, (SUB, BLOCK), 0)


def lane_index():
    return lax.broadcasted_iota(jnp.int32, (SUB, BLOCK), 1)


def spread_entries(x, at):
    cols = [lane_rep(x, at + k) for k in range(SUB)]
    return [[sub_rep(cols[k], i) for k in range(i + 1)] for i in range(SUB)]


def merge_rows(rows):
    sub = sub_index()
    step = SUB // 2
    while step:
        rows = [
            jnp.where((sub & step) == 0, rows[i], rows[i + step]) for i in range(step)
        ]
        step //= 2
    return rows[0]


def micro_inverse(entries):
    m = {(i, k): entries[i][k] for i in range(SUB) for k in range(i + 1)}
    key = lambda i, k: (i, k) if i >= k else (k, i)
    for p in range(0, SUB, 2):
        q = p + 1
        a, b, d = m[p, p], m[q, p], m[q, q]
        inv_det = 1.0 / (a * d - b * b)
        rest = [i for i in range(SUB) if i not in (p, q)]
        x0 = {i: m[key(i, p)] for i in rest}
        x1 = {i: m[key(i, q)] for i in rest}
        n0 = {i: d * x0[i] - b * x1[i] for i in rest}
        n1 = {i: a * x1[i] - b * x0[i] for i in rest}
        for i in rest:
            for k in rest:
                if k <= i:
                    m[i, k] = m[i, k] - (x0[i] * n0[k] + x1[i] * n1[k]) * inv_det
        for i in rest:
            m[key(i, p)] = n0[i] * inv_det
            m[key(i, q)] = n1[i] * inv_det
        m[p, p], m[q, p], m[q, q] = -d * inv_det, b * inv_det, -a * inv_det
    return [[m[key(i, k)] for k in range(SUB)] for i in range(SUB)]


def micro_factor(entries):
    m = [list(row) for row in entries]
    low = [[None] * SUB for _ in range(SUB)]
    scale = []
    for j in range(SUB):
        inv_piv = 1.0 / m[j][j]
        scale.append(lax.rsqrt(m[j][j]))
        for i in range(j + 1, SUB):
            factor = m[i][j] * inv_piv
            for k in range(j + 1, i + 1):
                m[i][k] = m[i][k] - factor * m[k][j]
            for k in range(j):
                change = factor * low[j][k]
                low[i][k] = -change if low[i][k] is None else low[i][k] - change
            low[i][j] = -factor if low[i][j] is None else low[i][j] - factor
    return [
        [scale[i] if k == i else scale[i] * low[i][k] for k in range(i + 1)] for i in range(SUB)
    ]


def band_left(x, band):
    lanes = BAND * SUB
    hi = x.astype(BF16).astype(F32)
    rest = x - hi
    mid = rest.astype(BF16).astype(F32)
    lo = rest - mid
    place = lax.rem(
        lax.broadcasted_iota(jnp.int32, x.shape, 1) // lanes - band + BLOCK // lanes, BLOCK // lanes
    )
    hi_next = pltpu.roll(hi, lanes, 1)
    mid_two = pltpu.roll(mid, 2 * lanes, 1)
    mid_three = pltpu.roll(mid, 3 * lanes, 1)
    one = jnp.where(
        place == 0, hi, jnp.where(place == 1, hi_next, jnp.where(place == 2, mid_two, mid_three))
    )
    two = jnp.where(place == 0, lo, jnp.where(place == 1, hi_next, 0.0))
    return jnp.concatenate([one, two], axis=1).astype(BF16)


def band_right(x, band):
    hi, mid, lo = split3(x)
    none = jnp.zeros(x.shape, BF16)
    turn = lambda parts: [parts[(i - band) % len(parts)] for i in range(len(parts))]
    return jnp.concatenate(turn([hi, mid, hi, mid]) + turn([hi, lo, none, none]), axis=0)


def block_inverse(rows, ahead, below, below_ahead, work):
    rows, ahead, below, below_ahead = list(rows), list(ahead), list(below), list(below_ahead)
    count = len(rows)
    sub, lane = sub_index(), lane_index()
    for first in range(0, count, BAND):
        band = range(first, first + BAND)
        others = [(first + BAND + i) % count for i in range(count - BAND)]
        left = band_left(
            jnp.concatenate([rows[i] for i in others] + below, axis=0), first // BAND
        )
        for g in band:
            at = g * SUB
            inside = (lane >= at) & (lane < at + SUB)
            negative = micro_inverse(spread_entries(rows[g], at))
            own = jnp.where(inside, jnp.where(lane - at == sub, -1.0, 0.0), -rows[g])
            owns = [sub_rep(own, k) for k in range(SUB)]
            owns_ahead = [sub_rep(-ahead[g], k) for k in range(SUB)]
            news = [tree_sum([row[k] * owns[k] for k in range(SUB)]) for row in negative]
            news_ahead = [
                tree_sum([row[k] * owns_ahead[k] for k in range(SUB)]) for row in negative
            ]
            for i in [first + (g - first + 1 + i) % BAND for i in range(BAND - 1)]:
                factors = [lane_rep(rows[i], at + k) for k in range(SUB)]
                kept = jnp.where(inside, 0.0, rows[i])
                rows[i] = kept - tree_sum([factors[k] * news[k] for k in range(SUB)])
                ahead[i] = ahead[i] - tree_sum([factors[k] * news_ahead[k] for k in range(SUB)])
            rows[g], ahead[g] = merge_rows(news), merge_rows(news_ahead)
            for piece in work[g * len(work) // count : (g + 1) * len(work) // count]:
                piece()
        inside = (lane >= first * SUB) & (lane < (first + BAND) * SUB)
        top = jnp.concatenate(
            [jnp.concatenate([x[i] for i in band], axis=0) for x in (rows, ahead)], axis=1
        )
        change = lax.dot_general(
            left, band_right(top, first // BAND), NN, preferred_element_type=F32
        )
        here, there = as_rows(change[:, :BLOCK]), as_rows(change[:, BLOCK:])
        for j, i in enumerate(others):
            rows[i] = jnp.where(inside, 0.0, rows[i]) - here[j]
            ahead[i] = ahead[i] - there[j]
        for j in range(count):
            below[j] = below[j] - here[len(others) + j]
            below_ahead[j] = below_ahead[j] - there[len(others) + j]
    return rows, below_ahead


def factor_inverse(rows, width):
    rows = list(rows)
    count = width // SUB
    for g in range(count):
        at = g * SUB
        low = micro_factor(spread_entries(rows[g], at))
        own = [sub_rep(rows[g], k) for k in range(SUB)]
        done = [tree_sum([low[i][k] * own[k] for k in range(i + 1)]) for i in range(SUB)]
        news = [tree_sum([low[i][k] * done[i] for i in range(k, SUB)]) for k in range(SUB)]
        for i in range(g + 1, count):
            rows[i] = rows[i] - tree_sum(
                [lane_rep(rows[i], at + k) * news[k] for k in range(SUB)]
            )
        rows[g] = merge_rows(done)
    return rows


def as_rows(x):
    return [x[i * SUB : (i + 1) * SUB, :] for i in range(x.shape[0] // SUB)]


def inverse_kernel(
    own_rows,
    gathered_hbm,
    col_rank,
    diag,
    inverse_out,
    solved,
    products,
    scale_row,
    inverse,
    tangents,
    gathered,
    pivot,
    upcoming,
    left,
    right,
    scale_col,
    sems,
):
    size = inverse.shape[0]
    steps = size // BLOCK
    shards, height, width = gathered.shape
    fetch = pltpu.make_async_copy(diag.at[pl.ds(1, 3)], tangents, sems.at[0])
    receive = pltpu.make_async_copy(gathered_hbm, gathered, sems.at[2])
    receive.start()
    fetch.start()
    receive.wait()
    eye = lax.broadcasted_iota(jnp.int32, (BLOCK, BLOCK), 0) == lax.broadcasted_iota(
        jnp.int32, (BLOCK, BLOCK), 1
    )
    part = lambda c, n=BLOCK: slice(c * n, (c + 1) * n)

    def set_scale(c, block):
        own = jnp.where(eye, block, 0.0)
        scale_row[:, part(c)] = lax.rsqrt(jnp.sum(own, axis=0, keepdims=True))
        scale_col[part(c), :] = jnp.broadcast_to(
            lax.rsqrt(jnp.sum(own, axis=1, keepdims=True)), (BLOCK, BLOCK)
        )

    if width < size:
        for c in range(steps):
            set_scale(c, gathered[c, :BLOCK, :BLOCK])
        for r in range(steps):
            for o in range(width // BLOCK):
                c = (r + o) % steps
                block = gathered[r, :BLOCK, part(o)] * scale_col[part(r), :] * scale_row[:, part(c)]
                inverse[part(r), part(c)] = block
                if 0 < o and 2 * o < steps:
                    inverse[part(c), part(r)] = block.T
    else:
        for r in range(shards):
            inverse[part(r, own_rows), :] = gathered[r, :own_rows, :]
        for c in range(steps):
            set_scale(c, inverse[part(c), part(c)])
        for r in range(steps):
            for c in range(steps):
                inverse[part(r), part(c)] = (
                    inverse[part(r), part(c)] * scale_col[part(r), :] * scale_row[:, part(c)]
                )

    def eliminate(k, at, inv):
        chunk = 2 * BLOCK
        chunks = size // chunk
        twice = jnp.concatenate([inv, inv], axis=1)

        def fill_left(c):
            column = inverse[part(c, chunk), at]
            owner = 2 * c + lax.broadcasted_iota(jnp.int32, column.shape, 0) // BLOCK
            left[part(c, chunk), :] = left_terms(jnp.where(owner == k, 0.0, column))
            inverse[part(c, chunk), at] = jnp.zeros((chunk, BLOCK), F32)

        def fill_right(c):
            row = mm(inv, inverse[at, part(c, chunk)])
            owner = 2 * c + lax.broadcasted_iota(jnp.int32, row.shape, 1) // BLOCK
            row = jnp.where(owner == k, twice, row)
            right[:, part(c, chunk)] = right_terms(row)
            inverse[at, part(c, chunk)] = row

        def update(r, c):
            here = (part(r, 2 * chunk), part(c, chunk))
            inverse[here] = inverse[here] - lax.dot_general(
                left[here[0], :], right[:, here[1]], NN, preferred_element_type=F32
            )

        work = [functools.partial(fill_left, c) for c in range(chunks)]
        for c in range(chunks):
            work.append(functools.partial(fill_right, c))
            work += [functools.partial(update, r, c) for r in range(chunks // 2)]
        return work

    def invert_to_pivot(blocks, work):
        inv, following = block_inverse(*[as_rows(block) for block in blocks], work)
        pivot[...] = jnp.concatenate(inv, axis=0)
        upcoming[...] = jnp.concatenate(following, axis=0)

    one, two = part(0), part(1)
    invert_to_pivot([inverse[one, one], inverse[one, two], inverse[two, one], inverse[two, two]], [])

    def step(k, carry):
        at = pl.ds(pl.multiple_of(k * BLOCK, BLOCK), BLOCK)
        one = pl.ds(pl.multiple_of((k + 1) * BLOCK, BLOCK), BLOCK)
        two = pl.ds(pl.multiple_of(lax.min(k + 2, steps - 1) * BLOCK, BLOCK), BLOCK)
        inv = pivot[...]
        block = upcoming[...]
        row = mm(inv, jnp.concatenate([inverse[at, one], inverse[at, two]], axis=1))
        ahead = inverse[one, two] - mm(inverse[one, at], row[:, BLOCK:])
        change = mm(inverse[two, at], row)
        below = inverse[two, one] - change[:, :BLOCK]
        below_ahead = inverse[two, two] - change[:, BLOCK:]
        invert_to_pivot([block, ahead, below, below_ahead], eliminate(k, at, inv))
        return carry

    lax.fori_loop(0, steps - 1, step, 0)
    for piece in eliminate(steps - 1, slice(size - BLOCK, size), pivot[...]):
        piece()
    store = pltpu.make_async_copy(inverse, inverse_out, sems.at[1])
    store.start()

    rank_count = solved.shape[0]
    own_ranks = rank_count // shards
    values = []
    for r in range(shards):
        pieces = []
        for at in range(own_rows, height, own_ranks):
            pieces.append(gathered[r, at : at + own_ranks, :])
        values.append(jnp.concatenate(pieces, axis=1)[:, :size])
    values = keep_rows(jnp.concatenate(values, axis=0), col_rank[0])
    z = mm(values * scale_row[...], inverse[...]) * scale_row[...]
    solved[...] = z
    fetch.wait()
    for t in range(3):
        products[t] = mm(z, tangents[t], NT)
    store.wait()


def in_hbm(*arrays):
    return [pltpu.with_memory_space_constraint(x, pltpu.HBM) for x in arrays]


def run_inverse(gathered, diag, col_rank, own_ranks):
    shards = gathered.shape[0]
    _, own_rows, size = diag.shape
    rank_count = own_ranks * shards
    vmem = pl.BlockSpec(memory_space=pltpu.VMEM)
    hbm = pl.BlockSpec(memory_space=pltpu.HBM)
    gathered, diag = in_hbm(gathered, diag)
    return pl.pallas_call(
        functools.partial(inverse_kernel, own_rows),
        out_shape=(
            pltpu.HBM((size, size), F32),
            jax.ShapeDtypeStruct((rank_count, size), F32),
            jax.ShapeDtypeStruct((3, rank_count, own_rows), F32),
            jax.ShapeDtypeStruct((1, size), F32),
        ),
        in_specs=[hbm, pl.BlockSpec(memory_space=pltpu.SMEM), hbm],
        out_specs=(hbm, vmem, vmem, vmem),
        scratch_shapes=[
            pltpu.VMEM((size, size), F32),
            pltpu.VMEM((3, own_rows, size), F32),
            pltpu.VMEM(gathered.shape, F32),
            pltpu.VMEM((BLOCK, BLOCK), F32),
            pltpu.VMEM((BLOCK, BLOCK), F32),
            pltpu.VMEM((size, 4 * BLOCK), BF16),
            pltpu.VMEM((4 * BLOCK, size), BF16),
            pltpu.VMEM((size, BLOCK), F32),
            pltpu.SemaphoreType.DMA((3,)),
        ],
        compiler_params=pltpu.CompilerParams(vmem_limit_bytes=INVERSE_VMEM),
        cost_estimate=pl.CostEstimate(
            flops=40 * 10**9, bytes_accessed=10 * 2**20, transcendentals=0
        ),
        name="inverse",
    )(gathered, col_rank, diag)


def dot_split(left, right, dims=NN):
    left_hi, left_lo = left
    right_hi, right_lo = right
    rows = left_hi.shape[0]
    both = lax.dot_general(
        jnp.concatenate([left_hi, left_lo], axis=0), right_hi, dims, preferred_element_type=F32
    )
    cross = lax.dot_general(left_hi, right_lo, dims, preferred_element_type=F32)
    return both[:rows] + (both[rows:] + cross)


def keep_rows(x, rank):
    return jnp.where(lax.broadcasted_iota(jnp.int32, x.shape, 0) < rank, x, 0.0)


def put(refs, at, x):
    hi, lo = split2(x)
    refs[0][at] = hi
    refs[1][at] = lo


def put_shards(refs, slot, sources, position, p, comp, rank):
    count = len(sources)
    width = sources[0].shape[-1]
    rank_count = sources[0].shape[-2]
    for s, ref in enumerate(sources):
        owner = lax.rem(position - s + count, count)
        at = pl.ds(pl.multiple_of(owner * width, width), width)
        put(refs, (p, pl.ds(slot * rank_count, rank_count), at), keep_rows(ref[p, comp], rank))


def col_component(ref, comp, rank):
    whole = jnp.concatenate([ref[g, comp] for g in range(ref.shape[0])], axis=0)
    return keep_rows(whole, rank)


def recompress_kernel(
    tiles, shards, place, panel_rank, col_rank, tile_rank, keep_rank, *refs
):
    first_any = refs[:shards]
    second_any = refs[shards : 2 * shards]
    (
        cols_any,
        trailing_any,
        sketch_any,
        solved_any,
        inverse_any,
        scale,
        products_any,
        out_any,
        left_hi,
        left_lo,
        right_hi,
        right_lo,
        panel_hi,
        panel_lo,
        cols,
        trailing,
        first_all,
        second_all,
        inverse,
        sketch,
        solved,
        products,
        out,
        sems,
    ) = refs[2 * shards :]
    first = [first_all.at[i] for i in range(shards)]
    second = [second_all.at[i] for i in range(shards)]
    pairs = [(cols_any, cols)]
    pairs += [(trailing_any.at[p], trailing.at[p]) for p in range(tiles)]
    pairs += list(zip(first_any, first)) + list(zip(second_any, second))
    pairs += [(sketch_any, sketch), (solved_any, solved), (products_any, products)]
    pairs.append((inverse_any, inverse))
    copies = [
        pltpu.make_async_copy(source, target, sems.at[i])
        for i, (source, target) in enumerate(pairs)
    ]
    for copy in copies:
        copy.start()
    stores = []

    def store(p, begin):
        part = pl.ds(begin, 4)
        copy = pltpu.make_async_copy(
            out.at[p, 0, part], out_any.at[p, 0, part], sems.at[len(pairs) + len(stores)]
        )
        copy.start()
        stores.append(copy)

    lefts, rights, panels = (left_hi, left_lo), (right_hi, right_lo), (panel_hi, panel_lo)
    rank_count, size = sketch.shape
    up_scale = math.sqrt(size)
    down_scale = 1.0 / math.sqrt(rank_count)
    position = place[0]
    block = lambda x, i: x[:, i * rank_count : (i + 1) * rank_count]
    band = lambda x, i: x[i * rank_count : (i + 1) * rank_count]
    slot = lambda p, i, n=1: (p, slice(i * rank_count, (i + n) * rank_count), slice(None))
    take = lambda pair, at: (pair[0][at], pair[1][at])

    copies[0].wait()
    for t in range(4):
        u_col = col_component(cols, t, col_rank[0])
        for p in range(tiles):
            put(rights, slot(p, 1 if t == 0 else 4 + t), u_col)
    for p in range(tiles):
        copies[1 + p].wait()
        for t in range(4):
            rank = tile_rank[p, 0]
            put(lefts, slot(p, 0 if t == 0 else 1 + t), keep_rows(trailing[p, 0, t], rank))
            put(rights, slot(p, 0 if t == 0 else 1 + t), keep_rows(trailing[p, 0, 4 + t], rank))
    for copy in copies[1 + tiles : -1]:
        copy.wait()
    for p in range(tiles):
        put_shards(lefts, 1, first, position, p, 0, panel_rank[p])
        put_shards(panels, 0, first, position, p, 1, panel_rank[p])
        for t in range(3):
            put_shards(lefts, 5 + t, second, position, p, t, panel_rank[p])
            put_shards(panels, 1 + t, second, position, p, 3 + t, panel_rank[p])

    sides = []
    for t in range(3):
        whole = jnp.concatenate([products[r, t] for r in range(products.shape[0])], axis=1)
        sides.append(col_component(cols, 5 + t, col_rank[0]) - whole)
    sides = jnp.concatenate(sides, axis=0) * scale[...]
    copies[-1].wait()
    dz = dot_split(split2(sides), split2(inverse[...])) * scale[...]
    z_hi, z_lo = split2(solved[...])
    dz_hi, dz_lo = split2(dz)
    zz = (jnp.concatenate([z_hi, dz_hi], axis=0), jnp.concatenate([z_lo, dz_lo], axis=0))
    s = split2(sketch[...])

    state = []
    for p in range(tiles):
        live = lax.broadcasted_iota(jnp.int32, (rank_count, 1), 0) < keep_rank[p, 0]
        mixes = dot_split(take(panels, slot(p, 0, 4)), zz, NT)
        sketched = jnp.where(live, dot_split(s, take(rights, slot(p, 0, 8)), NT), 0.0)
        mix = mixes[:rank_count, :rank_count]
        base_u = -mm(block(sketched, 1), mix, NT)
        pair = jnp.concatenate([block(sketched, 0), base_u], axis=1)
        bases = take(lefts, slot(p, 0, 2))
        y = dot_split(split2(pair), bases)
        y_split = split2(y)
        gram = dot_split(y_split, y_split, NT)
        eye = lax.broadcasted_iota(jnp.int32, gram.shape, 0) == lax.broadcasted_iota(
            jnp.int32, gram.shape, 1
        )
        gram = gram + jnp.where(eye & jnp.logical_not(live), 1.0, 0.0)
        augmented = jnp.concatenate([gram, jnp.where(eye, 1.0, 0.0)], axis=1)
        cross = dot_split(bases, take(lefts, slot(p, 0, 8)), NT)
        state.append((mixes, sketched, pair, cross, augmented))

    factors = [factor_inverse(as_rows(entry[-1]), rank_count) for entry in state]

    for p in range(tiles):
        mixes, sketched, pair, cross, _ = state[p]
        rinv = jnp.concatenate(factors[p], axis=0)[:, rank_count:]
        mix = mixes[:rank_count, :rank_count]
        dmix = [band(block(mixes, 0), 1 + t) + band(block(mixes, 1 + t), 0) for t in range(3)]
        su = [block(sketched, 1)] + [block(sketched, 5 + t) for t in range(3)]
        u_mix = mm(jnp.concatenate(su[1:], axis=0), mix, NT)
        u_dmix = mm(su[0], jnp.concatenate(dmix, axis=0), NT)
        u_sides = [-(band(u_mix, t) + block(u_dmix, t)) for t in range(3)]
        sv = [block(sketched, 2 + t) for t in range(3)]
        coefs = mm(rinv, jnp.concatenate([pair] + sv + u_sides, axis=1))
        q_coef = coefs[:, : 2 * rank_count]
        q_parts = mm(q_coef, cross)
        phis = []
        for t in range(3):
            e_coef = jnp.concatenate(
                [block(coefs, 2 + t), block(coefs, 5 + t), q_coef], axis=1
            )
            q_side = jnp.concatenate(
                [block(q_parts, 0), block(q_parts, 1), block(q_parts, 2 + t), block(q_parts, 5 + t)],
                axis=1,
            )
            half = mm(e_coef, q_side, NT)
            sym = half + half.T
            i0 = lax.broadcasted_iota(jnp.int32, sym.shape, 0)
            i1 = lax.broadcasted_iota(jnp.int32, sym.shape, 1)
            phis.append(jnp.where(i0 > i1, sym, jnp.where(i0 == i1, 0.5 * sym, 0.0)))
        turned = mm(jnp.concatenate(phis, axis=0), q_coef)
        none = jnp.zeros((rank_count, rank_count), F32)
        rows = [jnp.concatenate([q_coef] + [none] * 6, axis=1)]
        for t in range(3):
            head = jnp.concatenate([block(coefs, 2 + t), block(coefs, 5 + t)], axis=1)
            tail = [none] * 6
            tail[t], tail[3 + t] = block(q_coef, 0), block(q_coef, 1)
            rows.append(jnp.concatenate([head - band(turned, t)] + tail, axis=1))
        basis_coef = jnp.concatenate(rows, axis=0)
        basis = dot_split(split2(basis_coef), take(lefts, slot(p, 0, 8))) * up_scale
        for t in range(4):
            out[p, 0, t] = band(basis, t)
        store(p, 0)
        dq_parts = mm(basis_coef[rank_count:], cross, NT)
        on_u = mm(
            block(dq_parts, 1)
            + jnp.concatenate([block(q_parts, 5 + t) for t in range(3)], axis=0),
            mix,
        )
        on_dmix = mm(block(q_parts, 1), jnp.concatenate(dmix, axis=1))
        q_mix = mm(block(q_parts, 1), mix)
        rows = [jnp.concatenate([block(q_parts, 0), -q_mix] + [none] * 6, axis=1)]
        for t in range(3):
            on_v = band(block(dq_parts, 0), t) + block(q_parts, 2 + t)
            tail = [none] * 6
            tail[t], tail[3 + t] = block(q_parts, 0), -q_mix
            rows.append(
                jnp.concatenate([on_v, -(band(on_u, t) + block(on_dmix, t))] + tail, axis=1)
            )
        coeff = dot_split(
            split2(jnp.concatenate(rows, axis=0) * down_scale), take(rights, slot(p, 0, 8))
        )
        for t in range(4):
            out[p, 0, 4 + t] = band(coeff, t)
        store(p, 4)
    for copy in stores:
        copy.wait()


def run_recompress(
    place, ranks, first, second, cols, trailing, sketch, solved, inverse, scale, products
):
    tiles = trailing.shape[0]
    rank_count, size = sketch.shape
    vmem = pl.BlockSpec(memory_space=pltpu.VMEM)
    smem = pl.BlockSpec(memory_space=pltpu.SMEM)
    hbm = pl.BlockSpec(memory_space=pltpu.HBM)
    cols, trailing, sketch, solved, inverse, products = in_hbm(
        cols, trailing, sketch, solved, inverse, products
    )
    return pl.pallas_call(
        functools.partial(recompress_kernel, tiles, len(first)),
        out_shape=jax.ShapeDtypeStruct(trailing.shape, F32),
        in_specs=[smem] * 5
        + [pl.BlockSpec(memory_space=pl.ANY)] * (2 * len(first))
        + [hbm] * 5
        + [vmem, hbm],
        out_specs=hbm,
        scratch_shapes=[pltpu.VMEM((tiles, 8 * rank_count, size), BF16)] * 4
        + [pltpu.VMEM((tiles, 4 * rank_count, size), BF16)] * 2
        + [
            pltpu.VMEM(cols.shape, F32),
            pltpu.VMEM(trailing.shape, F32),
            pltpu.VMEM((len(first),) + first[0].shape, F32),
            pltpu.VMEM((len(second),) + second[0].shape, F32),
            pltpu.VMEM(inverse.shape, F32),
            pltpu.VMEM(sketch.shape, F32),
            pltpu.VMEM(solved.shape, F32),
            pltpu.VMEM(products.shape, F32),
            pltpu.VMEM(trailing.shape, F32),
            pltpu.SemaphoreType.DMA((5 + tiles + 2 * len(first) + 2 * tiles,)),
        ],
        compiler_params=pltpu.CompilerParams(vmem_limit_bytes=RECOMPRESS_VMEM),
        cost_estimate=pl.CostEstimate(
            flops=10 * 10**9, bytes_accessed=20 * 2**20, transcendentals=0
        ),
        name="recompress",
    )(place, *ranks, *first, *second, cols, trailing, sketch, solved, inverse, scale, products)


def on_device(
    row_count,
    col_count,
    diag,
    panel_rows,
    panel_cols,
    trailing,
    sketch,
    panel_rank,
    col_rank,
    tile_rank,
    keep_rank,
):
    own_rows = diag.shape[1]
    own_ranks = panel_cols.shape[2]
    comps = panel_cols.shape[1]
    size = sketch.shape[1]
    values = panel_cols[0, 4]
    own = diag[0]
    if own_rows == BLOCK and row_count > 2:
        width = (row_count // 2 + 1) * BLOCK
        own = lax.dynamic_slice(
            jnp.concatenate([own, own[:, : width - BLOCK]], axis=1),
            (0, lax.axis_index("row") * BLOCK),
            (BLOCK, width),
        )
        values = jnp.pad(values, ((0, 0), (0, -size % width)))
        values = jnp.concatenate(
            [values[:, i : i + width] for i in range(0, values.shape[1], width)], axis=0
        )
    gathered = lax.all_gather(jnp.concatenate([own, values], axis=0), "row", axis=0)
    first = panel_rows[:, 0::4]
    second = jnp.concatenate([panel_rows[:, 1:4], panel_rows[:, 5:8]], axis=1)
    first_shards, second_shards = [first], [second]
    for source, shards in ((first, first_shards), (second, second_shards)):
        for s in range(1, col_count):
            shards.append(
                lax.ppermute(source, "col", [(i, (i + s) % col_count) for i in range(col_count)])
            )
    late_cols, gathered = lax.optimization_barrier((panel_cols[0], gathered))
    cols = lax.all_gather(late_cols, "row", axis=0)
    if own_ranks != SUB:
        cols = cols.reshape(-1, SUB // own_ranks, comps, own_ranks, size)
        cols = cols.transpose(0, 2, 1, 3, 4).reshape(-1, comps, SUB, size)
    inverse, solved, products, scale = run_inverse(
        gathered, diag, col_rank, own_ranks
    )
    all_products = lax.all_gather(products, "row", axis=0)
    place = lax.axis_index("col").astype(jnp.int32).reshape(1)
    ranks = (panel_rank, col_rank, tile_rank, keep_rank)
    return run_recompress(
        place,
        ranks,
        first_shards,
        second_shards,
        cols,
        trailing,
        sketch,
        solved,
        inverse,
        scale,
        all_products,
    )


def solution(mesh):
    in_specs = (
        P(None, "row", None),
        P("row", None, None, "col"),
        P("col", None, "row", None),
        P("row", "col", None, None, None),
        P(),
        P("row"),
        P("col"),
        P("row", "col"),
        P("row", "col"),
    )
    out_specs = P("row", "col", None, None, None)
    body = functools.partial(on_device, mesh.shape["row"], mesh.shape["col"])
    return jax.shard_map(body, mesh=mesh, in_specs=in_specs, out_specs=out_specs, check_vma=False)
```

```python
import functools
import math

import jax
import jax.numpy as jnp
from jax import lax
from jax.experimental import pallas as pl
from jax.experimental.pallas import tpu as pltpu
from jax.sharding import PartitionSpec as P

HIGHEST = lax.Precision.HIGHEST
F32 = jnp.float32
BF16 = jnp.bfloat16
BLOCK = 128
SUB = 8
BAND = 4
INVERSE_VMEM = 28 * 1024 * 1024
RECOMPRESS_VMEM = 46 * 1024 * 1024

NN = (((1,), (0,)), ((), ()))
NT = (((1,), (1,)), ((), ()))


def mm(left, right, dims=NN):
    return lax.dot_general(left, right, dims, precision=HIGHEST, preferred_element_type=F32)


def split2(x):
    hi = x.astype(BF16)
    return hi, (x - hi.astype(F32)).astype(BF16)


def split3(x):
    hi = x.astype(BF16)
    rest = x - hi.astype(F32)
    mid = rest.astype(BF16)
    return hi, mid, (rest - mid.astype(F32)).astype(BF16)


def left_terms(x):
    hi, lo = split2(x)
    return jnp.concatenate([hi, hi, lo, lo], axis=1)


def right_terms(x):
    hi, lo = split2(x)
    return jnp.concatenate([hi, lo, hi, lo], axis=0)


def lane_rep(x, lane):
    return jnp.broadcast_to(x[:, lane : lane + 1], (SUB, BLOCK))


def sub_rep(x, row):
    return jnp.broadcast_to(x[row : row + 1, :], (SUB, BLOCK))


def tree_sum(terms):
    while len(terms) > 1:
        terms = [
            terms[i] + terms[i + 1] if i + 1 < len(terms) else terms[i]
            for i in range(0, len(terms), 2)
        ]
    return terms[0]


def sub_index():
    return lax.broadcasted_iota(jnp.int32, (SUB, BLOCK), 0)


def lane_index():
    return lax.broadcasted_iota(jnp.int32, (SUB, BLOCK), 1)


def micro_inverse(cols):
    sub = sub_index()
    cols = list(cols)
    for j in range(0, SUB, 2):
        first, second = sub == j, sub == j + 1
        pair = first | second
        a, b, d = sub_rep(cols[j], j), sub_rep(cols[j], j + 1), sub_rep(cols[j + 1], j + 1)
        inv_det = 1.0 / (a * d - b * b)
        f0 = jnp.where(first, -1.0, jnp.where(second, 0.0, cols[j]))
        f1 = jnp.where(second, -1.0, jnp.where(first, 0.0, cols[j + 1]))
        fresh = []
        for k in range(SUB):
            if k == j:
                fresh.append((f1 * b - f0 * d) * inv_det)
            elif k == j + 1:
                fresh.append((f0 * b - f1 * a) * inv_det)
            else:
                x0, x1 = sub_rep(cols[k], j), sub_rep(cols[k], j + 1)
                change = f0 * (d * x0 - b * x1) + f1 * (a * x1 - b * x0)
                fresh.append(jnp.where(pair, 0.0, cols[k]) - change * inv_det)
        cols = fresh
    return cols


def micro_factor(cols):
    sub = sub_index()
    cols = list(cols)
    low = [jnp.where(sub == k, 1.0, 0.0) for k in range(SUB)]
    pivots = jnp.zeros((SUB, BLOCK), F32)
    for j in range(SUB):
        here = sub == j
        piv = sub_rep(cols[j], j)
        inv_piv = 1.0 / piv
        factor = jnp.where(here, -1.0, cols[j])
        pivots = jnp.where(here, piv, pivots)
        below = jnp.where(sub > j, cols[j], 0.0)
        for k in range(j + 1):
            low[k] = low[k] - below * sub_rep(low[k], j) * inv_piv
        cols = [
            -factor * inv_piv
            if k == j
            else jnp.where(here, 0.0, cols[k]) - factor * (sub_rep(cols[k], j) * inv_piv)
            for k in range(SUB)
        ]
    scale = lax.rsqrt(pivots)
    return cols, [scale * c for c in low]


def band_left(x, band):
    lanes = BAND * SUB
    hi = x.astype(BF16).astype(F32)
    rest = x - hi
    mid = rest.astype(BF16).astype(F32)
    lo = rest - mid
    place = lax.rem(
        lax.broadcasted_iota(jnp.int32, x.shape, 1) // lanes - band + BLOCK // lanes, BLOCK // lanes
    )
    hi_next = pltpu.roll(hi, lanes, 1)
    mid_two = pltpu.roll(mid, 2 * lanes, 1)
    mid_three = pltpu.roll(mid, 3 * lanes, 1)
    one = jnp.where(
        place == 0, hi, jnp.where(place == 1, hi_next, jnp.where(place == 2, mid_two, mid_three))
    )
    two = jnp.where(place == 0, lo, jnp.where(place == 1, hi_next, 0.0))
    return jnp.concatenate([one, two], axis=1).astype(BF16)


def band_right(x, band):
    hi, mid, lo = split3(x)
    none = jnp.zeros(x.shape, BF16)
    turn = lambda parts: [parts[(i - band) % len(parts)] for i in range(len(parts))]
    return jnp.concatenate(turn([hi, mid, hi, mid]) + turn([hi, lo, none, none]), axis=0)


def block_inverse(rows, ahead, below, below_ahead, work):
    rows, ahead, below, below_ahead = list(rows), list(ahead), list(below), list(below_ahead)
    count = len(rows)
    sub, lane = sub_index(), lane_index()
    for first in range(0, count, BAND):
        band = range(first, first + BAND)
        others = [(first + BAND + i) % count for i in range(count - BAND)]
        left = band_left(
            jnp.concatenate([rows[i] for i in others] + below, axis=0), first // BAND
        )
        for g in band:
            at = g * SUB
            inside = (lane >= at) & (lane < at + SUB)
            inv = micro_inverse([lane_rep(rows[g], at + k) for k in range(SUB)])
            own = jnp.where(inside, jnp.where(lane - at == sub, 1.0, 0.0), rows[g])
            new = tree_sum([inv[k] * sub_rep(own, k) for k in range(SUB)])
            news = [sub_rep(new, k) for k in range(SUB)]
            new_ahead = tree_sum([inv[k] * sub_rep(ahead[g], k) for k in range(SUB)])
            news_ahead = [sub_rep(new_ahead, k) for k in range(SUB)]
            for i in [first + (g - first + 1 + i) % BAND for i in range(BAND - 1)]:
                factors = [lane_rep(rows[i], at + k) for k in range(SUB)]
                kept = jnp.where(inside, 0.0, rows[i])
                rows[i] = kept - tree_sum([factors[k] * news[k] for k in range(SUB)])
                ahead[i] = ahead[i] - tree_sum([factors[k] * news_ahead[k] for k in range(SUB)])
            rows[g], ahead[g] = new, new_ahead
            for piece in work[g * len(work) // count : (g + 1) * len(work) // count]:
                piece()
        inside = (lane >= first * SUB) & (lane < (first + BAND) * SUB)
        top = jnp.concatenate(
            [jnp.concatenate([x[i] for i in band], axis=0) for x in (rows, ahead)], axis=1
        )
        change = lax.dot_general(
            left, band_right(top, first // BAND), NN, preferred_element_type=F32
        )
        here, there = as_rows(change[:, :BLOCK]), as_rows(change[:, BLOCK:])
        for j, i in enumerate(others):
            rows[i] = jnp.where(inside, 0.0, rows[i]) - here[j]
            ahead[i] = ahead[i] - there[j]
        for j in range(count):
            below[j] = below[j] - here[len(others) + j]
            below_ahead[j] = below_ahead[j] - there[len(others) + j]
    return rows, below_ahead


def factor_inverse(rows, width):
    rows = list(rows)
    count = width // SUB
    for g in range(count):
        at = g * SUB
        inv, low = micro_factor([lane_rep(rows[g], at + k) for k in range(SUB)])
        own = rows[g]
        own_rep = [sub_rep(own, k) for k in range(SUB)]
        new = tree_sum([inv[k] * own_rep[k] for k in range(SUB)])
        news = [sub_rep(new, k) for k in range(SUB)]
        for i in range(g + 1, count):
            rows[i] = rows[i] - tree_sum(
                [lane_rep(rows[i], at + k) * news[k] for k in range(SUB)]
            )
        rows[g] = tree_sum([low[k] * own_rep[k] for k in range(SUB)])
    return rows


def as_rows(x):
    return [x[i * SUB : (i + 1) * SUB, :] for i in range(x.shape[0] // SUB)]


def inverse_kernel(
    own_rows,
    gathered_hbm,
    col_rank,
    diag,
    inverse_out,
    solved,
    products,
    scale_row,
    inverse,
    tangents,
    gathered,
    pivot,
    upcoming,
    left,
    right,
    scale_col,
    sems,
):
    size = inverse.shape[0]
    steps = size // BLOCK
    shards, height, width = gathered.shape
    fetch = pltpu.make_async_copy(diag.at[pl.ds(1, 3)], tangents, sems.at[0])
    receive = pltpu.make_async_copy(gathered_hbm, gathered, sems.at[2])
    receive.start()
    fetch.start()
    receive.wait()
    eye = lax.broadcasted_iota(jnp.int32, (BLOCK, BLOCK), 0) == lax.broadcasted_iota(
        jnp.int32, (BLOCK, BLOCK), 1
    )
    part = lambda c, n=BLOCK: slice(c * n, (c + 1) * n)

    def set_scale(c, block):
        own = jnp.where(eye, block, 0.0)
        scale_row[:, part(c)] = lax.rsqrt(jnp.sum(own, axis=0, keepdims=True))
        scale_col[part(c), :] = jnp.broadcast_to(
            lax.rsqrt(jnp.sum(own, axis=1, keepdims=True)), (BLOCK, BLOCK)
        )

    if width < size:
        for c in range(steps):
            set_scale(c, gathered[c, :BLOCK, :BLOCK])


        def place(r, o):
            c = (r + o) % steps
            block = gathered[r, :BLOCK, part(o)] * scale_col[part(r), :] * scale_row[:, part(c)]
            inverse[part(r), part(c)] = block
            if 0 < o and 2 * o < steps:
                inverse[part(c), part(r)] = block.T

        for r, o in ((0, 0), (0, 1), (1, 0)):
            place(r, o)
        beside = [
            functools.partial(place, r, o)
            for r in range(steps)
            for o in range(width // BLOCK)
            if (r, o) not in ((0, 0), (0, 1), (1, 0))
        ]
    else:
        beside = []
        for r in range(shards):
            inverse[part(r, own_rows), :] = gathered[r, :own_rows, :]
        for c in range(steps):
            set_scale(c, inverse[part(c), part(c)])
        for r in range(steps):
            for c in range(steps):
                inverse[part(r), part(c)] = (
                    inverse[part(r), part(c)] * scale_col[part(r), :] * scale_row[:, part(c)]
                )

    def eliminate(k, at, inv):
        chunk = 2 * BLOCK
        chunks = size // chunk
        twice = jnp.concatenate([inv, inv], axis=1)

        def fill_left(c):
            column = inverse[part(c, chunk), at]
            owner = 2 * c + lax.broadcasted_iota(jnp.int32, column.shape, 0) // BLOCK
            left[part(c, chunk), :] = left_terms(jnp.where(owner == k, 0.0, column))
            inverse[part(c, chunk), at] = jnp.zeros((chunk, BLOCK), F32)

        def fill_right(c):
            row = mm(inv, inverse[at, part(c, chunk)])
            owner = 2 * c + lax.broadcasted_iota(jnp.int32, row.shape, 1) // BLOCK
            row = jnp.where(owner == k, twice, row)
            right[:, part(c, chunk)] = right_terms(row)
            inverse[at, part(c, chunk)] = row

        def update(r, c):
            here = (part(r, 2 * chunk), part(c, chunk))
            inverse[here] = inverse[here] - lax.dot_general(
                left[here[0], :], right[:, here[1]], NN, preferred_element_type=F32
            )

        work = [functools.partial(fill_left, c) for c in range(chunks)]
        for c in range(chunks):
            work.append(functools.partial(fill_right, c))
            work += [functools.partial(update, r, c) for r in range(chunks // 2)]
        return work

    def invert_to_pivot(blocks, work):
        inv, following = block_inverse(*[as_rows(block) for block in blocks], work)
        pivot[...] = jnp.concatenate(inv, axis=0)
        upcoming[...] = jnp.concatenate(following, axis=0)

    one, two = part(0), part(1)
    invert_to_pivot([inverse[one, one], inverse[one, two], inverse[two, one], inverse[two, two]], beside)

    def step(k, carry):
        at = pl.ds(pl.multiple_of(k * BLOCK, BLOCK), BLOCK)
        one = pl.ds(pl.multiple_of((k + 1) * BLOCK, BLOCK), BLOCK)
        two = pl.ds(pl.multiple_of(lax.min(k + 2, steps - 1) * BLOCK, BLOCK), BLOCK)
        inv = pivot[...]
        block = upcoming[...]
        row = mm(inv, jnp.concatenate([inverse[at, one], inverse[at, two]], axis=1))
        ahead = inverse[one, two] - mm(inverse[one, at], row[:, BLOCK:])
        change = mm(inverse[two, at], row)
        below = inverse[two, one] - change[:, :BLOCK]
        below_ahead = inverse[two, two] - change[:, BLOCK:]
        invert_to_pivot([block, ahead, below, below_ahead], eliminate(k, at, inv))
        return carry

    lax.fori_loop(0, steps - 1, step, 0)
    for piece in eliminate(steps - 1, slice(size - BLOCK, size), pivot[...]):
        piece()
    store = pltpu.make_async_copy(inverse, inverse_out, sems.at[1])
    store.start()

    rank_count = solved.shape[0]
    own_ranks = rank_count // shards
    values = []
    for r in range(shards):
        pieces = []
        for at in range(own_rows, height, own_ranks):
            pieces.append(gathered[r, at : at + own_ranks, :])
        values.append(jnp.concatenate(pieces, axis=1)[:, :size])
    values = keep_rows(jnp.concatenate(values, axis=0), col_rank[0])
    z = dot_split(split2(values * scale_row[...]), split2(inverse[...])) * scale_row[...]
    solved[...] = z
    fetch.wait()
    rows = 3 * own_rows
    terms = lax.dot_general(
        jnp.concatenate(split3(tangents[...].reshape(rows, size)), axis=0),
        jnp.concatenate(split3(z), axis=0),
        NT,
        preferred_element_type=F32,
    )
    term = lambda i, k: terms[i * rows : (i + 1) * rows, k * rank_count : (k + 1) * rank_count]
    total = term(0, 0) + (
        (term(0, 1) + term(1, 0)) + (term(1, 1) + (term(0, 2) + term(2, 0)))
    )
    for t in range(3):
        products[t] = total[t * own_rows : (t + 1) * own_rows].T
    store.wait()


def in_hbm(*arrays):
    return [pltpu.with_memory_space_constraint(x, pltpu.HBM) for x in arrays]


def run_inverse(gathered, diag, col_rank, own_ranks):
    shards = gathered.shape[0]
    _, own_rows, size = diag.shape
    rank_count = own_ranks * shards
    vmem = pl.BlockSpec(memory_space=pltpu.VMEM)
    hbm = pl.BlockSpec(memory_space=pltpu.HBM)
    gathered, diag = in_hbm(gathered, diag)
    return pl.pallas_call(
        functools.partial(inverse_kernel, own_rows),
        out_shape=(
            pltpu.HBM((size, size), F32),
            jax.ShapeDtypeStruct((rank_count, size), F32),
            jax.ShapeDtypeStruct((3, rank_count, own_rows), F32),
            jax.ShapeDtypeStruct((1, size), F32),
        ),
        in_specs=[hbm, pl.BlockSpec(memory_space=pltpu.SMEM), hbm],
        out_specs=(hbm, vmem, vmem, vmem),
        scratch_shapes=[
            pltpu.VMEM((size, size), F32),
            pltpu.VMEM((3, own_rows, size), F32),
            pltpu.VMEM(gathered.shape, F32),
            pltpu.VMEM((BLOCK, BLOCK), F32),
            pltpu.VMEM((BLOCK, BLOCK), F32),
            pltpu.VMEM((size, 4 * BLOCK), BF16),
            pltpu.VMEM((4 * BLOCK, size), BF16),
            pltpu.VMEM((size, BLOCK), F32),
            pltpu.SemaphoreType.DMA((3,)),
        ],
        compiler_params=pltpu.CompilerParams(vmem_limit_bytes=INVERSE_VMEM),
        cost_estimate=pl.CostEstimate(
            flops=40 * 10**9, bytes_accessed=10 * 2**20, transcendentals=0
        ),
        name="inverse",
    )(gathered, col_rank, diag)


def dot_split(left, right, dims=NN):
    left_hi, left_lo = left
    right_hi, right_lo = right
    rows = left_hi.shape[0]
    both = lax.dot_general(
        jnp.concatenate([left_hi, left_lo], axis=0), right_hi, dims, preferred_element_type=F32
    )
    cross = lax.dot_general(left_hi, right_lo, dims, preferred_element_type=F32)
    return both[:rows] + (both[rows:] + cross)


def keep_rows(x, rank):
    return jnp.where(lax.broadcasted_iota(jnp.int32, x.shape, 0) < rank, x, 0.0)


def put(refs, at, x):
    hi, lo = split2(x)
    refs[0][at] = hi
    refs[1][at] = lo


def put_shards(refs, slot, sources, position, p, comp, rank):
    count = len(sources)
    width = sources[0].shape[-1]
    rank_count = sources[0].shape[-2]
    for s, ref in enumerate(sources):
        owner = lax.rem(position - s + count, count)
        at = pl.ds(pl.multiple_of(owner * width, width), width)
        put(refs, (p, pl.ds(slot * rank_count, rank_count), at), keep_rows(ref[p, comp], rank))


def col_component(ref, comp, rank):
    whole = jnp.concatenate([ref[g, comp] for g in range(ref.shape[0])], axis=0)
    return keep_rows(whole, rank)


def recompress_kernel(
    tiles, shards, place, panel_rank, col_rank, tile_rank, keep_rank, *refs
):
    first_any = refs[:shards]
    second_any = refs[shards : 2 * shards]
    (
        cols_any,
        trailing_any,
        sketch_any,
        solved_any,
        inverse_any,
        scale,
        products_any,
        out_any,
        left_hi,
        left_lo,
        right_hi,
        right_lo,
        panel_hi,
        panel_lo,
        cols,
        trailing,
        first_all,
        second_all,
        inverse,
        sketch,
        solved,
        products,
        out,
        sems,
    ) = refs[2 * shards :]
    first = [first_all.at[i] for i in range(shards)]
    second = [second_all.at[i] for i in range(shards)]
    pairs = [(cols_any, cols)]
    pairs += [(trailing_any.at[p], trailing.at[p]) for p in range(tiles)]
    pairs += list(zip(first_any, first)) + list(zip(second_any, second))
    pairs += [(sketch_any, sketch), (solved_any, solved), (products_any, products)]
    pairs.append((inverse_any, inverse))
    copies = [
        pltpu.make_async_copy(source, target, sems.at[i])
        for i, (source, target) in enumerate(pairs)
    ]
    for copy in copies:
        copy.start()
    stores = []

    def store(p, begin):
        part = pl.ds(begin, 4)
        copy = pltpu.make_async_copy(
            out.at[p, 0, part], out_any.at[p, 0, part], sems.at[len(pairs) + len(stores)]
        )
        copy.start()
        stores.append(copy)

    lefts, rights, panels = (left_hi, left_lo), (right_hi, right_lo), (panel_hi, panel_lo)
    rank_count, size = sketch.shape
    up_scale = math.sqrt(size)
    down_scale = 1.0 / math.sqrt(rank_count)
    position = place[0]
    block = lambda x, i: x[:, i * rank_count : (i + 1) * rank_count]
    band = lambda x, i: x[i * rank_count : (i + 1) * rank_count]
    slot = lambda p, i, n=1: (p, slice(i * rank_count, (i + n) * rank_count), slice(None))
    take = lambda pair, at: (pair[0][at], pair[1][at])

    copies[0].wait()
    for t in range(4):
        u_col = col_component(cols, t, col_rank[0])
        for p in range(tiles):
            put(rights, slot(p, 1 if t == 0 else 4 + t), u_col)
    for p in range(tiles):
        copies[1 + p].wait()
        for t in range(4):
            rank = tile_rank[p, 0]
            put(lefts, slot(p, 0 if t == 0 else 1 + t), keep_rows(trailing[p, 0, t], rank))
            put(rights, slot(p, 0 if t == 0 else 1 + t), keep_rows(trailing[p, 0, 4 + t], rank))
    for copy in copies[1 + tiles : -1]:
        copy.wait()
    for p in range(tiles):
        put_shards(lefts, 1, first, position, p, 0, panel_rank[p])
        put_shards(panels, 0, first, position, p, 1, panel_rank[p])
        for t in range(3):
            put_shards(lefts, 5 + t, second, position, p, t, panel_rank[p])
            put_shards(panels, 1 + t, second, position, p, 3 + t, panel_rank[p])

    sides = []
    for t in range(3):
        whole = jnp.concatenate([products[r, t] for r in range(products.shape[0])], axis=1)
        sides.append(col_component(cols, 5 + t, col_rank[0]) - whole)
    sides = jnp.concatenate(sides, axis=0) * scale[...]
    copies[-1].wait()
    dz = dot_split(split2(sides), split2(inverse[...])) * scale[...]
    z_hi, z_lo = split2(solved[...])
    dz_hi, dz_lo = split2(dz)
    zz = (jnp.concatenate([z_hi, dz_hi], axis=0), jnp.concatenate([z_lo, dz_lo], axis=0))
    s = split2(sketch[...])

    state = []
    for p in range(tiles):
        live = lax.broadcasted_iota(jnp.int32, (rank_count, 1), 0) < keep_rank[p, 0]
        mixes = dot_split(take(panels, slot(p, 0, 4)), zz, NT)
        sketched = jnp.where(live, dot_split(s, take(rights, slot(p, 0, 8)), NT), 0.0)
        mix = mixes[:rank_count, :rank_count]
        base_u = -mm(block(sketched, 1), mix, NT)
        pair = jnp.concatenate([block(sketched, 0), base_u], axis=1)
        bases = take(lefts, slot(p, 0, 2))
        y = dot_split(split2(pair), bases)
        y_split = split2(y)
        gram = dot_split(y_split, y_split, NT)
        eye = lax.broadcasted_iota(jnp.int32, gram.shape, 0) == lax.broadcasted_iota(
            jnp.int32, gram.shape, 1
        )
        gram = gram + jnp.where(eye & jnp.logical_not(live), 1.0, 0.0)
        augmented = jnp.concatenate([gram, jnp.where(eye, 1.0, 0.0)], axis=1)
        cross = dot_split(bases, take(lefts, slot(p, 0, 8)), NT)
        state.append((mixes, sketched, pair, cross, augmented))

    factors = [factor_inverse(as_rows(entry[-1]), rank_count) for entry in state]

    for p in range(tiles):
        mixes, sketched, pair, cross, _ = state[p]
        rinv = jnp.concatenate(factors[p], axis=0)[:, rank_count:]
        mix = mixes[:rank_count, :rank_count]
        dmix = [band(block(mixes, 0), 1 + t) + band(block(mixes, 1 + t), 0) for t in range(3)]
        su = [block(sketched, 1)] + [block(sketched, 5 + t) for t in range(3)]
        u_mix = mm(jnp.concatenate(su[1:], axis=0), mix, NT)
        u_dmix = mm(su[0], jnp.concatenate(dmix, axis=0), NT)
        u_sides = [-(band(u_mix, t) + block(u_dmix, t)) for t in range(3)]
        sv = [block(sketched, 2 + t) for t in range(3)]
        coefs = mm(rinv, jnp.concatenate([pair] + sv + u_sides, axis=1))
        q_coef = coefs[:, : 2 * rank_count]
        q_parts = mm(q_coef, cross)
        phis = []
        for t in range(3):
            e_coef = jnp.concatenate(
                [block(coefs, 2 + t), block(coefs, 5 + t), q_coef], axis=1
            )
            q_side = jnp.concatenate(
                [block(q_parts, 0), block(q_parts, 1), block(q_parts, 2 + t), block(q_parts, 5 + t)],
                axis=1,
            )
            half = mm(e_coef, q_side, NT)
            sym = half + half.T
            i0 = lax.broadcasted_iota(jnp.int32, sym.shape, 0)
            i1 = lax.broadcasted_iota(jnp.int32, sym.shape, 1)
            phis.append(jnp.where(i0 > i1, sym, jnp.where(i0 == i1, 0.5 * sym, 0.0)))
        turned = mm(jnp.concatenate(phis, axis=0), q_coef)
        none = jnp.zeros((rank_count, rank_count), F32)
        rows = [jnp.concatenate([q_coef] + [none] * 6, axis=1)]
        for t in range(3):
            head = jnp.concatenate([block(coefs, 2 + t), block(coefs, 5 + t)], axis=1)
            tail = [none] * 6
            tail[t], tail[3 + t] = block(q_coef, 0), block(q_coef, 1)
            rows.append(jnp.concatenate([head - band(turned, t)] + tail, axis=1))
        basis_coef = jnp.concatenate(rows, axis=0)
        basis = dot_split(split2(basis_coef), take(lefts, slot(p, 0, 8))) * up_scale
        for t in range(4):
            out[p, 0, t] = band(basis, t)
        store(p, 0)
        dq_parts = mm(basis_coef[rank_count:], cross, NT)
        on_u = mm(
            block(dq_parts, 1)
            + jnp.concatenate([block(q_parts, 5 + t) for t in range(3)], axis=0),
            mix,
        )
        on_dmix = mm(block(q_parts, 1), jnp.concatenate(dmix, axis=1))
        q_mix = mm(block(q_parts, 1), mix)
        rows = [jnp.concatenate([block(q_parts, 0), -q_mix] + [none] * 6, axis=1)]
        for t in range(3):
            on_v = band(block(dq_parts, 0), t) + block(q_parts, 2 + t)
            tail = [none] * 6
            tail[t], tail[3 + t] = block(q_parts, 0), -q_mix
            rows.append(
                jnp.concatenate([on_v, -(band(on_u, t) + block(on_dmix, t))] + tail, axis=1)
            )
        coeff = dot_split(
            split2(jnp.concatenate(rows, axis=0) * down_scale), take(rights, slot(p, 0, 8))
        )
        for t in range(4):
            out[p, 0, 4 + t] = band(coeff, t)
        store(p, 4)
    for copy in stores:
        copy.wait()


def run_recompress(
    place, ranks, first, second, cols, trailing, sketch, solved, inverse, scale, products
):
    tiles = trailing.shape[0]
    rank_count, size = sketch.shape
    vmem = pl.BlockSpec(memory_space=pltpu.VMEM)
    smem = pl.BlockSpec(memory_space=pltpu.SMEM)
    hbm = pl.BlockSpec(memory_space=pltpu.HBM)
    cols, trailing, sketch, solved, inverse, products = in_hbm(
        cols, trailing, sketch, solved, inverse, products
    )
    return pl.pallas_call(
        functools.partial(recompress_kernel, tiles, len(first)),
        out_shape=jax.ShapeDtypeStruct(trailing.shape, F32),
        in_specs=[smem] * 5
        + [pl.BlockSpec(memory_space=pl.ANY)] * (2 * len(first))
        + [hbm] * 5
        + [vmem, hbm],
        out_specs=hbm,
        scratch_shapes=[pltpu.VMEM((tiles, 8 * rank_count, size), BF16)] * 4
        + [pltpu.VMEM((tiles, 4 * rank_count, size), BF16)] * 2
        + [
            pltpu.VMEM(cols.shape, F32),
            pltpu.VMEM(trailing.shape, F32),
            pltpu.VMEM((len(first),) + first[0].shape, F32),
            pltpu.VMEM((len(second),) + second[0].shape, F32),
            pltpu.VMEM(inverse.shape, F32),
            pltpu.VMEM(sketch.shape, F32),
            pltpu.VMEM(solved.shape, F32),
            pltpu.VMEM(products.shape, F32),
            pltpu.VMEM(trailing.shape, F32),
            pltpu.SemaphoreType.DMA((5 + tiles + 2 * len(first) + 2 * tiles,)),
        ],
        compiler_params=pltpu.CompilerParams(vmem_limit_bytes=RECOMPRESS_VMEM),
        cost_estimate=pl.CostEstimate(
            flops=10 * 10**9, bytes_accessed=20 * 2**20, transcendentals=0
        ),
        name="recompress",
    )(place, *ranks, *first, *second, cols, trailing, sketch, solved, inverse, scale, products)


def on_device(
    row_count,
    col_count,
    diag,
    panel_rows,
    panel_cols,
    trailing,
    sketch,
    panel_rank,
    col_rank,
    tile_rank,
    keep_rank,
):
    own_rows = diag.shape[1]
    own_ranks = panel_cols.shape[2]
    comps = panel_cols.shape[1]
    size = sketch.shape[1]
    values = panel_cols[0, 4]
    own = diag[0]
    if own_rows == BLOCK and row_count > 2:
        width = (row_count // 2 + 1) * BLOCK
        own = lax.dynamic_slice(
            jnp.concatenate([own, own[:, : width - BLOCK]], axis=1),
            (0, lax.axis_index("row") * BLOCK),
            (BLOCK, width),
        )
        values = jnp.pad(values, ((0, 0), (0, -size % width)))
        values = jnp.concatenate(
            [values[:, i : i + width] for i in range(0, values.shape[1], width)], axis=0
        )
    gathered = lax.all_gather(jnp.concatenate([own, values], axis=0), "row", axis=0)
    first = panel_rows[:, 0::4]
    second = jnp.concatenate([panel_rows[:, 1:4], panel_rows[:, 5:8]], axis=1)
    first_shards, second_shards = [first], [second]
    for source, shards in ((first, first_shards), (second, second_shards)):
        for s in range(1, col_count):
            shards.append(
                lax.ppermute(source, "col", [(i, (i + s) % col_count) for i in range(col_count)])
            )
    late_cols, gathered = lax.optimization_barrier((panel_cols[0], gathered))
    cols = lax.all_gather(late_cols, "row", axis=0)
    if own_ranks != SUB:
        cols = cols.reshape(-1, SUB // own_ranks, comps, own_ranks, size)
        cols = cols.transpose(0, 2, 1, 3, 4).reshape(-1, comps, SUB, size)
    inverse, solved, products, scale = run_inverse(
        gathered, diag, col_rank, own_ranks
    )
    all_products = lax.all_gather(products, "row", axis=0)
    place = lax.axis_index("col").astype(jnp.int32).reshape(1)
    ranks = (panel_rank, col_rank, tile_rank, keep_rank)
    return run_recompress(
        place,
        ranks,
        first_shards,
        second_shards,
        cols,
        trailing,
        sketch,
        solved,
        inverse,
        scale,
        all_products,
    )


def solution(mesh):
    in_specs = (
        P(None, "row", None),
        P("row", None, None, "col"),
        P("col", None, "row", None),
        P("row", "col", None, None, None),
        P(),
        P("row"),
        P("col"),
        P("row", "col"),
        P("row", "col"),
    )
    out_specs = P("row", "col", None, None, None)
    body = functools.partial(on_device, mesh.shape["row"], mesh.shape["col"])
    return jax.shard_map(body, mesh=mesh, in_specs=in_specs, out_specs=out_specs, check_vma=False)
```

```python
import functools
import math

import jax
import jax.numpy as jnp
from jax import lax
from jax.experimental import pallas as pl
from jax.experimental.pallas import tpu as pltpu
from jax.sharding import PartitionSpec as P

HIGHEST = lax.Precision.HIGHEST
F32 = jnp.float32
BF16 = jnp.bfloat16
BLOCK = 128
SUB = 8
BAND = 4
INVERSE_VMEM = 28 * 1024 * 1024
RECOMPRESS_VMEM = 46 * 1024 * 1024

NN = (((1,), (0,)), ((), ()))
NT = (((1,), (1,)), ((), ()))


def mm(left, right, dims=NN):
    return lax.dot_general(left, right, dims, precision=HIGHEST, preferred_element_type=F32)


def split2(x):
    hi = x.astype(BF16)
    return hi, (x - hi.astype(F32)).astype(BF16)


def split3(x):
    hi = x.astype(BF16)
    rest = x - hi.astype(F32)
    mid = rest.astype(BF16)
    return hi, mid, (rest - mid.astype(F32)).astype(BF16)


def left_terms(x):
    hi, lo = split2(x)
    return jnp.concatenate([hi, hi, lo, lo], axis=1)


def right_terms(x):
    hi, lo = split2(x)
    return jnp.concatenate([hi, lo, hi, lo], axis=0)


def lane_rep(x, lane):
    return jnp.broadcast_to(x[:, lane : lane + 1], (SUB, BLOCK))


def sub_rep(x, row):
    return jnp.broadcast_to(x[row : row + 1, :], (SUB, BLOCK))


def tree_sum(terms):
    while len(terms) > 1:
        terms = [
            terms[i] + terms[i + 1] if i + 1 < len(terms) else terms[i]
            for i in range(0, len(terms), 2)
        ]
    return terms[0]


def sub_index():
    return lax.broadcasted_iota(jnp.int32, (SUB, BLOCK), 0)


def lane_index():
    return lax.broadcasted_iota(jnp.int32, (SUB, BLOCK), 1)


def micro_inverse(cols):
    sub = sub_index()
    cols = list(cols)
    for j in range(0, SUB, 2):
        first, second = sub == j, sub == j + 1
        pair = first | second
        a, b, d = sub_rep(cols[j], j), sub_rep(cols[j], j + 1), sub_rep(cols[j + 1], j + 1)
        inv_det = 1.0 / (a * d - b * b)
        f0 = jnp.where(first, -1.0, jnp.where(second, 0.0, cols[j]))
        f1 = jnp.where(second, -1.0, jnp.where(first, 0.0, cols[j + 1]))
        fresh = []
        for k in range(SUB):
            if k == j:
                fresh.append((f1 * b - f0 * d) * inv_det)
            elif k == j + 1:
                fresh.append((f0 * b - f1 * a) * inv_det)
            else:
                x0, x1 = sub_rep(cols[k], j), sub_rep(cols[k], j + 1)
                change = f0 * (d * x0 - b * x1) + f1 * (a * x1 - b * x0)
                fresh.append(jnp.where(pair, 0.0, cols[k]) - change * inv_det)
        cols = fresh
    return cols


def micro_factor(cols):
    sub = sub_index()
    cols = list(cols)
    low = [jnp.where(sub == k, 1.0, 0.0) for k in range(SUB)]
    pivots = jnp.zeros((SUB, BLOCK), F32)
    for j in range(SUB):
        here = sub == j
        piv = sub_rep(cols[j], j)
        inv_piv = 1.0 / piv
        factor = jnp.where(here, -1.0, cols[j])
        pivots = jnp.where(here, piv, pivots)
        below = jnp.where(sub > j, cols[j], 0.0)
        for k in range(j + 1):
            low[k] = low[k] - below * sub_rep(low[k], j) * inv_piv
        cols = [
            -factor * inv_piv
            if k == j
            else jnp.where(here, 0.0, cols[k]) - factor * (sub_rep(cols[k], j) * inv_piv)
            for k in range(SUB)
        ]
    scale = lax.rsqrt(pivots)
    return cols, [scale * c for c in low]


def band_left(x, band):
    lanes = BAND * SUB
    hi = x.astype(BF16).astype(F32)
    rest = x - hi
    mid = rest.astype(BF16).astype(F32)
    lo = rest - mid
    place = lax.rem(
        lax.broadcasted_iota(jnp.int32, x.shape, 1) // lanes - band + BLOCK // lanes, BLOCK // lanes
    )
    hi_next = pltpu.roll(hi, lanes, 1)
    mid_two = pltpu.roll(mid, 2 * lanes, 1)
    mid_three = pltpu.roll(mid, 3 * lanes, 1)
    one = jnp.where(
        place == 0, hi, jnp.where(place == 1, hi_next, jnp.where(place == 2, mid_two, mid_three))
    )
    two = jnp.where(place == 0, lo, jnp.where(place == 1, hi_next, 0.0))
    return jnp.concatenate([one, two], axis=1).astype(BF16)


def band_right(x, band):
    hi, mid, lo = split3(x)
    none = jnp.zeros(x.shape, BF16)
    turn = lambda parts: [parts[(i - band) % len(parts)] for i in range(len(parts))]
    return jnp.concatenate(turn([hi, mid, hi, mid]) + turn([hi, lo, none, none]), axis=0)


def block_inverse(rows, ahead, below, below_ahead, work):
    rows, ahead, below, below_ahead = list(rows), list(ahead), list(below), list(below_ahead)
    count = len(rows)
    sub, lane = sub_index(), lane_index()
    for first in range(0, count, BAND):
        band = range(first, first + BAND)
        others = [(first + BAND + i) % count for i in range(count - BAND)]
        left = band_left(
            jnp.concatenate([rows[i] for i in others] + below, axis=0), first // BAND
        )
        for g in band:
            at = g * SUB
            inside = (lane >= at) & (lane < at + SUB)
            inv = micro_inverse([lane_rep(rows[g], at + k) for k in range(SUB)])
            own = jnp.where(inside, jnp.where(lane - at == sub, 1.0, 0.0), rows[g])
            new = tree_sum([inv[k] * sub_rep(own, k) for k in range(SUB)])
            news = [sub_rep(new, k) for k in range(SUB)]
            new_ahead = tree_sum([inv[k] * sub_rep(ahead[g], k) for k in range(SUB)])
            news_ahead = [sub_rep(new_ahead, k) for k in range(SUB)]
            for i in [first + (g - first + 1 + i) % BAND for i in range(BAND - 1)]:
                factors = [lane_rep(rows[i], at + k) for k in range(SUB)]
                kept = jnp.where(inside, 0.0, rows[i])
                rows[i] = kept - tree_sum([factors[k] * news[k] for k in range(SUB)])
                ahead[i] = ahead[i] - tree_sum([factors[k] * news_ahead[k] for k in range(SUB)])
            rows[g], ahead[g] = new, new_ahead
            for piece in work[g * len(work) // count : (g + 1) * len(work) // count]:
                piece()
        inside = (lane >= first * SUB) & (lane < (first + BAND) * SUB)
        top = jnp.concatenate(
            [jnp.concatenate([x[i] for i in band], axis=0) for x in (rows, ahead)], axis=1
        )
        change = lax.dot_general(
            left, band_right(top, first // BAND), NN, preferred_element_type=F32
        )
        here, there = as_rows(change[:, :BLOCK]), as_rows(change[:, BLOCK:])
        for j, i in enumerate(others):
            rows[i] = jnp.where(inside, 0.0, rows[i]) - here[j]
            ahead[i] = ahead[i] - there[j]
        for j in range(count):
            below[j] = below[j] - here[len(others) + j]
            below_ahead[j] = below_ahead[j] - there[len(others) + j]
    return rows, below_ahead


def factor_inverse(rows, width):
    rows = list(rows)
    count = width // SUB
    for g in range(count):
        at = g * SUB
        inv, low = micro_factor([lane_rep(rows[g], at + k) for k in range(SUB)])
        own = rows[g]
        own_rep = [sub_rep(own, k) for k in range(SUB)]
        new = tree_sum([inv[k] * own_rep[k] for k in range(SUB)])
        news = [sub_rep(new, k) for k in range(SUB)]
        for i in range(g + 1, count):
            rows[i] = rows[i] - tree_sum(
                [lane_rep(rows[i], at + k) * news[k] for k in range(SUB)]
            )
        rows[g] = tree_sum([low[k] * own_rep[k] for k in range(SUB)])
    return rows


def as_rows(x):
    return [x[i * SUB : (i + 1) * SUB, :] for i in range(x.shape[0] // SUB)]


def inverse_kernel(
    own_rows,
    gathered_hbm,
    col_rank,
    diag,
    inverse_out,
    solved,
    products,
    scale_row,
    inverse,
    tangents,
    gathered,
    pivot,
    upcoming,
    left,
    right,
    scale_col,
    sems,
):
    size = inverse.shape[0]
    steps = size // BLOCK
    shards, height, width = gathered.shape
    fetch = pltpu.make_async_copy(diag.at[pl.ds(1, 3)], tangents, sems.at[0])
    receive = pltpu.make_async_copy(gathered_hbm, gathered, sems.at[2])
    receive.start()
    fetch.start()
    receive.wait()
    eye = lax.broadcasted_iota(jnp.int32, (BLOCK, BLOCK), 0) == lax.broadcasted_iota(
        jnp.int32, (BLOCK, BLOCK), 1
    )
    part = lambda c, n=BLOCK: slice(c * n, (c + 1) * n)

    def set_scale(c, block):
        own = jnp.where(eye, block, 0.0)
        scale_row[:, part(c)] = lax.rsqrt(jnp.sum(own, axis=0, keepdims=True))
        scale_col[part(c), :] = jnp.broadcast_to(
            lax.rsqrt(jnp.sum(own, axis=1, keepdims=True)), (BLOCK, BLOCK)
        )

    if width < size:
        for c in range(steps):
            set_scale(c, gathered[c, :BLOCK, :BLOCK])


        def place(r, o):
            c = (r + o) % steps
            block = gathered[r, :BLOCK, part(o)] * scale_col[part(r), :] * scale_row[:, part(c)]
            inverse[part(r), part(c)] = block
            if 0 < o and 2 * o < steps:
                inverse[part(c), part(r)] = block.T

        for r, o in ((0, 0), (0, 1), (1, 0)):
            place(r, o)
        beside = [
            functools.partial(place, r, o)
            for r in range(steps)
            for o in range(width // BLOCK)
            if (r, o) not in ((0, 0), (0, 1), (1, 0))
        ]
    else:
        beside = []
        for r in range(shards):
            inverse[part(r, own_rows), :] = gathered[r, :own_rows, :]
        for c in range(steps):
            set_scale(c, inverse[part(c), part(c)])
        for r in range(steps):
            for c in range(steps):
                inverse[part(r), part(c)] = (
                    inverse[part(r), part(c)] * scale_col[part(r), :] * scale_row[:, part(c)]
                )

    def eliminate(k, at, inv):
        chunk = 2 * BLOCK
        chunks = size // chunk
        twice = jnp.concatenate([inv, inv], axis=1)

        def fill_left(c):
            column = inverse[part(c, chunk), at]
            owner = 2 * c + lax.broadcasted_iota(jnp.int32, column.shape, 0) // BLOCK
            left[part(c, chunk), :] = left_terms(jnp.where(owner == k, 0.0, column))
            inverse[part(c, chunk), at] = jnp.zeros((chunk, BLOCK), F32)

        def fill_right(c):
            row = mm(inv, inverse[at, part(c, chunk)])
            owner = 2 * c + lax.broadcasted_iota(jnp.int32, row.shape, 1) // BLOCK
            row = jnp.where(owner == k, twice, row)
            right[:, part(c, chunk)] = right_terms(row)
            inverse[at, part(c, chunk)] = row

        def update(r, c):
            here = (part(r, 2 * chunk), part(c, chunk))
            inverse[here] = inverse[here] - lax.dot_general(
                left[here[0], :], right[:, here[1]], NN, preferred_element_type=F32
            )

        work = [functools.partial(fill_left, c) for c in range(chunks)]
        for c in range(chunks):
            work.append(functools.partial(fill_right, c))
            work += [functools.partial(update, r, c) for r in range(chunks // 2)]
        return work

    def invert_to_pivot(blocks, work):
        inv, following = block_inverse(*[as_rows(block) for block in blocks], work)
        pivot[...] = jnp.concatenate(inv, axis=0)
        upcoming[...] = jnp.concatenate(following, axis=0)

    one, two = part(0), part(1)
    invert_to_pivot([inverse[one, one], inverse[one, two], inverse[two, one], inverse[two, two]], beside)

    def step(k, carry):
        at = pl.ds(pl.multiple_of(k * BLOCK, BLOCK), BLOCK)
        one = pl.ds(pl.multiple_of((k + 1) * BLOCK, BLOCK), BLOCK)
        two = pl.ds(pl.multiple_of(lax.min(k + 2, steps - 1) * BLOCK, BLOCK), BLOCK)
        inv = pivot[...]
        block = upcoming[...]
        row = mm(inv, jnp.concatenate([inverse[at, one], inverse[at, two]], axis=1))
        ahead = inverse[one, two] - mm(inverse[one, at], row[:, BLOCK:])
        change = mm(inverse[two, at], row)
        below = inverse[two, one] - change[:, :BLOCK]
        below_ahead = inverse[two, two] - change[:, BLOCK:]
        invert_to_pivot([block, ahead, below, below_ahead], eliminate(k, at, inv))
        return carry

    lax.fori_loop(0, steps - 1, step, 0)
    for piece in eliminate(steps - 1, slice(size - BLOCK, size), pivot[...]):
        piece()
    store = pltpu.make_async_copy(inverse, inverse_out, sems.at[1])
    store.start()

    rank_count = solved.shape[0]
    own_ranks = rank_count // shards
    values = []
    for r in range(shards):
        pieces = []
        for at in range(own_rows, height, own_ranks):
            pieces.append(gathered[r, at : at + own_ranks, :])
        values.append(jnp.concatenate(pieces, axis=1)[:, :size])
    values = keep_rows(jnp.concatenate(values, axis=0), col_rank[0])
    z = dot_split(split2(values * scale_row[...]), split2(inverse[...])) * scale_row[...]
    solved[...] = z
    fetch.wait()
    rows = 3 * own_rows
    terms = lax.dot_general(
        jnp.concatenate(split3(tangents[...].reshape(rows, size)), axis=0),
        jnp.concatenate(split3(z), axis=0),
        NT,
        preferred_element_type=F32,
    )
    term = lambda i, k: terms[i * rows : (i + 1) * rows, k * rank_count : (k + 1) * rank_count]
    total = term(0, 0) + (
        (term(0, 1) + term(1, 0)) + (term(1, 1) + (term(0, 2) + term(2, 0)))
    )
    for t in range(3):
        products[t] = total[t * own_rows : (t + 1) * own_rows].T
    store.wait()


def in_hbm(*arrays):
    return [pltpu.with_memory_space_constraint(x, pltpu.HBM) for x in arrays]


def run_inverse(gathered, diag, col_rank, own_ranks):
    shards = gathered.shape[0]
    _, own_rows, size = diag.shape
    rank_count = own_ranks * shards
    vmem = pl.BlockSpec(memory_space=pltpu.VMEM)
    hbm = pl.BlockSpec(memory_space=pltpu.HBM)
    gathered, diag = in_hbm(gathered, diag)
    return pl.pallas_call(
        functools.partial(inverse_kernel, own_rows),
        out_shape=(
            pltpu.HBM((size, size), F32),
            jax.ShapeDtypeStruct((rank_count, size), F32),
            jax.ShapeDtypeStruct((3, rank_count, own_rows), F32),
            jax.ShapeDtypeStruct((1, size), F32),
        ),
        in_specs=[hbm, pl.BlockSpec(memory_space=pltpu.SMEM), hbm],
        out_specs=(hbm, vmem, vmem, vmem),
        scratch_shapes=[
            pltpu.VMEM((size, size), F32),
            pltpu.VMEM((3, own_rows, size), F32),
            pltpu.VMEM(gathered.shape, F32),
            pltpu.VMEM((BLOCK, BLOCK), F32),
            pltpu.VMEM((BLOCK, BLOCK), F32),
            pltpu.VMEM((size, 4 * BLOCK), BF16),
            pltpu.VMEM((4 * BLOCK, size), BF16),
            pltpu.VMEM((size, BLOCK), F32),
            pltpu.SemaphoreType.DMA((3,)),
        ],
        compiler_params=pltpu.CompilerParams(vmem_limit_bytes=INVERSE_VMEM),
        cost_estimate=pl.CostEstimate(
            flops=40 * 10**9, bytes_accessed=10 * 2**20, transcendentals=0
        ),
        name="inverse",
    )(gathered, col_rank, diag)


def dot_split(left, right, dims=NN):
    left_hi, left_lo = left
    right_hi, right_lo = right
    rows = left_hi.shape[0]
    both = lax.dot_general(
        jnp.concatenate([left_hi, left_lo], axis=0), right_hi, dims, preferred_element_type=F32
    )
    cross = lax.dot_general(left_hi, right_lo, dims, preferred_element_type=F32)
    return both[:rows] + (both[rows:] + cross)


def keep_rows(x, rank):
    return jnp.where(lax.broadcasted_iota(jnp.int32, x.shape, 0) < rank, x, 0.0)


def put(refs, at, x):
    hi, lo = split2(x)
    refs[0][at] = hi
    refs[1][at] = lo


def shard_values(refs, position, count, p, comp):
    value = lambda i: refs[i][p, comp]
    if len(refs) == count:
        return [value(i) for i in range(count)]
    pick = lambda here, i, k: jnp.where(here, value(i), value(k))
    return [
        value(0),
        pick(position == 0, 3, 1),
        pick(position < 2, 4, 5),
        pick(position == 3, 3, 2),
    ]


def put_shards(refs, slot, sources, position, count, p, comp, rank):
    values = shard_values(sources, position, count, p, comp)
    rank_count, width = values[0].shape
    for s, value in enumerate(values):
        owner = lax.rem(position - s + count, count)
        at = pl.ds(pl.multiple_of(owner * width, width), width)
        put(refs, (p, pl.ds(slot * rank_count, rank_count), at), keep_rows(value, rank))


def col_component(ref, comp, rank):
    whole = jnp.concatenate([ref[g, comp] for g in range(ref.shape[0])], axis=0)
    return keep_rows(whole, rank)


def recompress_kernel(
    tiles, shards, count, place, panel_rank, col_rank, tile_rank, keep_rank, *refs
):
    rows_any = refs[:shards]
    (
        cols_any,
        trailing_any,
        sketch_any,
        solved_any,
        inverse_any,
        scale,
        products_any,
        out_any,
        left_hi,
        left_lo,
        right_hi,
        right_lo,
        panel_hi,
        panel_lo,
        cols,
        trailing,
        rows_all,
        inverse,
        sketch,
        solved,
        products,
        out,
        sems,
    ) = refs[shards:]
    rows_in = [rows_all.at[i] for i in range(shards)]
    pairs = [(cols_any, cols)]
    pairs += [(trailing_any.at[p], trailing.at[p]) for p in range(tiles)]
    pairs += list(zip(rows_any, rows_in))
    pairs += [(sketch_any, sketch), (solved_any, solved), (products_any, products)]
    pairs.append((inverse_any, inverse))
    copies = [
        pltpu.make_async_copy(source, target, sems.at[i])
        for i, (source, target) in enumerate(pairs)
    ]
    for copy in copies:
        copy.start()
    stores = []

    def store(p, begin):
        part = pl.ds(begin, 4)
        copy = pltpu.make_async_copy(
            out.at[p, 0, part], out_any.at[p, 0, part], sems.at[len(pairs) + len(stores)]
        )
        copy.start()
        stores.append(copy)

    lefts, rights, panels = (left_hi, left_lo), (right_hi, right_lo), (panel_hi, panel_lo)
    rank_count, size = sketch.shape
    up_scale = math.sqrt(size)
    down_scale = 1.0 / math.sqrt(rank_count)
    position = place[0]
    block = lambda x, i: x[:, i * rank_count : (i + 1) * rank_count]
    band = lambda x, i: x[i * rank_count : (i + 1) * rank_count]
    slot = lambda p, i, n=1: (p, slice(i * rank_count, (i + n) * rank_count), slice(None))
    take = lambda pair, at: (pair[0][at], pair[1][at])

    copies[0].wait()
    for t in range(4):
        u_col = col_component(cols, t, col_rank[0])
        for p in range(tiles):
            put(rights, slot(p, 1 if t == 0 else 4 + t), u_col)
    for p in range(tiles):
        copies[1 + p].wait()
        for t in range(4):
            rank = tile_rank[p, 0]
            put(lefts, slot(p, 0 if t == 0 else 1 + t), keep_rows(trailing[p, 0, t], rank))
            put(rights, slot(p, 0 if t == 0 else 1 + t), keep_rows(trailing[p, 0, 4 + t], rank))
    for copy in copies[1 + tiles : -1]:
        copy.wait()
    for p in range(tiles):
        for t in range(4):
            rank = panel_rank[p]
            put_shards(lefts, 1 if t == 0 else 4 + t, rows_in, position, count, p, t, rank)
            put_shards(panels, t, rows_in, position, count, p, 4 + t, rank)

    sides = []
    for t in range(3):
        whole = jnp.concatenate([products[r, t] for r in range(products.shape[0])], axis=1)
        sides.append(col_component(cols, 5 + t, col_rank[0]) - whole)
    sides = jnp.concatenate(sides, axis=0) * scale[...]
    copies[-1].wait()
    dz = dot_split(split2(sides), split2(inverse[...])) * scale[...]
    z_hi, z_lo = split2(solved[...])
    dz_hi, dz_lo = split2(dz)
    zz = (jnp.concatenate([z_hi, dz_hi], axis=0), jnp.concatenate([z_lo, dz_lo], axis=0))
    s = split2(sketch[...])

    state = []
    for p in range(tiles):
        live = lax.broadcasted_iota(jnp.int32, (rank_count, 1), 0) < keep_rank[p, 0]
        mixes = dot_split(take(panels, slot(p, 0, 4)), zz, NT)
        sketched = jnp.where(live, dot_split(s, take(rights, slot(p, 0, 8)), NT), 0.0)
        mix = mixes[:rank_count, :rank_count]
        base_u = -mm(block(sketched, 1), mix, NT)
        pair = jnp.concatenate([block(sketched, 0), base_u], axis=1)
        bases = take(lefts, slot(p, 0, 2))
        y = dot_split(split2(pair), bases)
        y_split = split2(y)
        gram = dot_split(y_split, y_split, NT)
        eye = lax.broadcasted_iota(jnp.int32, gram.shape, 0) == lax.broadcasted_iota(
            jnp.int32, gram.shape, 1
        )
        gram = gram + jnp.where(eye & jnp.logical_not(live), 1.0, 0.0)
        augmented = jnp.concatenate([gram, jnp.where(eye, 1.0, 0.0)], axis=1)
        cross = dot_split(bases, take(lefts, slot(p, 0, 8)), NT)
        state.append((mixes, sketched, pair, cross, augmented))

    factors = [factor_inverse(as_rows(entry[-1]), rank_count) for entry in state]

    for p in range(tiles):
        mixes, sketched, pair, cross, _ = state[p]
        rinv = jnp.concatenate(factors[p], axis=0)[:, rank_count:]
        mix = mixes[:rank_count, :rank_count]
        dmix = [band(block(mixes, 0), 1 + t) + band(block(mixes, 1 + t), 0) for t in range(3)]
        su = [block(sketched, 1)] + [block(sketched, 5 + t) for t in range(3)]
        u_mix = mm(jnp.concatenate(su[1:], axis=0), mix, NT)
        u_dmix = mm(su[0], jnp.concatenate(dmix, axis=0), NT)
        u_sides = [-(band(u_mix, t) + block(u_dmix, t)) for t in range(3)]
        sv = [block(sketched, 2 + t) for t in range(3)]
        coefs = mm(rinv, jnp.concatenate([pair] + sv + u_sides, axis=1))
        q_coef = coefs[:, : 2 * rank_count]
        q_parts = mm(q_coef, cross)
        phis = []
        for t in range(3):
            e_coef = jnp.concatenate(
                [block(coefs, 2 + t), block(coefs, 5 + t), q_coef], axis=1
            )
            q_side = jnp.concatenate(
                [block(q_parts, 0), block(q_parts, 1), block(q_parts, 2 + t), block(q_parts, 5 + t)],
                axis=1,
            )
            half = mm(e_coef, q_side, NT)
            sym = half + half.T
            i0 = lax.broadcasted_iota(jnp.int32, sym.shape, 0)
            i1 = lax.broadcasted_iota(jnp.int32, sym.shape, 1)
            phis.append(jnp.where(i0 > i1, sym, jnp.where(i0 == i1, 0.5 * sym, 0.0)))
        turned = mm(jnp.concatenate(phis, axis=0), q_coef)
        none = jnp.zeros((rank_count, rank_count), F32)
        rows = [jnp.concatenate([q_coef] + [none] * 6, axis=1)]
        for t in range(3):
            head = jnp.concatenate([block(coefs, 2 + t), block(coefs, 5 + t)], axis=1)
            tail = [none] * 6
            tail[t], tail[3 + t] = block(q_coef, 0), block(q_coef, 1)
            rows.append(jnp.concatenate([head - band(turned, t)] + tail, axis=1))
        basis_coef = jnp.concatenate(rows, axis=0)
        basis = dot_split(split2(basis_coef), take(lefts, slot(p, 0, 8))) * up_scale
        for t in range(4):
            out[p, 0, t] = band(basis, t)
        store(p, 0)
        dq_parts = mm(basis_coef[rank_count:], cross, NT)
        on_u = mm(
            block(dq_parts, 1)
            + jnp.concatenate([block(q_parts, 5 + t) for t in range(3)], axis=0),
            mix,
        )
        on_dmix = mm(block(q_parts, 1), jnp.concatenate(dmix, axis=1))
        q_mix = mm(block(q_parts, 1), mix)
        rows = [jnp.concatenate([block(q_parts, 0), -q_mix] + [none] * 6, axis=1)]
        for t in range(3):
            on_v = band(block(dq_parts, 0), t) + block(q_parts, 2 + t)
            tail = [none] * 6
            tail[t], tail[3 + t] = block(q_parts, 0), -q_mix
            rows.append(
                jnp.concatenate([on_v, -(band(on_u, t) + block(on_dmix, t))] + tail, axis=1)
            )
        coeff = dot_split(
            split2(jnp.concatenate(rows, axis=0) * down_scale), take(rights, slot(p, 0, 8))
        )
        for t in range(4):
            out[p, 0, 4 + t] = band(coeff, t)
        store(p, 4)
    for copy in stores:
        copy.wait()


def run_recompress(
    place, ranks, count, shards, cols, trailing, sketch, solved, inverse, scale, products
):
    tiles = trailing.shape[0]
    rank_count, size = sketch.shape
    vmem = pl.BlockSpec(memory_space=pltpu.VMEM)
    smem = pl.BlockSpec(memory_space=pltpu.SMEM)
    hbm = pl.BlockSpec(memory_space=pltpu.HBM)
    cols, trailing, sketch, solved, inverse, products = in_hbm(
        cols, trailing, sketch, solved, inverse, products
    )
    return pl.pallas_call(
        functools.partial(recompress_kernel, tiles, len(shards), count),
        out_shape=jax.ShapeDtypeStruct(trailing.shape, F32),
        in_specs=[smem] * 5
        + [pl.BlockSpec(memory_space=pl.ANY)] * len(shards)
        + [hbm] * 5
        + [vmem, hbm],
        out_specs=hbm,
        scratch_shapes=[pltpu.VMEM((tiles, 8 * rank_count, size), BF16)] * 4
        + [pltpu.VMEM((tiles, 4 * rank_count, size), BF16)] * 2
        + [
            pltpu.VMEM(cols.shape, F32),
            pltpu.VMEM(trailing.shape, F32),
            pltpu.VMEM((len(shards),) + shards[0].shape, F32),
            pltpu.VMEM(inverse.shape, F32),
            pltpu.VMEM(sketch.shape, F32),
            pltpu.VMEM(solved.shape, F32),
            pltpu.VMEM(products.shape, F32),
            pltpu.VMEM(trailing.shape, F32),
            pltpu.SemaphoreType.DMA((5 + tiles + len(shards) + 2 * tiles,)),
        ],
        compiler_params=pltpu.CompilerParams(vmem_limit_bytes=RECOMPRESS_VMEM),
        cost_estimate=pl.CostEstimate(
            flops=10 * 10**9, bytes_accessed=20 * 2**20, transcendentals=0
        ),
        name="recompress",
    )(place, *ranks, *shards, cols, trailing, sketch, solved, inverse, scale, products)


def on_device(
    row_count,
    col_count,
    diag,
    panel_rows,
    panel_cols,
    trailing,
    sketch,
    panel_rank,
    col_rank,
    tile_rank,
    keep_rank,
):
    own_rows = diag.shape[1]
    own_ranks = panel_cols.shape[2]
    comps = panel_cols.shape[1]
    size = sketch.shape[1]
    values = panel_cols[0, 4]
    own = diag[0]
    if own_rows == BLOCK and row_count > 2:
        width = (row_count // 2 + 1) * BLOCK
        own = lax.dynamic_slice(
            jnp.concatenate([own, own[:, : width - BLOCK]], axis=1),
            (0, lax.axis_index("row") * BLOCK),
            (BLOCK, width),
        )
        values = jnp.pad(values, ((0, 0), (0, -size % width)))
        values = jnp.concatenate(
            [values[:, i : i + width] for i in range(0, values.shape[1], width)], axis=0
        )
    gathered = lax.all_gather(jnp.concatenate([own, values], axis=0), "row", axis=0)
    if col_count == 4:
        send = lambda x, pairs: lax.ppermute(x, "col", pairs)
        from_left = send(panel_rows, [(0, 1), (1, 2), (2, 3)])
        from_right = send(panel_rows, [(1, 0), (2, 1), (3, 2)])
        late_cols, late_rows, from_left, from_right, gathered = lax.optimization_barrier(
            (panel_cols[0], panel_rows, from_left, from_right, gathered)
        )
        shards = [
            panel_rows,
            from_left,
            from_right,
            send(late_rows, [(0, 3), (3, 0)]),
            send(from_right, [(1, 0), (2, 1)]),
            send(from_left, [(1, 2), (2, 3)]),
        ]
    else:
        shards = [panel_rows] + [
            lax.ppermute(panel_rows, "col", [(i, (i + s) % col_count) for i in range(col_count)])
            for s in range(1, col_count)
        ]
        late_cols, gathered = lax.optimization_barrier((panel_cols[0], gathered))
    cols = lax.all_gather(late_cols, "row", axis=0)
    if own_ranks != SUB:
        cols = cols.reshape(-1, SUB // own_ranks, comps, own_ranks, size)
        cols = cols.transpose(0, 2, 1, 3, 4).reshape(-1, comps, SUB, size)
    inverse, solved, products, scale = run_inverse(
        gathered, diag, col_rank, own_ranks
    )
    all_products = lax.all_gather(products, "row", axis=0)
    place = lax.axis_index("col").astype(jnp.int32).reshape(1)
    ranks = (panel_rank, col_rank, tile_rank, keep_rank)
    return run_recompress(
        place,
        ranks,
        col_count,
        shards,
        cols,
        trailing,
        sketch,
        solved,
        inverse,
        scale,
        all_products,
    )


def solution(mesh):
    in_specs = (
        P(None, "row", None),
        P("row", None, None, "col"),
        P("col", None, "row", None),
        P("row", "col", None, None, None),
        P(),
        P("row"),
        P("col"),
        P("row", "col"),
        P("row", "col"),
    )
    out_specs = P("row", "col", None, None, None)
    body = functools.partial(on_device, mesh.shape["row"], mesh.shape["col"])
    return jax.shard_map(body, mesh=mesh, in_specs=in_specs, out_specs=out_specs, check_vma=False)
```

```python
import functools
import math

import jax
import jax.numpy as jnp
from jax import lax
from jax.experimental import pallas as pl
from jax.experimental.pallas import tpu as pltpu
from jax.sharding import PartitionSpec as P

HIGHEST = lax.Precision.HIGHEST
F32 = jnp.float32
BF16 = jnp.bfloat16
BLOCK = 128
SUB = 8
BAND = 4
INVERSE_VMEM = 28 * 1024 * 1024
RECOMPRESS_VMEM = 46 * 1024 * 1024

NN = (((1,), (0,)), ((), ()))
NT = (((1,), (1,)), ((), ()))


def mm(left, right, dims=NN):
    return lax.dot_general(left, right, dims, precision=HIGHEST, preferred_element_type=F32)


def split2(x):
    hi = x.astype(BF16)
    return hi, (x - hi.astype(F32)).astype(BF16)


def split3(x):
    hi = x.astype(BF16)
    rest = x - hi.astype(F32)
    mid = rest.astype(BF16)
    return hi, mid, (rest - mid.astype(F32)).astype(BF16)


def left_terms(x):
    hi, lo = split2(x)
    return jnp.concatenate([hi, hi, lo, lo], axis=1)


def right_terms(x):
    hi, lo = split2(x)
    return jnp.concatenate([hi, lo, hi, lo], axis=0)


def lane_rep(x, lane):
    return jnp.broadcast_to(x[:, lane : lane + 1], (SUB, BLOCK))


def sub_rep(x, row):
    return jnp.broadcast_to(x[row : row + 1, :], (SUB, BLOCK))


def tree_sum(terms):
    while len(terms) > 1:
        terms = [
            terms[i] + terms[i + 1] if i + 1 < len(terms) else terms[i]
            for i in range(0, len(terms), 2)
        ]
    return terms[0]


def sub_index():
    return lax.broadcasted_iota(jnp.int32, (SUB, BLOCK), 0)


def lane_index():
    return lax.broadcasted_iota(jnp.int32, (SUB, BLOCK), 1)


def micro_inverse(cols):
    sub = sub_index()
    cols = list(cols)
    for j in range(0, SUB, 2):
        first, second = sub == j, sub == j + 1
        pair = first | second
        a, b, d = sub_rep(cols[j], j), sub_rep(cols[j], j + 1), sub_rep(cols[j + 1], j + 1)
        inv_det = 1.0 / (a * d - b * b)
        f0 = jnp.where(first, -1.0, jnp.where(second, 0.0, cols[j]))
        f1 = jnp.where(second, -1.0, jnp.where(first, 0.0, cols[j + 1]))
        fresh = []
        for k in range(SUB):
            if k == j:
                fresh.append((f1 * b - f0 * d) * inv_det)
            elif k == j + 1:
                fresh.append((f0 * b - f1 * a) * inv_det)
            else:
                x0, x1 = sub_rep(cols[k], j), sub_rep(cols[k], j + 1)
                change = f0 * (d * x0 - b * x1) + f1 * (a * x1 - b * x0)
                fresh.append(jnp.where(pair, 0.0, cols[k]) - change * inv_det)
        cols = fresh
    return cols


def micro_factor(cols):
    sub = sub_index()
    cols = list(cols)
    low = [jnp.where(sub == k, 1.0, 0.0) for k in range(SUB)]
    pivots = jnp.zeros((SUB, BLOCK), F32)
    for j in range(SUB):
        here = sub == j
        piv = sub_rep(cols[j], j)
        inv_piv = 1.0 / piv
        factor = jnp.where(here, -1.0, cols[j])
        pivots = jnp.where(here, piv, pivots)
        below = jnp.where(sub > j, cols[j], 0.0)
        for k in range(j + 1):
            low[k] = low[k] - below * sub_rep(low[k], j) * inv_piv
        cols = [
            -factor * inv_piv
            if k == j
            else jnp.where(here, 0.0, cols[k]) - factor * (sub_rep(cols[k], j) * inv_piv)
            for k in range(SUB)
        ]
    scale = lax.rsqrt(pivots)
    return cols, [scale * c for c in low]


def band_left(x, band):
    lanes = BAND * SUB
    hi = x.astype(BF16).astype(F32)
    rest = x - hi
    mid = rest.astype(BF16).astype(F32)
    lo = rest - mid
    place = lax.rem(
        lax.broadcasted_iota(jnp.int32, x.shape, 1) // lanes - band + BLOCK // lanes, BLOCK // lanes
    )
    hi_next = pltpu.roll(hi, lanes, 1)
    mid_two = pltpu.roll(mid, 2 * lanes, 1)
    mid_three = pltpu.roll(mid, 3 * lanes, 1)
    one = jnp.where(
        place == 0, hi, jnp.where(place == 1, hi_next, jnp.where(place == 2, mid_two, mid_three))
    )
    two = jnp.where(place == 0, lo, jnp.where(place == 1, hi_next, 0.0))
    return jnp.concatenate([one, two], axis=1).astype(BF16)


def band_right(x, band):
    hi, mid, lo = split3(x)
    none = jnp.zeros(x.shape, BF16)
    turn = lambda parts: [parts[(i - band) % len(parts)] for i in range(len(parts))]
    return jnp.concatenate(turn([hi, mid, hi, mid]) + turn([hi, lo, none, none]), axis=0)


def block_inverse(rows, ahead, below, below_ahead, work):
    rows, ahead, below, below_ahead = list(rows), list(ahead), list(below), list(below_ahead)
    count = len(rows)
    sub, lane = sub_index(), lane_index()
    for first in range(0, count, BAND):
        band = range(first, first + BAND)
        others = [(first + BAND + i) % count for i in range(count - BAND)]
        left = band_left(
            jnp.concatenate([rows[i] for i in others] + below, axis=0), first // BAND
        )
        for g in band:
            at = g * SUB
            inside = (lane >= at) & (lane < at + SUB)
            inv = micro_inverse([lane_rep(rows[g], at + k) for k in range(SUB)])
            own = jnp.where(inside, jnp.where(lane - at == sub, 1.0, 0.0), rows[g])
            new = tree_sum([inv[k] * sub_rep(own, k) for k in range(SUB)])
            news = [sub_rep(new, k) for k in range(SUB)]
            new_ahead = tree_sum([inv[k] * sub_rep(ahead[g], k) for k in range(SUB)])
            news_ahead = [sub_rep(new_ahead, k) for k in range(SUB)]
            for i in [first + (g - first + 1 + i) % BAND for i in range(BAND - 1)]:
                factors = [lane_rep(rows[i], at + k) for k in range(SUB)]
                kept = jnp.where(inside, 0.0, rows[i])
                rows[i] = kept - tree_sum([factors[k] * news[k] for k in range(SUB)])
                ahead[i] = ahead[i] - tree_sum([factors[k] * news_ahead[k] for k in range(SUB)])
            rows[g], ahead[g] = new, new_ahead
            for piece in work[g * len(work) // count : (g + 1) * len(work) // count]:
                piece()
        inside = (lane >= first * SUB) & (lane < (first + BAND) * SUB)
        top = jnp.concatenate(
            [jnp.concatenate([x[i] for i in band], axis=0) for x in (rows, ahead)], axis=1
        )
        change = lax.dot_general(
            left, band_right(top, first // BAND), NN, preferred_element_type=F32
        )
        here, there = as_rows(change[:, :BLOCK]), as_rows(change[:, BLOCK:])
        for j, i in enumerate(others):
            rows[i] = jnp.where(inside, 0.0, rows[i]) - here[j]
            ahead[i] = ahead[i] - there[j]
        for j in range(count):
            below[j] = below[j] - here[len(others) + j]
            below_ahead[j] = below_ahead[j] - there[len(others) + j]
    return rows, below_ahead


def factor_inverse(rows, width):
    rows = list(rows)
    count = width // SUB
    for g in range(count):
        at = g * SUB
        inv, low = micro_factor([lane_rep(rows[g], at + k) for k in range(SUB)])
        own = rows[g]
        own_rep = [sub_rep(own, k) for k in range(SUB)]
        new = tree_sum([inv[k] * own_rep[k] for k in range(SUB)])
        news = [sub_rep(new, k) for k in range(SUB)]
        for i in range(g + 1, count):
            rows[i] = rows[i] - tree_sum(
                [lane_rep(rows[i], at + k) * news[k] for k in range(SUB)]
            )
        rows[g] = tree_sum([low[k] * own_rep[k] for k in range(SUB)])
    return rows


def as_rows(x):
    return [x[i * SUB : (i + 1) * SUB, :] for i in range(x.shape[0] // SUB)]


def inverse_kernel(
    own_rows,
    gathered_hbm,
    col_rank,
    diag,
    inverse_out,
    solved,
    products,
    scale_row,
    inverse,
    tangents,
    gathered,
    pivot,
    upcoming,
    left,
    right,
    scale_col,
    sems,
):
    size = inverse.shape[0]
    steps = size // BLOCK
    shards, height, width = gathered.shape
    fetch = pltpu.make_async_copy(diag.at[pl.ds(1, 3)], tangents, sems.at[0])
    receive = pltpu.make_async_copy(gathered_hbm, gathered, sems.at[2])
    receive.start()
    fetch.start()
    receive.wait()
    eye = lax.broadcasted_iota(jnp.int32, (BLOCK, BLOCK), 0) == lax.broadcasted_iota(
        jnp.int32, (BLOCK, BLOCK), 1
    )
    part = lambda c, n=BLOCK: slice(c * n, (c + 1) * n)

    def set_scale(c, block):
        own = jnp.where(eye, block, 0.0)
        scale_row[:, part(c)] = lax.rsqrt(jnp.sum(own, axis=0, keepdims=True))
        scale_col[part(c), :] = jnp.broadcast_to(
            lax.rsqrt(jnp.sum(own, axis=1, keepdims=True)), (BLOCK, BLOCK)
        )

    if width < size:
        for c in range(steps):
            set_scale(c, gathered[c, :BLOCK, :BLOCK])


        def place(r, o):
            c = (r + o) % steps
            block = gathered[r, :BLOCK, part(o)] * scale_col[part(r), :] * scale_row[:, part(c)]
            inverse[part(r), part(c)] = block
            if 0 < o and 2 * o < steps:
                inverse[part(c), part(r)] = block.T

        for r, o in ((0, 0), (0, 1), (1, 0)):
            place(r, o)
        beside = [
            functools.partial(place, r, o)
            for r in range(steps)
            for o in range(width // BLOCK)
            if (r, o) not in ((0, 0), (0, 1), (1, 0))
        ]
    else:
        beside = []
        for r in range(shards):
            inverse[part(r, own_rows), :] = gathered[r, :own_rows, :]
        for c in range(steps):
            set_scale(c, inverse[part(c), part(c)])
        for r in range(steps):
            for c in range(steps):
                inverse[part(r), part(c)] = (
                    inverse[part(r), part(c)] * scale_col[part(r), :] * scale_row[:, part(c)]
                )

    def eliminate(k, at, inv):
        chunk = 2 * BLOCK
        chunks = size // chunk
        twice = jnp.concatenate([inv, inv], axis=1)

        def fill_left(c):
            column = inverse[part(c, chunk), at]
            owner = 2 * c + lax.broadcasted_iota(jnp.int32, column.shape, 0) // BLOCK
            left[part(c, chunk), :] = left_terms(jnp.where(owner == k, 0.0, column))
            inverse[part(c, chunk), at] = jnp.zeros((chunk, BLOCK), F32)

        def fill_right(c):
            row = mm(inv, inverse[at, part(c, chunk)])
            owner = 2 * c + lax.broadcasted_iota(jnp.int32, row.shape, 1) // BLOCK
            row = jnp.where(owner == k, twice, row)
            right[:, part(c, chunk)] = right_terms(row)
            inverse[at, part(c, chunk)] = row

        def update(r, c):
            here = (part(r, 2 * chunk), part(c, chunk))
            inverse[here] = inverse[here] - lax.dot_general(
                left[here[0], :], right[:, here[1]], NN, preferred_element_type=F32
            )

        work = [functools.partial(fill_left, c) for c in range(chunks)]
        for c in range(chunks):
            work.append(functools.partial(fill_right, c))
            work += [functools.partial(update, r, c) for r in range(chunks // 2)]
        return work

    def invert_to_pivot(blocks, work):
        inv, following = block_inverse(*[as_rows(block) for block in blocks], work)
        pivot[...] = jnp.concatenate(inv, axis=0)
        upcoming[...] = jnp.concatenate(following, axis=0)

    one, two = part(0), part(1)
    invert_to_pivot([inverse[one, one], inverse[one, two], inverse[two, one], inverse[two, two]], beside)

    def step(k, carry):
        at = pl.ds(pl.multiple_of(k * BLOCK, BLOCK), BLOCK)
        one = pl.ds(pl.multiple_of((k + 1) * BLOCK, BLOCK), BLOCK)
        two = pl.ds(pl.multiple_of(lax.min(k + 2, steps - 1) * BLOCK, BLOCK), BLOCK)
        inv = pivot[...]
        block = upcoming[...]
        row = mm(inv, jnp.concatenate([inverse[at, one], inverse[at, two]], axis=1))
        ahead = inverse[one, two] - mm(inverse[one, at], row[:, BLOCK:])
        change = mm(inverse[two, at], row)
        below = inverse[two, one] - change[:, :BLOCK]
        below_ahead = inverse[two, two] - change[:, BLOCK:]
        invert_to_pivot([block, ahead, below, below_ahead], eliminate(k, at, inv))
        return carry

    lax.fori_loop(0, steps - 1, step, 0)
    for piece in eliminate(steps - 1, slice(size - BLOCK, size), pivot[...]):
        piece()
    store = pltpu.make_async_copy(inverse, inverse_out, sems.at[1])
    store.start()

    rank_count = solved.shape[0]
    own_ranks = rank_count // shards
    values = []
    for r in range(shards):
        pieces = []
        for at in range(own_rows, height, own_ranks):
            pieces.append(gathered[r, at : at + own_ranks, :])
        values.append(jnp.concatenate(pieces, axis=1)[:, :size])
    values = keep_rows(jnp.concatenate(values, axis=0), col_rank[0])
    z = dot_split(split2(values * scale_row[...]), split2(inverse[...])) * scale_row[...]
    solved[...] = z
    fetch.wait()
    rows = 3 * own_rows
    terms = lax.dot_general(
        jnp.concatenate(split3(tangents[...].reshape(rows, size)), axis=0),
        jnp.concatenate(split3(z), axis=0),
        NT,
        preferred_element_type=F32,
    )
    term = lambda i, k: terms[i * rows : (i + 1) * rows, k * rank_count : (k + 1) * rank_count]
    total = term(0, 0) + (
        (term(0, 1) + term(1, 0)) + (term(1, 1) + (term(0, 2) + term(2, 0)))
    )
    for t in range(3):
        products[t] = total[t * own_rows : (t + 1) * own_rows].T
    store.wait()


def in_hbm(*arrays):
    return [pltpu.with_memory_space_constraint(x, pltpu.HBM) for x in arrays]


def run_inverse(gathered, diag, col_rank, own_ranks):
    shards = gathered.shape[0]
    _, own_rows, size = diag.shape
    rank_count = own_ranks * shards
    vmem = pl.BlockSpec(memory_space=pltpu.VMEM)
    hbm = pl.BlockSpec(memory_space=pltpu.HBM)
    gathered, diag = in_hbm(gathered, diag)
    return pl.pallas_call(
        functools.partial(inverse_kernel, own_rows),
        out_shape=(
            pltpu.HBM((size, size), F32),
            jax.ShapeDtypeStruct((rank_count, size), F32),
            jax.ShapeDtypeStruct((3, rank_count, own_rows), F32),
            jax.ShapeDtypeStruct((1, size), F32),
        ),
        in_specs=[hbm, pl.BlockSpec(memory_space=pltpu.SMEM), hbm],
        out_specs=(hbm, vmem, vmem, vmem),
        scratch_shapes=[
            pltpu.VMEM((size, size), F32),
            pltpu.VMEM((3, own_rows, size), F32),
            pltpu.VMEM(gathered.shape, F32),
            pltpu.VMEM((BLOCK, BLOCK), F32),
            pltpu.VMEM((BLOCK, BLOCK), F32),
            pltpu.VMEM((size, 4 * BLOCK), BF16),
            pltpu.VMEM((4 * BLOCK, size), BF16),
            pltpu.VMEM((size, BLOCK), F32),
            pltpu.SemaphoreType.DMA((3,)),
        ],
        compiler_params=pltpu.CompilerParams(vmem_limit_bytes=INVERSE_VMEM),
        cost_estimate=pl.CostEstimate(
            flops=40 * 10**9, bytes_accessed=10 * 2**20, transcendentals=0
        ),
        name="inverse",
    )(gathered, col_rank, diag)


def dot_split(left, right, dims=NN):
    left_hi, left_lo = left
    right_hi, right_lo = right
    rows = left_hi.shape[0]
    both = lax.dot_general(
        jnp.concatenate([left_hi, left_lo], axis=0), right_hi, dims, preferred_element_type=F32
    )
    cross = lax.dot_general(left_hi, right_lo, dims, preferred_element_type=F32)
    return both[:rows] + (both[rows:] + cross)


def keep_rows(x, rank):
    return jnp.where(lax.broadcasted_iota(jnp.int32, x.shape, 0) < rank, x, 0.0)


def put(refs, at, x):
    hi, lo = split2(x)
    refs[0][at] = hi
    refs[1][at] = lo


def shard_values(refs, position, count, p, comp):
    value = lambda i: refs[i][p, comp]
    if len(refs) == count:
        return [value(i) for i in range(count)]
    pick = lambda here, i, k: jnp.where(here, value(i), value(k))
    return [
        value(0),
        pick(position == 0, 3, 1),
        pick(position < 2, 4, 5),
        pick(position == 3, 3, 2),
    ]


def put_shards(refs, slot, sources, position, count, p, comp, rank):
    values = shard_values(sources, position, count, p, comp)
    rank_count, width = values[0].shape
    for s, value in enumerate(values):
        owner = lax.rem(position - s + count, count)
        at = pl.ds(pl.multiple_of(owner * width, width), width)
        put(refs, (p, pl.ds(slot * rank_count, rank_count), at), keep_rows(value, rank))


def col_component(ref, comp, rank):
    whole = jnp.concatenate([ref[g, comp] for g in range(ref.shape[0])], axis=0)
    return keep_rows(whole, rank)


def recompress_kernel(
    tiles, shards, count, place, panel_rank, col_rank, tile_rank, keep_rank, *refs
):
    rows_any = refs[:shards]
    (
        cols_any,
        trailing_any,
        sketch_any,
        solved_any,
        inverse_any,
        scale,
        products_any,
        out_any,
        left_hi,
        left_lo,
        right_hi,
        right_lo,
        panel_hi,
        panel_lo,
        cols,
        trailing,
        rows_all,
        inverse,
        sketch,
        solved,
        products,
        out,
        sems,
    ) = refs[shards:]
    rows_in = [rows_all.at[i] for i in range(shards)]
    pairs = [(cols_any, cols)]
    pairs += [(trailing_any.at[p], trailing.at[p]) for p in range(tiles)]
    pairs += list(zip(rows_any, rows_in))
    pairs += [(sketch_any, sketch), (solved_any, solved), (products_any, products)]
    pairs.append((inverse_any, inverse))
    copies = [
        pltpu.make_async_copy(source, target, sems.at[i])
        for i, (source, target) in enumerate(pairs)
    ]
    for copy in copies:
        copy.start()
    stores = []

    def store(p, begin):
        part = pl.ds(begin, 4)
        copy = pltpu.make_async_copy(
            out.at[p, 0, part], out_any.at[p, 0, part], sems.at[len(pairs) + len(stores)]
        )
        copy.start()
        stores.append(copy)

    lefts, rights, panels = (left_hi, left_lo), (right_hi, right_lo), (panel_hi, panel_lo)
    rank_count, size = sketch.shape
    up_scale = math.sqrt(size)
    down_scale = 1.0 / math.sqrt(rank_count)
    position = place[0]
    block = lambda x, i: x[:, i * rank_count : (i + 1) * rank_count]
    band = lambda x, i: x[i * rank_count : (i + 1) * rank_count]
    slot = lambda p, i, n=1: (p, slice(i * rank_count, (i + n) * rank_count), slice(None))
    take = lambda pair, at: (pair[0][at], pair[1][at])

    copies[0].wait()
    for t in range(4):
        u_col = col_component(cols, t, col_rank[0])
        for p in range(tiles):
            put(rights, slot(p, 1 if t == 0 else 4 + t), u_col)
    for p in range(tiles):
        copies[1 + p].wait()
        for t in range(4):
            rank = tile_rank[p, 0]
            put(lefts, slot(p, 0 if t == 0 else 1 + t), keep_rows(trailing[p, 0, t], rank))
            put(rights, slot(p, 0 if t == 0 else 1 + t), keep_rows(trailing[p, 0, 4 + t], rank))
    for copy in copies[1 + tiles : -1]:
        copy.wait()
    for p in range(tiles):
        for t in range(4):
            rank = panel_rank[p]
            put_shards(lefts, 1 if t == 0 else 4 + t, rows_in, position, count, p, t, rank)
            put_shards(panels, t, rows_in, position, count, p, 4 + t, rank)

    sides = []
    for t in range(3):
        whole = jnp.concatenate([products[r, t] for r in range(products.shape[0])], axis=1)
        sides.append(col_component(cols, 5 + t, col_rank[0]) - whole)
    sides = jnp.concatenate(sides, axis=0) * scale[...]
    copies[-1].wait()
    dz = dot_split(split2(sides), split2(inverse[...])) * scale[...]
    z_hi, z_lo = split2(solved[...])
    dz_hi, dz_lo = split2(dz)
    zz = (jnp.concatenate([z_hi, dz_hi], axis=0), jnp.concatenate([z_lo, dz_lo], axis=0))
    s = split2(sketch[...])

    state = []
    for p in range(tiles):
        live = lax.broadcasted_iota(jnp.int32, (rank_count, 1), 0) < keep_rank[p, 0]
        mixes = dot_split(take(panels, slot(p, 0, 4)), zz, NT)
        sketched = jnp.where(live, dot_split(s, take(rights, slot(p, 0, 8)), NT), 0.0)
        mix = mixes[:rank_count, :rank_count]
        base_u = -mm(block(sketched, 1), mix, NT)
        pair = jnp.concatenate([block(sketched, 0), base_u], axis=1)
        bases = take(lefts, slot(p, 0, 2))
        y = dot_split(split2(pair), bases)
        y_split = split2(y)
        gram = dot_split(y_split, y_split, NT)
        eye = lax.broadcasted_iota(jnp.int32, gram.shape, 0) == lax.broadcasted_iota(
            jnp.int32, gram.shape, 1
        )
        gram = gram + jnp.where(eye & jnp.logical_not(live), 1.0, 0.0)
        augmented = jnp.concatenate([gram, jnp.where(eye, 1.0, 0.0)], axis=1)
        cross = dot_split(bases, take(lefts, slot(p, 0, 8)), NT)
        state.append((mixes, sketched, pair, cross, augmented))

    factors = [factor_inverse(as_rows(entry[-1]), rank_count) for entry in state]

    for p in range(tiles):
        mixes, sketched, pair, cross, _ = state[p]
        rinv = jnp.concatenate(factors[p], axis=0)[:, rank_count:]
        mix = mixes[:rank_count, :rank_count]
        dmix = [band(block(mixes, 0), 1 + t) + band(block(mixes, 1 + t), 0) for t in range(3)]
        su = [block(sketched, 1)] + [block(sketched, 5 + t) for t in range(3)]
        u_mix = mm(jnp.concatenate(su[1:], axis=0), mix, NT)
        u_dmix = mm(su[0], jnp.concatenate(dmix, axis=0), NT)
        u_sides = [-(band(u_mix, t) + block(u_dmix, t)) for t in range(3)]
        sv = [block(sketched, 2 + t) for t in range(3)]
        coefs = mm(rinv, jnp.concatenate([pair] + sv + u_sides, axis=1))
        q_coef = coefs[:, : 2 * rank_count]
        q_parts = mm(q_coef, cross)
        phis = []
        for t in range(3):
            e_coef = jnp.concatenate(
                [block(coefs, 2 + t), block(coefs, 5 + t), q_coef], axis=1
            )
            q_side = jnp.concatenate(
                [block(q_parts, 0), block(q_parts, 1), block(q_parts, 2 + t), block(q_parts, 5 + t)],
                axis=1,
            )
            half = mm(e_coef, q_side, NT)
            sym = half + half.T
            i0 = lax.broadcasted_iota(jnp.int32, sym.shape, 0)
            i1 = lax.broadcasted_iota(jnp.int32, sym.shape, 1)
            phis.append(jnp.where(i0 > i1, sym, jnp.where(i0 == i1, 0.5 * sym, 0.0)))
        turned = mm(jnp.concatenate(phis, axis=0), q_coef)
        none = jnp.zeros((rank_count, rank_count), F32)
        rows = [jnp.concatenate([q_coef] + [none] * 6, axis=1)]
        for t in range(3):
            head = jnp.concatenate([block(coefs, 2 + t), block(coefs, 5 + t)], axis=1)
            tail = [none] * 6
            tail[t], tail[3 + t] = block(q_coef, 0), block(q_coef, 1)
            rows.append(jnp.concatenate([head - band(turned, t)] + tail, axis=1))
        basis_coef = jnp.concatenate(rows, axis=0)
        basis = dot_split(split2(basis_coef), take(lefts, slot(p, 0, 8))) * up_scale
        for t in range(4):
            out[p, 0, t] = band(basis, t)
        store(p, 0)
        dq_parts = mm(basis_coef[rank_count:], cross, NT)
        on_u = mm(
            block(dq_parts, 1)
            + jnp.concatenate([block(q_parts, 5 + t) for t in range(3)], axis=0),
            mix,
        )
        on_dmix = mm(block(q_parts, 1), jnp.concatenate(dmix, axis=1))
        q_mix = mm(block(q_parts, 1), mix)
        rows = [jnp.concatenate([block(q_parts, 0), -q_mix] + [none] * 6, axis=1)]
        for t in range(3):
            on_v = band(block(dq_parts, 0), t) + block(q_parts, 2 + t)
            tail = [none] * 6
            tail[t], tail[3 + t] = block(q_parts, 0), -q_mix
            rows.append(
                jnp.concatenate([on_v, -(band(on_u, t) + block(on_dmix, t))] + tail, axis=1)
            )
        coeff = dot_split(
            split2(jnp.concatenate(rows, axis=0) * down_scale), take(rights, slot(p, 0, 8))
        )
        for t in range(4):
            out[p, 0, 4 + t] = band(coeff, t)
        store(p, 4)
    for copy in stores:
        copy.wait()


def run_recompress(
    place, ranks, count, shards, cols, trailing, sketch, solved, inverse, scale, products
):
    tiles = trailing.shape[0]
    rank_count, size = sketch.shape
    vmem = pl.BlockSpec(memory_space=pltpu.VMEM)
    smem = pl.BlockSpec(memory_space=pltpu.SMEM)
    hbm = pl.BlockSpec(memory_space=pltpu.HBM)
    shards = in_hbm(*shards)
    cols, trailing, sketch, solved, inverse, products = in_hbm(
        cols, trailing, sketch, solved, inverse, products
    )
    return pl.pallas_call(
        functools.partial(recompress_kernel, tiles, len(shards), count),
        out_shape=jax.ShapeDtypeStruct(trailing.shape, F32),
        in_specs=[smem] * 5
        + [hbm] * len(shards)
        + [hbm] * 5
        + [vmem, hbm],
        out_specs=hbm,
        scratch_shapes=[pltpu.VMEM((tiles, 8 * rank_count, size), BF16)] * 4
        + [pltpu.VMEM((tiles, 4 * rank_count, size), BF16)] * 2
        + [
            pltpu.VMEM(cols.shape, F32),
            pltpu.VMEM(trailing.shape, F32),
            pltpu.VMEM((len(shards),) + shards[0].shape, F32),
            pltpu.VMEM(inverse.shape, F32),
            pltpu.VMEM(sketch.shape, F32),
            pltpu.VMEM(solved.shape, F32),
            pltpu.VMEM(products.shape, F32),
            pltpu.VMEM(trailing.shape, F32),
            pltpu.SemaphoreType.DMA((5 + tiles + len(shards) + 2 * tiles,)),
        ],
        compiler_params=pltpu.CompilerParams(vmem_limit_bytes=RECOMPRESS_VMEM),
        cost_estimate=pl.CostEstimate(
            flops=10 * 10**9, bytes_accessed=20 * 2**20, transcendentals=0
        ),
        name="recompress",
    )(place, *ranks, *shards, cols, trailing, sketch, solved, inverse, scale, products)


def on_device(
    row_count,
    col_count,
    diag,
    panel_rows,
    panel_cols,
    trailing,
    sketch,
    panel_rank,
    col_rank,
    tile_rank,
    keep_rank,
):
    own_rows = diag.shape[1]
    own_ranks = panel_cols.shape[2]
    comps = panel_cols.shape[1]
    size = sketch.shape[1]
    values = panel_cols[0, 4]
    own = diag[0]
    if own_rows == BLOCK and row_count > 2:
        width = (row_count // 2 + 1) * BLOCK
        own = lax.dynamic_slice(
            jnp.concatenate([own, own[:, : width - BLOCK]], axis=1),
            (0, lax.axis_index("row") * BLOCK),
            (BLOCK, width),
        )
        values = jnp.pad(values, ((0, 0), (0, -size % width)))
        values = jnp.concatenate(
            [values[:, i : i + width] for i in range(0, values.shape[1], width)], axis=0
        )
    gathered = lax.all_gather(jnp.concatenate([own, values], axis=0), "row", axis=0)
    if col_count == 4:
        send = lambda x, pairs: lax.ppermute(x, "col", pairs)
        from_left = send(panel_rows, [(0, 1), (1, 2), (2, 3)])
        from_right = send(panel_rows, [(1, 0), (2, 1), (3, 2)])
        late_cols, late_rows, from_left, from_right, gathered = lax.optimization_barrier(
            (panel_cols[0], panel_rows, from_left, from_right, gathered)
        )
        shards = [
            panel_rows,
            from_left,
            from_right,
            send(late_rows, [(0, 3), (3, 0)]),
            send(from_right, [(1, 0), (2, 1)]),
            send(from_left, [(1, 2), (2, 3)]),
        ]
    else:
        shards = [panel_rows] + [
            lax.ppermute(panel_rows, "col", [(i, (i + s) % col_count) for i in range(col_count)])
            for s in range(1, col_count)
        ]
        late_cols, gathered = lax.optimization_barrier((panel_cols[0], gathered))
    cols = lax.all_gather(late_cols, "row", axis=0)
    if own_ranks != SUB:
        cols = cols.reshape(-1, SUB // own_ranks, comps, own_ranks, size)
        cols = cols.transpose(0, 2, 1, 3, 4).reshape(-1, comps, SUB, size)
    inverse, solved, products, scale = run_inverse(
        gathered, diag, col_rank, own_ranks
    )
    all_products = lax.all_gather(products, "row", axis=0)
    place = lax.axis_index("col").astype(jnp.int32).reshape(1)
    ranks = (panel_rank, col_rank, tile_rank, keep_rank)
    return run_recompress(
        place,
        ranks,
        col_count,
        shards,
        cols,
        trailing,
        sketch,
        solved,
        inverse,
        scale,
        all_products,
    )


def solution(mesh):
    in_specs = (
        P(None, "row", None),
        P("row", None, None, "col"),
        P("col", None, "row", None),
        P("row", "col", None, None, None),
        P(),
        P("row"),
        P("col"),
        P("row", "col"),
        P("row", "col"),
    )
    out_specs = P("row", "col", None, None, None)
    body = functools.partial(on_device, mesh.shape["row"], mesh.shape["col"])
    return jax.shard_map(body, mesh=mesh, in_specs=in_specs, out_specs=out_specs, check_vma=False)
```

```python
import functools
import math

import jax
import jax.numpy as jnp
from jax import lax
from jax.experimental import pallas as pl
from jax.experimental.pallas import tpu as pltpu
from jax.sharding import PartitionSpec as P

HIGHEST = lax.Precision.HIGHEST
F32 = jnp.float32
BF16 = jnp.bfloat16
BLOCK = 128
SUB = 8
BAND = 4
INVERSE_VMEM = 28 * 1024 * 1024
RECOMPRESS_VMEM = 46 * 1024 * 1024

NN = (((1,), (0,)), ((), ()))
NT = (((1,), (1,)), ((), ()))


def mm(left, right, dims=NN):
    return lax.dot_general(left, right, dims, precision=HIGHEST, preferred_element_type=F32)


def split2(x):
    hi = x.astype(BF16)
    return hi, (x - hi.astype(F32)).astype(BF16)


def split3(x):
    hi = x.astype(BF16)
    rest = x - hi.astype(F32)
    mid = rest.astype(BF16)
    return hi, mid, (rest - mid.astype(F32)).astype(BF16)


def left_terms(x):
    hi, lo = split2(x)
    return jnp.concatenate([hi, hi, lo, lo], axis=1)


def right_terms(x):
    hi, lo = split2(x)
    return jnp.concatenate([hi, lo, hi, lo], axis=0)


def lane_rep(x, lane):
    return jnp.broadcast_to(x[:, lane : lane + 1], (SUB, BLOCK))


def sub_rep(x, row):
    return jnp.broadcast_to(x[row : row + 1, :], (SUB, BLOCK))


def tree_sum(terms):
    while len(terms) > 1:
        terms = [
            terms[i] + terms[i + 1] if i + 1 < len(terms) else terms[i]
            for i in range(0, len(terms), 2)
        ]
    return terms[0]


def sub_index():
    return lax.broadcasted_iota(jnp.int32, (SUB, BLOCK), 0)


def lane_index():
    return lax.broadcasted_iota(jnp.int32, (SUB, BLOCK), 1)


def micro_inverse(cols):
    sub = sub_index()
    cols = list(cols)
    for j in range(0, SUB, 2):
        first, second = sub == j, sub == j + 1
        pair = first | second
        a, b, d = sub_rep(cols[j], j), sub_rep(cols[j], j + 1), sub_rep(cols[j + 1], j + 1)
        inv_det = 1.0 / (a * d - b * b)
        f0 = jnp.where(first, -1.0, jnp.where(second, 0.0, cols[j]))
        f1 = jnp.where(second, -1.0, jnp.where(first, 0.0, cols[j + 1]))
        fresh = []
        for k in range(SUB):
            if k == j:
                fresh.append((f1 * b - f0 * d) * inv_det)
            elif k == j + 1:
                fresh.append((f0 * b - f1 * a) * inv_det)
            else:
                x0, x1 = sub_rep(cols[k], j), sub_rep(cols[k], j + 1)
                change = f0 * (d * x0 - b * x1) + f1 * (a * x1 - b * x0)
                fresh.append(jnp.where(pair, 0.0, cols[k]) - change * inv_det)
        cols = fresh
    return cols


def micro_factor(cols):
    sub = sub_index()
    cols = list(cols)
    low = [jnp.where(sub == k, 1.0, 0.0) for k in range(SUB)]
    pivots = jnp.zeros((SUB, BLOCK), F32)
    for j in range(SUB):
        here = sub == j
        piv = sub_rep(cols[j], j)
        inv_piv = 1.0 / piv
        factor = jnp.where(here, -1.0, cols[j])
        pivots = jnp.where(here, piv, pivots)
        below = jnp.where(sub > j, cols[j], 0.0)
        for k in range(j + 1):
            low[k] = low[k] - below * sub_rep(low[k], j) * inv_piv
        cols = [
            -factor * inv_piv
            if k == j
            else jnp.where(here, 0.0, cols[k]) - factor * (sub_rep(cols[k], j) * inv_piv)
            for k in range(SUB)
        ]
    scale = lax.rsqrt(pivots)
    return cols, [scale * c for c in low]


def band_left(x, band):
    lanes = BAND * SUB
    hi = x.astype(BF16).astype(F32)
    rest = x - hi
    mid = rest.astype(BF16).astype(F32)
    lo = rest - mid
    place = lax.rem(
        lax.broadcasted_iota(jnp.int32, x.shape, 1) // lanes - band + BLOCK // lanes, BLOCK // lanes
    )
    hi_next = pltpu.roll(hi, lanes, 1)
    mid_two = pltpu.roll(mid, 2 * lanes, 1)
    mid_three = pltpu.roll(mid, 3 * lanes, 1)
    one = jnp.where(
        place == 0, hi, jnp.where(place == 1, hi_next, jnp.where(place == 2, mid_two, mid_three))
    )
    two = jnp.where(place == 0, lo, jnp.where(place == 1, hi_next, 0.0))
    return jnp.concatenate([one, two], axis=1).astype(BF16)


def band_right(x, band):
    hi, mid, lo = split3(x)
    none = jnp.zeros(x.shape, BF16)
    turn = lambda parts: [parts[(i - band) % len(parts)] for i in range(len(parts))]
    return jnp.concatenate(turn([hi, mid, hi, mid]) + turn([hi, lo, none, none]), axis=0)


def block_inverse(rows, ahead, below, below_ahead, work):
    rows, ahead, below, below_ahead = list(rows), list(ahead), list(below), list(below_ahead)
    count = len(rows)
    sub, lane = sub_index(), lane_index()
    for first in range(0, count, BAND):
        band = range(first, first + BAND)
        others = [(first + BAND + i) % count for i in range(count - BAND)]
        left = band_left(
            jnp.concatenate([rows[i] for i in others] + below, axis=0), first // BAND
        )
        for g in band:
            at = g * SUB
            inside = (lane >= at) & (lane < at + SUB)
            inv = micro_inverse([lane_rep(rows[g], at + k) for k in range(SUB)])
            own = jnp.where(inside, jnp.where(lane - at == sub, 1.0, 0.0), rows[g])
            new = tree_sum([inv[k] * sub_rep(own, k) for k in range(SUB)])
            news = [sub_rep(new, k) for k in range(SUB)]
            new_ahead = tree_sum([inv[k] * sub_rep(ahead[g], k) for k in range(SUB)])
            news_ahead = [sub_rep(new_ahead, k) for k in range(SUB)]
            for i in [first + (g - first + 1 + i) % BAND for i in range(BAND - 1)]:
                factors = [lane_rep(rows[i], at + k) for k in range(SUB)]
                kept = jnp.where(inside, 0.0, rows[i])
                rows[i] = kept - tree_sum([factors[k] * news[k] for k in range(SUB)])
                ahead[i] = ahead[i] - tree_sum([factors[k] * news_ahead[k] for k in range(SUB)])
            rows[g], ahead[g] = new, new_ahead
            for piece in work[g * len(work) // count : (g + 1) * len(work) // count]:
                piece()
        inside = (lane >= first * SUB) & (lane < (first + BAND) * SUB)
        top = jnp.concatenate(
            [jnp.concatenate([x[i] for i in band], axis=0) for x in (rows, ahead)], axis=1
        )
        change = lax.dot_general(
            left, band_right(top, first // BAND), NN, preferred_element_type=F32
        )
        here, there = as_rows(change[:, :BLOCK]), as_rows(change[:, BLOCK:])
        for j, i in enumerate(others):
            rows[i] = jnp.where(inside, 0.0, rows[i]) - here[j]
            ahead[i] = ahead[i] - there[j]
        for j in range(count):
            below[j] = below[j] - here[len(others) + j]
            below_ahead[j] = below_ahead[j] - there[len(others) + j]
    return rows, below_ahead


def factor_inverse(rows, width):
    rows = list(rows)
    count = width // SUB
    for g in range(count):
        at = g * SUB
        inv, low = micro_factor([lane_rep(rows[g], at + k) for k in range(SUB)])
        own = rows[g]
        own_rep = [sub_rep(own, k) for k in range(SUB)]
        new = tree_sum([inv[k] * own_rep[k] for k in range(SUB)])
        news = [sub_rep(new, k) for k in range(SUB)]
        for i in range(g + 1, count):
            rows[i] = rows[i] - tree_sum(
                [lane_rep(rows[i], at + k) * news[k] for k in range(SUB)]
            )
        rows[g] = tree_sum([low[k] * own_rep[k] for k in range(SUB)])
    return rows


def as_rows(x):
    return [x[i * SUB : (i + 1) * SUB, :] for i in range(x.shape[0] // SUB)]


def inverse_kernel(
    own_rows,
    gathered_hbm,
    col_rank,
    diag,
    inverse_out,
    solved,
    products,
    scale_row,
    inverse,
    tangents,
    gathered,
    pivot,
    upcoming,
    left,
    right,
    scale_col,
    sems,
):
    size = inverse.shape[0]
    steps = size // BLOCK
    shards, height, width = gathered.shape
    fetch = pltpu.make_async_copy(diag.at[pl.ds(1, 3)], tangents, sems.at[0])
    receive = pltpu.make_async_copy(gathered_hbm, gathered, sems.at[2])
    receive.start()
    fetch.start()
    receive.wait()
    eye = lax.broadcasted_iota(jnp.int32, (BLOCK, BLOCK), 0) == lax.broadcasted_iota(
        jnp.int32, (BLOCK, BLOCK), 1
    )
    part = lambda c, n=BLOCK: slice(c * n, (c + 1) * n)

    def set_scale(c, block):
        own = jnp.where(eye, block, 0.0)
        scale_row[:, part(c)] = lax.rsqrt(jnp.sum(own, axis=0, keepdims=True))
        scale_col[part(c), :] = jnp.broadcast_to(
            lax.rsqrt(jnp.sum(own, axis=1, keepdims=True)), (BLOCK, BLOCK)
        )

    if width < size:
        for c in range(steps):
            set_scale(c, gathered[c, :BLOCK, :BLOCK])


        def place(r, o):
            c = (r + o) % steps
            block = gathered[r, :BLOCK, part(o)] * scale_col[part(r), :] * scale_row[:, part(c)]
            inverse[part(r), part(c)] = block
            if 0 < o and 2 * o < steps:
                inverse[part(c), part(r)] = block.T

        for r, o in ((0, 0), (0, 1), (1, 0)):
            place(r, o)
        beside = [
            functools.partial(place, r, o)
            for r in range(steps)
            for o in range(width // BLOCK)
            if (r, o) not in ((0, 0), (0, 1), (1, 0))
        ]
    else:
        beside = []
        for r in range(shards):
            inverse[part(r, own_rows), :] = gathered[r, :own_rows, :]
        for c in range(steps):
            set_scale(c, inverse[part(c), part(c)])
        for r in range(steps):
            for c in range(steps):
                inverse[part(r), part(c)] = (
                    inverse[part(r), part(c)] * scale_col[part(r), :] * scale_row[:, part(c)]
                )

    def eliminate(k, at, inv):
        chunk = 2 * BLOCK
        chunks = size // chunk
        twice = jnp.concatenate([inv, inv], axis=1)

        def fill_left(c):
            column = inverse[part(c, chunk), at]
            owner = 2 * c + lax.broadcasted_iota(jnp.int32, column.shape, 0) // BLOCK
            left[part(c, chunk), :] = left_terms(jnp.where(owner == k, 0.0, column))
            inverse[part(c, chunk), at] = jnp.zeros((chunk, BLOCK), F32)

        def fill_right(c):
            row = mm(inv, inverse[at, part(c, chunk)])
            owner = 2 * c + lax.broadcasted_iota(jnp.int32, row.shape, 1) // BLOCK
            row = jnp.where(owner == k, twice, row)
            right[:, part(c, chunk)] = right_terms(row)
            inverse[at, part(c, chunk)] = row

        def update(r, c):
            here = (part(r, 2 * chunk), part(c, chunk))
            inverse[here] = inverse[here] - lax.dot_general(
                left[here[0], :], right[:, here[1]], NN, preferred_element_type=F32
            )

        work = [functools.partial(fill_left, c) for c in range(chunks)]
        for c in range(chunks):
            work.append(functools.partial(fill_right, c))
            work += [functools.partial(update, r, c) for r in range(chunks // 2)]
        return work

    def invert_to_pivot(blocks, work):
        inv, following = block_inverse(*[as_rows(block) for block in blocks], work)
        pivot[...] = jnp.concatenate(inv, axis=0)
        upcoming[...] = jnp.concatenate(following, axis=0)

    one, two = part(0), part(1)
    invert_to_pivot([inverse[one, one], inverse[one, two], inverse[two, one], inverse[two, two]], beside)

    def step(k, carry):
        at = pl.ds(pl.multiple_of(k * BLOCK, BLOCK), BLOCK)
        one = pl.ds(pl.multiple_of((k + 1) * BLOCK, BLOCK), BLOCK)
        two = pl.ds(pl.multiple_of(lax.min(k + 2, steps - 1) * BLOCK, BLOCK), BLOCK)
        inv = pivot[...]
        block = upcoming[...]
        row = mm(inv, jnp.concatenate([inverse[at, one], inverse[at, two]], axis=1))
        ahead = inverse[one, two] - mm(inverse[one, at], row[:, BLOCK:])
        change = mm(inverse[two, at], row)
        below = inverse[two, one] - change[:, :BLOCK]
        below_ahead = inverse[two, two] - change[:, BLOCK:]
        invert_to_pivot([block, ahead, below, below_ahead], eliminate(k, at, inv))
        return carry

    lax.fori_loop(0, steps - 1, step, 0)
    for piece in eliminate(steps - 1, slice(size - BLOCK, size), pivot[...]):
        piece()
    store = pltpu.make_async_copy(inverse, inverse_out, sems.at[1])
    store.start()

    rank_count = solved.shape[0]
    own_ranks = rank_count // shards
    values = []
    for r in range(shards):
        pieces = []
        for at in range(own_rows, height, own_ranks):
            pieces.append(gathered[r, at : at + own_ranks, :])
        values.append(jnp.concatenate(pieces, axis=1)[:, :size])
    values = keep_rows(jnp.concatenate(values, axis=0), col_rank[0])
    z = dot_split(split2(values * scale_row[...]), split2(inverse[...])) * scale_row[...]
    solved[...] = z
    fetch.wait()
    rows = 3 * own_rows
    terms = lax.dot_general(
        jnp.concatenate(split3(tangents[...].reshape(rows, size)), axis=0),
        jnp.concatenate(split3(z), axis=0),
        NT,
        preferred_element_type=F32,
    )
    term = lambda i, k: terms[i * rows : (i + 1) * rows, k * rank_count : (k + 1) * rank_count]
    total = term(0, 0) + (
        (term(0, 1) + term(1, 0)) + (term(1, 1) + (term(0, 2) + term(2, 0)))
    )
    for t in range(3):
        products[t] = total[t * own_rows : (t + 1) * own_rows].T
    store.wait()


def in_hbm(*arrays):
    return [pltpu.with_memory_space_constraint(x, pltpu.HBM) for x in arrays]


def run_inverse(gathered, diag, col_rank, own_ranks):
    shards = gathered.shape[0]
    _, own_rows, size = diag.shape
    rank_count = own_ranks * shards
    vmem = pl.BlockSpec(memory_space=pltpu.VMEM)
    hbm = pl.BlockSpec(memory_space=pltpu.HBM)
    gathered, diag = in_hbm(gathered, diag)
    return pl.pallas_call(
        functools.partial(inverse_kernel, own_rows),
        out_shape=(
            pltpu.HBM((size, size), F32),
            jax.ShapeDtypeStruct((rank_count, size), F32),
            jax.ShapeDtypeStruct((3, rank_count, own_rows), F32),
            jax.ShapeDtypeStruct((1, size), F32),
        ),
        in_specs=[hbm, pl.BlockSpec(memory_space=pltpu.SMEM), hbm],
        out_specs=(hbm, vmem, vmem, vmem),
        scratch_shapes=[
            pltpu.VMEM((size, size), F32),
            pltpu.VMEM((3, own_rows, size), F32),
            pltpu.VMEM(gathered.shape, F32),
            pltpu.VMEM((BLOCK, BLOCK), F32),
            pltpu.VMEM((BLOCK, BLOCK), F32),
            pltpu.VMEM((size, 4 * BLOCK), BF16),
            pltpu.VMEM((4 * BLOCK, size), BF16),
            pltpu.VMEM((size, BLOCK), F32),
            pltpu.SemaphoreType.DMA((3,)),
        ],
        compiler_params=pltpu.CompilerParams(vmem_limit_bytes=INVERSE_VMEM),
        cost_estimate=pl.CostEstimate(
            flops=40 * 10**9, bytes_accessed=10 * 2**20, transcendentals=0
        ),
        name="inverse",
    )(gathered, col_rank, diag)


def dot_split(left, right, dims=NN):
    left_hi, left_lo = left
    right_hi, right_lo = right
    rows = left_hi.shape[0]
    both = lax.dot_general(
        jnp.concatenate([left_hi, left_lo], axis=0), right_hi, dims, preferred_element_type=F32
    )
    cross = lax.dot_general(left_hi, right_lo, dims, preferred_element_type=F32)
    return both[:rows] + (both[rows:] + cross)


def keep_rows(x, rank):
    return jnp.where(lax.broadcasted_iota(jnp.int32, x.shape, 0) < rank, x, 0.0)


def put(refs, at, x):
    hi, lo = split2(x)
    refs[0][at] = hi
    refs[1][at] = lo


def shard_values(refs, position, count, p, comp):
    return [refs[i][p, comp] for i in range(count)]


def put_shards(refs, slot, sources, position, count, p, comp, rank):
    values = shard_values(sources, position, count, p, comp)
    rank_count, width = values[0].shape
    for s, value in enumerate(values):
        owner = lax.rem(position - s + count, count)
        at = pl.ds(pl.multiple_of(owner * width, width), width)
        put(refs, (p, pl.ds(slot * rank_count, rank_count), at), keep_rows(value, rank))


def col_component(ref, comp, rank):
    whole = jnp.concatenate([ref[g, comp] for g in range(ref.shape[0])], axis=0)
    return keep_rows(whole, rank)


def recompress_kernel(
    tiles, shards, count, place, panel_rank, col_rank, tile_rank, keep_rank, *refs
):
    rows_any = refs[:shards]
    (
        cols_any,
        trailing_any,
        sketch_any,
        solved_any,
        inverse_any,
        scale,
        products_any,
        out_any,
        left_hi,
        left_lo,
        right_hi,
        right_lo,
        panel_hi,
        panel_lo,
        cols,
        trailing,
        rows_all,
        inverse,
        sketch,
        solved,
        products,
        out,
        sems,
    ) = refs[shards:]
    rows_in = [rows_all.at[i] for i in range(shards)]
    pairs = [(cols_any, cols)]
    pairs += [(trailing_any.at[p], trailing.at[p]) for p in range(tiles)]
    pairs += list(zip(rows_any, rows_in))
    pairs += [(sketch_any, sketch), (solved_any, solved), (products_any, products)]
    pairs.append((inverse_any, inverse))
    copies = [
        pltpu.make_async_copy(source, target, sems.at[i])
        for i, (source, target) in enumerate(pairs)
    ]
    for copy in copies:
        copy.start()
    stores = []

    def store(p, begin):
        part = pl.ds(begin, 4)
        copy = pltpu.make_async_copy(
            out.at[p, 0, part], out_any.at[p, 0, part], sems.at[len(pairs) + len(stores)]
        )
        copy.start()
        stores.append(copy)

    lefts, rights, panels = (left_hi, left_lo), (right_hi, right_lo), (panel_hi, panel_lo)
    rank_count, size = sketch.shape
    up_scale = math.sqrt(size)
    down_scale = 1.0 / math.sqrt(rank_count)
    position = place[0]
    block = lambda x, i: x[:, i * rank_count : (i + 1) * rank_count]
    band = lambda x, i: x[i * rank_count : (i + 1) * rank_count]
    slot = lambda p, i, n=1: (p, slice(i * rank_count, (i + n) * rank_count), slice(None))
    take = lambda pair, at: (pair[0][at], pair[1][at])

    copies[0].wait()
    for t in range(4):
        u_col = col_component(cols, t, col_rank[0])
        for p in range(tiles):
            put(rights, slot(p, 1 if t == 0 else 4 + t), u_col)
    for p in range(tiles):
        copies[1 + p].wait()
        for t in range(4):
            rank = tile_rank[p, 0]
            put(lefts, slot(p, 0 if t == 0 else 1 + t), keep_rows(trailing[p, 0, t], rank))
            put(rights, slot(p, 0 if t == 0 else 1 + t), keep_rows(trailing[p, 0, 4 + t], rank))
    for copy in copies[1 + tiles : -1]:
        copy.wait()
    for p in range(tiles):
        for t in range(4):
            rank = panel_rank[p]
            put_shards(lefts, 1 if t == 0 else 4 + t, rows_in, position, count, p, t, rank)
            put_shards(panels, t, rows_in, position, count, p, 4 + t, rank)

    sides = []
    for t in range(3):
        whole = jnp.concatenate([products[r, t] for r in range(products.shape[0])], axis=1)
        sides.append(col_component(cols, 5 + t, col_rank[0]) - whole)
    sides = jnp.concatenate(sides, axis=0) * scale[...]
    copies[-1].wait()
    dz = dot_split(split2(sides), split2(inverse[...])) * scale[...]
    z_hi, z_lo = split2(solved[...])
    dz_hi, dz_lo = split2(dz)
    zz = (jnp.concatenate([z_hi, dz_hi], axis=0), jnp.concatenate([z_lo, dz_lo], axis=0))
    s = split2(sketch[...])

    state = []
    for p in range(tiles):
        live = lax.broadcasted_iota(jnp.int32, (rank_count, 1), 0) < keep_rank[p, 0]
        mixes = dot_split(take(panels, slot(p, 0, 4)), zz, NT)
        sketched = jnp.where(live, dot_split(s, take(rights, slot(p, 0, 8)), NT), 0.0)
        mix = mixes[:rank_count, :rank_count]
        base_u = -mm(block(sketched, 1), mix, NT)
        pair = jnp.concatenate([block(sketched, 0), base_u], axis=1)
        bases = take(lefts, slot(p, 0, 2))
        y = dot_split(split2(pair), bases)
        y_split = split2(y)
        gram = dot_split(y_split, y_split, NT)
        eye = lax.broadcasted_iota(jnp.int32, gram.shape, 0) == lax.broadcasted_iota(
            jnp.int32, gram.shape, 1
        )
        gram = gram + jnp.where(eye & jnp.logical_not(live), 1.0, 0.0)
        augmented = jnp.concatenate([gram, jnp.where(eye, 1.0, 0.0)], axis=1)
        cross = dot_split(bases, take(lefts, slot(p, 0, 8)), NT)
        state.append((mixes, sketched, pair, cross, augmented))

    factors = [factor_inverse(as_rows(entry[-1]), rank_count) for entry in state]

    for p in range(tiles):
        mixes, sketched, pair, cross, _ = state[p]
        rinv = jnp.concatenate(factors[p], axis=0)[:, rank_count:]
        mix = mixes[:rank_count, :rank_count]
        dmix = [band(block(mixes, 0), 1 + t) + band(block(mixes, 1 + t), 0) for t in range(3)]
        su = [block(sketched, 1)] + [block(sketched, 5 + t) for t in range(3)]
        u_mix = mm(jnp.concatenate(su[1:], axis=0), mix, NT)
        u_dmix = mm(su[0], jnp.concatenate(dmix, axis=0), NT)
        u_sides = [-(band(u_mix, t) + block(u_dmix, t)) for t in range(3)]
        sv = [block(sketched, 2 + t) for t in range(3)]
        coefs = mm(rinv, jnp.concatenate([pair] + sv + u_sides, axis=1))
        q_coef = coefs[:, : 2 * rank_count]
        q_parts = mm(q_coef, cross)
        phis = []
        for t in range(3):
            e_coef = jnp.concatenate(
                [block(coefs, 2 + t), block(coefs, 5 + t), q_coef], axis=1
            )
            q_side = jnp.concatenate(
                [block(q_parts, 0), block(q_parts, 1), block(q_parts, 2 + t), block(q_parts, 5 + t)],
                axis=1,
            )
            half = mm(e_coef, q_side, NT)
            sym = half + half.T
            i0 = lax.broadcasted_iota(jnp.int32, sym.shape, 0)
            i1 = lax.broadcasted_iota(jnp.int32, sym.shape, 1)
            phis.append(jnp.where(i0 > i1, sym, jnp.where(i0 == i1, 0.5 * sym, 0.0)))
        turned = mm(jnp.concatenate(phis, axis=0), q_coef)
        none = jnp.zeros((rank_count, rank_count), F32)
        rows = [jnp.concatenate([q_coef] + [none] * 6, axis=1)]
        for t in range(3):
            head = jnp.concatenate([block(coefs, 2 + t), block(coefs, 5 + t)], axis=1)
            tail = [none] * 6
            tail[t], tail[3 + t] = block(q_coef, 0), block(q_coef, 1)
            rows.append(jnp.concatenate([head - band(turned, t)] + tail, axis=1))
        basis_coef = jnp.concatenate(rows, axis=0)
        basis = dot_split(split2(basis_coef), take(lefts, slot(p, 0, 8))) * up_scale
        for t in range(4):
            out[p, 0, t] = band(basis, t)
        store(p, 0)
        dq_parts = mm(basis_coef[rank_count:], cross, NT)
        on_u = mm(
            block(dq_parts, 1)
            + jnp.concatenate([block(q_parts, 5 + t) for t in range(3)], axis=0),
            mix,
        )
        on_dmix = mm(block(q_parts, 1), jnp.concatenate(dmix, axis=1))
        q_mix = mm(block(q_parts, 1), mix)
        rows = [jnp.concatenate([block(q_parts, 0), -q_mix] + [none] * 6, axis=1)]
        for t in range(3):
            on_v = band(block(dq_parts, 0), t) + block(q_parts, 2 + t)
            tail = [none] * 6
            tail[t], tail[3 + t] = block(q_parts, 0), -q_mix
            rows.append(
                jnp.concatenate([on_v, -(band(on_u, t) + block(on_dmix, t))] + tail, axis=1)
            )
        coeff = dot_split(
            split2(jnp.concatenate(rows, axis=0) * down_scale), take(rights, slot(p, 0, 8))
        )
        for t in range(4):
            out[p, 0, 4 + t] = band(coeff, t)
        store(p, 4)
    for copy in stores:
        copy.wait()


def run_recompress(
    place, ranks, count, shards, cols, trailing, sketch, solved, inverse, scale, products
):
    tiles = trailing.shape[0]
    rank_count, size = sketch.shape
    vmem = pl.BlockSpec(memory_space=pltpu.VMEM)
    smem = pl.BlockSpec(memory_space=pltpu.SMEM)
    hbm = pl.BlockSpec(memory_space=pltpu.HBM)
    shards = in_hbm(*shards)
    cols, trailing, sketch, solved, inverse, products = in_hbm(
        cols, trailing, sketch, solved, inverse, products
    )
    return pl.pallas_call(
        functools.partial(recompress_kernel, tiles, len(shards), count),
        out_shape=jax.ShapeDtypeStruct(trailing.shape, F32),
        in_specs=[smem] * 5
        + [hbm] * len(shards)
        + [hbm] * 5
        + [vmem, hbm],
        out_specs=hbm,
        scratch_shapes=[pltpu.VMEM((tiles, 8 * rank_count, size), BF16)] * 4
        + [pltpu.VMEM((tiles, 4 * rank_count, size), BF16)] * 2
        + [
            pltpu.VMEM(cols.shape, F32),
            pltpu.VMEM(trailing.shape, F32),
            pltpu.VMEM((len(shards),) + shards[0].shape, F32),
            pltpu.VMEM(inverse.shape, F32),
            pltpu.VMEM(sketch.shape, F32),
            pltpu.VMEM(solved.shape, F32),
            pltpu.VMEM(products.shape, F32),
            pltpu.VMEM(trailing.shape, F32),
            pltpu.SemaphoreType.DMA((5 + tiles + len(shards) + 2 * tiles,)),
        ],
        compiler_params=pltpu.CompilerParams(vmem_limit_bytes=RECOMPRESS_VMEM),
        cost_estimate=pl.CostEstimate(
            flops=10 * 10**9, bytes_accessed=20 * 2**20, transcendentals=0
        ),
        name="recompress",
    )(place, *ranks, *shards, cols, trailing, sketch, solved, inverse, scale, products)


def on_device(
    row_count,
    col_count,
    diag,
    panel_rows,
    panel_cols,
    trailing,
    sketch,
    panel_rank,
    col_rank,
    tile_rank,
    keep_rank,
):
    own_rows = diag.shape[1]
    own_ranks = panel_cols.shape[2]
    comps = panel_cols.shape[1]
    size = sketch.shape[1]
    values = panel_cols[0, 4]
    own = diag[0]
    if own_rows == BLOCK and row_count > 2:
        width = (row_count // 2 + 1) * BLOCK
        own = lax.dynamic_slice(
            jnp.concatenate([own, own[:, : width - BLOCK]], axis=1),
            (0, lax.axis_index("row") * BLOCK),
            (BLOCK, width),
        )
        values = jnp.pad(values, ((0, 0), (0, -size % width)))
        values = jnp.concatenate(
            [values[:, i : i + width] for i in range(0, values.shape[1], width)], axis=0
        )
    gathered = lax.all_gather(jnp.concatenate([own, values], axis=0), "row", axis=0)
    shards = [panel_rows] + [
        lax.ppermute(panel_rows, "col", [(i, (i + s) % col_count) for i in range(col_count)])
        for s in range(1, col_count)
    ]
    late_cols, gathered = lax.optimization_barrier((panel_cols[0], gathered))
    cols = lax.all_gather(late_cols, "row", axis=0)
    if own_ranks != SUB:
        cols = cols.reshape(-1, SUB // own_ranks, comps, own_ranks, size)
        cols = cols.transpose(0, 2, 1, 3, 4).reshape(-1, comps, SUB, size)
    inverse, solved, products, scale = run_inverse(
        gathered, diag, col_rank, own_ranks
    )
    all_products = lax.all_gather(products, "row", axis=0)
    place = lax.axis_index("col").astype(jnp.int32).reshape(1)
    ranks = (panel_rank, col_rank, tile_rank, keep_rank)
    return run_recompress(
        place,
        ranks,
        col_count,
        shards,
        cols,
        trailing,
        sketch,
        solved,
        inverse,
        scale,
        all_products,
    )


def solution(mesh):
    in_specs = (
        P(None, "row", None),
        P("row", None, None, "col"),
        P("col", None, "row", None),
        P("row", "col", None, None, None),
        P(),
        P("row"),
        P("col"),
        P("row", "col"),
        P("row", "col"),
    )
    out_specs = P("row", "col", None, None, None)
    body = functools.partial(on_device, mesh.shape["row"], mesh.shape["col"])
    return jax.shard_map(body, mesh=mesh, in_specs=in_specs, out_specs=out_specs, check_vma=False)
```
